128 devices in a mesh: dp: 2 (over core), row: 4 (over x), col: 16 (over y, z).
Axes of the slice: x: 4, y: 4, z: 4, core: 2. Of those that a mesh axis runs over, the one named last changes fastest.
Arguments:
- tokens: bfloat16 [18912, 1024], P(('dp', 'col'), 'row'), may hold values from -6 to 6
- norm_gain: float32 [2, 2, 1024], P(None, None, 'row'), may hold values from 0.5 to 1.5
- norm_shift: float32 [2, 2, 1024], P(None, None, 'row'), may hold values from -3 to 3
- qkv_weight: bfloat16 [2, 1024, 3072], P(None, 'row', 'col')
- qv_bias: float32 [2, 2048], P(None, 'col'), may hold values from -3 to 3
- proj_weight: bfloat16 [2, 1024, 1024], P(None, 'col', 'row'), may hold values from -0.75 to 0.75
- proj_bias: float32 [2, 1024], P(None, 'row'), may hold values from -3 to 3
- up_weight: bfloat16 [2, 1024, 4096], P(None, 'row', 'col'), may hold values from -0.1875 to 0.1875
- up_bias: float32 [2, 4096], P(None, 'col'), may hold values from -3 to 3
- down_weight: bfloat16 [2, 4096, 1024], P(None, 'col', 'row'), may hold values from -0.09375 to 0.09375
- down_bias: float32 [2, 1024], P(None, 'row'), may hold values from -3 to 3
- cotangent: float32 [18912, 1024], P(('dp', 'col'), 'row'), may hold values from -6 to 6
Outputs:
- encoded: float32 [18912, 1024], P(('dp', 'col'), 'row')
- grad_tokens: float32 [18912, 1024], P(('dp', 'col'), 'row')
- grad_norm_gain: float32 [2, 2, 1024], P(None, None, 'row')
- grad_norm_shift: float32 [2, 2, 1024], P(None, None, 'row')
- grad_qkv_weight: float32 [2, 1024, 3072], P(None, 'row', 'col')
- grad_qv_bias: float32 [2, 2048], P(None, 'col')
- grad_proj_weight: float32 [2, 1024, 1024], P(None, 'col', 'row')
- grad_proj_bias: float32 [2, 1024], P(None, 'row')
- grad_up_weight: float32 [2, 1024, 4096], P(None, 'row', 'col')
- grad_up_bias: float32 [2, 4096], P(None, 'col')
- grad_down_weight: float32 [2, 4096, 1024], P(None, 'col', 'row')
- grad_down_bias: float32 [2, 1024], P(None, 'row')
The draws below stay inside these ranges and needn't reach their ends.
All inputs are finite; a program needn't handle non-finite values.
Results may differ from the reference program's by a relative error of at most 0.03.
Values may be sent and summed in bfloat16 or wider, within the bound.
A program may use at most 256 MiB of HBM per device.

```python
import jax
import jax.numpy as jnp
from jax import lax

D = 1024
FF = 4096
HEAD = 64
SEQ = 197
LAYERS = 2
IMG_DEV = 12
HEADS = 16
TOKENS = 18912
IMAGES = 96


def draw_qkv_weight(key, part):
    key = jax.random.fold_in(key, 11)
    random_key, shared_key = jax.random.split(key)
    random_part = jax.random.truncated_normal(random_key, -4.0, 4.0, (LAYERS, D, 3 * D), jnp.float32)
    shared_part = jax.random.truncated_normal(shared_key, -4.0, 4.0, (LAYERS, 1, 3 * D), jnp.float32)
    return ((random_part + 0.6 * shared_part) * D ** (-0.5)).astype(jnp.bfloat16)


def levels(own_key, dims, cuts, low, largest):
    def one(dim, shards_of):
        heights = jax.random.uniform(jax.random.fold_in(jax.random.fold_in(own_key, 6), dim), (shards_of,), jnp.float32, low / len(cuts), largest / len(cuts))
        return jnp.repeat(jnp.exp(heights), dims[dim] // shards_of).reshape((-1,) + (1,) * (len(dims) - dim - 1))

    level = one(*cuts[0])
    for cut in cuts[1:]:
        level = level * one(*cut)
    return level


def noise(key, extent, width, most, shards=(), held_as=jnp.bfloat16):
    level = levels(key, extent, shards, -0.22, 0.18) if shards else 1.0
    entries = jax.random.normal(key, extent, jnp.float32) * width * level
    return jnp.minimum(jnp.maximum(entries, -most), most).astype(held_as)


def setup_inputs(seed: int = 0) -> dict:
    key_of = jax.random.split(jax.random.key(seed), 13)
    tokens = noise(key_of[0], (TOKENS, D), 1.0, 6.0, ((0, 32), (1, 4)))
    norm_gain = jnp.clip(1.0 + 0.1 * jax.random.normal(key_of[1], (LAYERS, 2, D), jnp.float32), 0.5, 1.5)
    norm_shift = noise(key_of[2], (LAYERS, 2, D), 0.5, 3.0, ((2, 4),), jnp.float32)
    qkv_weight = draw_qkv_weight(jax.random.fold_in(key_of[12], 71), 0)
    qv_bias = noise(key_of[4], (LAYERS, 2 * D), 0.5, 3.0, ((1, 16),), jnp.float32)
    proj_weight = noise(key_of[5], (LAYERS, D, D), (D // 14) ** -0.5, 0.75, ((1, 16), (2, 4)))
    proj_bias = noise(key_of[6], (LAYERS, D), 0.5, 3.0, ((1, 4),), jnp.float32)
    up_weight = noise(key_of[7], (LAYERS, D, FF), D ** -0.5, 0.1875, ((1, 4), (2, 16)))
    up_bias = noise(key_of[8], (LAYERS, FF), 0.5, 3.0, ((1, 16),), jnp.float32)
    down_weight = noise(key_of[9], (LAYERS, FF, D), FF ** -0.5, 0.09375, ((1, 16), (2, 4)))
    down_bias = noise(key_of[10], (LAYERS, D), 0.5, 3.0, ((1, 4),), jnp.float32)
    cotangent = noise(key_of[11], (TOKENS, D), 1.0, 6.0, ((0, 32), (1, 4)), jnp.float32)
    return dict(tokens=tokens, norm_gain=norm_gain, norm_shift=norm_shift, qkv_weight=qkv_weight, qv_bias=qv_bias, proj_weight=proj_weight, proj_bias=proj_bias, up_weight=up_weight, up_bias=up_bias, down_weight=down_weight, down_bias=down_bias, cotangent=cotangent)


@jax.custom_vjp
def low(v):
    return lax.optimization_barrier(v.astype(jnp.bfloat16)).astype(jnp.float32)

@jax.custom_vjp
def low_back(v):
    return v

def low_keep(v):
    return (low(v), None)

def low_pass(kept, grad):
    return (grad,)

def back_keep(v):
    return (v, None)

def back_low(kept, grad):
    return (low(grad),)
low.defvjp(low_keep, low_pass)
low_back.defvjp(back_keep, back_low)
EXACT = lax.Precision.HIGHEST

def normalize(resid, gain, shift):
    average = lax.optimization_barrier(jnp.mean(resid, axis=-1, keepdims=True))
    centered = resid - average
    variance = lax.optimization_barrier(jnp.mean(centered * centered, axis=-1, keepdims=True))
    return centered * lax.rsqrt(variance + 1e-06) * gain + shift

def attend(blocks):
    queries, keys_in, values_in = blocks
    raw_scores = low_back(jnp.einsum('gqhe,gkhe->ghqk', queries, keys_in, precision=EXACT))
    softmax_w = jax.nn.softmax(raw_scores * HEAD ** (-0.5), axis=-1)
    return jnp.einsum('ghqk,gkhe->gqhe', low(softmax_w), values_in, precision=EXACT)

def matmul(left, right):
    return jnp.dot(left, right, precision=EXACT, preferred_element_type=jnp.float32)

def forward(resid, norm_gain, norm_shift, qkv_weight, qv_bias, proj_weight, proj_bias, up_weight, up_bias, down_weight, down_bias):
    groups = IMAGES // IMG_DEV
    for layer_no in range(LAYERS):
        normed = low(normalize(resid, norm_gain[layer_no, 0], norm_shift[layer_no, 0]))
        paired = qv_bias[layer_no].reshape(HEADS, 2, HEAD)
        zeros_key = jnp.zeros((HEADS, 1, HEAD), jnp.float32)
        bias_full = jnp.concatenate([paired[:, 0:1], zeros_key, paired[:, 1:2]], axis=1).reshape(3 * D)
        mixed = low(low_back(matmul(normed, qkv_weight[layer_no]) + bias_full))
        mixed = mixed.reshape(groups, IMG_DEV, SEQ, HEADS, 3, HEAD)
        attended = lax.map(jax.checkpoint(attend), (mixed[..., 0, :], mixed[..., 1, :], mixed[..., 2, :]))
        attended = low(low_back(attended.reshape(TOKENS, D)))
        resid = resid + low_back(matmul(attended, proj_weight[layer_no]) + proj_bias[layer_no])
        normed_mid = low(normalize(resid, norm_gain[layer_no, 1], norm_shift[layer_no, 1]))
        upward = low_back(matmul(normed_mid, up_weight[layer_no]) + up_bias[layer_no])
        activated = low(jax.nn.gelu(upward, approximate=False))
        resid = resid + low_back(matmul(activated, down_weight[layer_no]) + down_bias[layer_no])
    return resid

def reference(tokens, norm_gain, norm_shift, qkv_weight, qv_bias, proj_weight, proj_bias, up_weight, up_bias, down_weight, down_bias, cotangent):
    encoded, pullback = jax.vjp(forward, tokens.astype(jnp.float32), norm_gain.astype(jnp.float32), norm_shift.astype(jnp.float32), qkv_weight.astype(jnp.float32), qv_bias.astype(jnp.float32), proj_weight.astype(jnp.float32), proj_bias.astype(jnp.float32), up_weight.astype(jnp.float32), up_bias.astype(jnp.float32), down_weight.astype(jnp.float32), down_bias.astype(jnp.float32))
    gradients = pullback(cotangent.astype(jnp.float32))
    return (encoded, gradients[0], gradients[1], gradients[2], gradients[3], gradients[4], gradients[5], gradients[6], gradients[7], gradients[8], gradients[9], gradients[10])
```

```python
import functools

import jax
import jax.numpy as jnp
from jax import lax
from jax.experimental import pallas as pl
from jax.experimental.pallas import tpu as pltpu
from jax.sharding import PartitionSpec as P

MESH = pl.DeviceIdType.MESH
RING = 4
ORDERS = (("x", "y", "z"), ("y", "z", "x"), ("z", "x", "y"))
CUTS = {128: ((0, 48, 32), (48, 48, 16), (96, 32, 16)), 256: ((0, 80, 48), (80, 80, 32), (160, 96, 48))}


class Place:
    def __init__(self):
        self.core = lax.axis_index("dp")
        block = lax.axis_index("col")
        self.at = {"x": lax.axis_index("row"), "y": block // RING, "z": block % RING}

    def shifted(self, axis, by):
        moved = dict(self.at)
        moved[axis] = (self.at[axis] + by + RING) % RING
        return moved

    def device(self, at, core=None):
        return (self.core if core is None else core, at["x"], at["y"] * RING + at["z"])

    def neighbour(self, axis, by):
        return self.device(self.shifted(axis, by))

    def sibling(self):
        return self.device(self.at, 1 - self.core)

    def greet(self):
        barrier = pltpu.get_barrier_semaphore()
        for axis in "xyz":
            for by in (1, -1):
                pl.semaphore_signal(barrier, inc=1, device_id=self.neighbour(axis, by), device_id_type=MESH)
        pl.semaphore_signal(barrier, inc=1, device_id=self.sibling(), device_id_type=MESH)
        pl.semaphore_wait(barrier, 7)


def region(ref, at, whole, start, count):
    index = tuple(pl.ds(0, RING) if a in whole else at[a] for a in "yzx")
    return ref.at[index + (pl.ds(start, count),)]


def remote(src, dst, send, recv, device):
    return pltpu.make_async_remote_copy(
        src_ref=src, dst_ref=dst, send_sem=send, recv_sem=recv, device_id=device, device_id_type=MESH
    )


class Gather:
    def __init__(self, place, own, full, order, start, count, half, send, recv, share):
        self.place, self.own, self.full, self.order = place, own, full, order
        self.start, self.count, self.half = start, count, half
        self.send, self.recv, self.share = send, recv, share
        self.sent = []
        self.shared = []

    def piece(self, phase, by, start, count):
        at = self.place.shifted(self.order[phase], by)
        return region(self.full, at, self.order[:phase], start, count)

    def pass_on(self, ref, send, recv):
        if self.share:
            copy = remote(ref, ref, send, recv, self.place.sibling())
            copy.start()
            self.shared.append(copy)

    def first(self, phase):
        axis = self.order[phase]
        src = self.own if phase == 0 else self.piece(phase, 0, self.start, self.count)
        dst = self.piece(phase, 0, self.start, self.count)
        self.now = []
        for i, by in enumerate((1, -1)):
            copy = remote(src, dst, self.send.at[phase, i], self.recv.at[phase, i], self.place.neighbour(axis, by))
            copy.start()
            self.now.append(copy)
        self.sent += self.now

    def second(self, phase):
        axis = self.order[phase]
        later = []
        for i, by in enumerate((1, -1)):
            self.now[i].wait_recv()
            start, count = (self.start, self.half) if i == 0 else (self.start + self.half, self.count - self.half)
            ref = self.piece(phase, -by, start, count)
            copy = remote(ref, ref, self.send.at[phase, 2 + i], self.recv.at[phase, 2 + i], self.place.neighbour(axis, by))
            copy.start()
            later.append(copy)
        for i, by in enumerate((1, -1)):
            if self.share:
                self.pass_on(self.piece(phase, -by, self.start, self.count), self.send.at[phase, 4 + i], self.recv.at[phase, 4 + i])
        self.now = later
        self.sent += later

    def third(self, phase):
        for i in range(2):
            self.now[i].wait_recv()
            if self.share:
                start, count = (self.start, self.half) if i == 0 else (self.start + self.half, self.count - self.half)
                self.pass_on(self.piece(phase, 2, start, count), self.send.at[phase, 6 + i], self.recv.at[phase, 6 + i])

    def finish(self):
        for copy in self.sent:
            copy.wait_send()
        for copy in self.shared:
            copy.wait_send()
            copy.wait_recv()


def gather_kernel(units, plan, *refs):
    n = len(units)
    own, small, full, small_full = refs[:n], refs[n], refs[n + 1 : 2 * n + 1], refs[2 * n + 1]
    send, recv, small_send, small_recv, local = refs[2 * n + 2 :]
    place = Place()
    place.greet()
    copies = [
        pltpu.make_async_copy(own[u], region(full[u], place.at, (), 0, units[u]), local.at[u]) for u in range(n)
    ]
    copies.append(pltpu.make_async_copy(small, region(small_full, place.at, (), 0, small.shape[0]), local.at[n]))
    for copy in copies:
        copy.start()
    parts = []
    for u in range(n):
        rows = units[u] // 2
        base = pl.multiple_of(place.core * rows, rows)
        parts.append(
            [
                Gather(place, own[u].at[pl.ds(base + start, count)], full[u], ORDERS[p], base + start, count, half,
                       send.at[u, p], recv.at[u, p], True)
                for p, (start, count, half) in enumerate(CUTS[rows])
            ]
        )
    rows = small.shape[0]
    parts[0].append(
        Gather(place, small, small_full, ORDERS[0], 0, rows, rows // 2, small_send, small_recv, False)
    )

    def first(u, phase):
        for part in parts[u]:
            part.first(phase)

    def second(u, phase):
        for part in parts[u]:
            part.second(phase)

    def third(u, phase):
        for part in parts[u]:
            part.third(phase)

    def whole(u, phase):
        first(u, phase)
        second(u, phase)
        third(u, phase)

    units_all = range(n)
    for u in units_all:
        first(u, 0)
    for u in units_all:
        second(u, 0)
    for u in units_all:
        third(u, 0)
    for copy in copies:
        copy.wait()
    if plan == "all":
        for phase in (1, 2):
            for u in units_all:
                first(u, phase)
            for u in units_all:
                second(u, phase)
            for u in units_all:
                third(u, phase)
    if plan == "mixed":
        whole(0, 1)
        first(0, 2)
        for u in range(n):
            if u + 1 < n:
                whole(u + 1, 1)
            second(u, 2)
            if u + 1 < n:
                first(u + 1, 2)
            third(u, 2)
    if plan == "mixed2":
        first(0, 1)
        second(0, 1)
        first(1, 1)
        third(0, 1)
        first(0, 2)
        for u in range(n):
            if u + 1 < n:
                second(u + 1, 1)
            if u + 2 < n:
                first(u + 2, 1)
            if u + 1 < n:
                third(u + 1, 1)
            second(u, 2)
            if u + 1 < n:
                first(u + 1, 2)
            third(u, 2)
    if plan == "serial":
        for u in range(n):
            for phase in range(3):
                whole(u, phase)
    elif plan == "early":
        for u in range(n):
            whole(u, 0)
            whole(u, 1)
        first(0, 2)
        for u in range(n):
            second(u, 2)
            if u + 1 < n:
                first(u + 1, 2)
            third(u, 2)
    elif plan == "pipe":
        whole(0, 0)
        whole(0, 1)
        first(0, 2)
        for u in range(n):
            if u + 1 < n:
                whole(u + 1, 0)
                whole(u + 1, 1)
            second(u, 2)
            if u + 1 < n:
                first(u + 1, 2)
            third(u, 2)
    for unit in parts:
        for part in unit:
            part.finish()


def gather_all(own, small, plan, collective_id):
    units = [a.shape[0] for a in own]
    n = len(units)
    any_space = pl.BlockSpec(memory_space=pl.ANY)
    shapes = [jax.ShapeDtypeStruct((RING, RING, RING) + a.shape, a.dtype) for a in (*own, small)]
    return pl.pallas_call(
        functools.partial(gather_kernel, units, plan),
        out_shape=shapes,
        in_specs=[pl.BlockSpec(memory_space=pltpu.VMEM)] * (n + 1),
        out_specs=[any_space] * (n + 1),
        scratch_shapes=[
            pltpu.SemaphoreType.DMA((n, 3, 3, 8)),
            pltpu.SemaphoreType.DMA((n, 3, 3, 8)),
            pltpu.SemaphoreType.DMA((3, 4)),
            pltpu.SemaphoreType.DMA((3, 4)),
            pltpu.SemaphoreType.DMA((n + 1,)),
        ],
        compiler_params=pltpu.CompilerParams(collective_id=collective_id, has_side_effects=True),
        name="gather_weights",
    )(*own, small)


def blockwise(ref_shape, body):
    lead = ref_shape[:-2]
    total = 1
    for size in lead:
        total *= size
    if total == 1:
        body((0,) * len(lead))
        return

    def step(i, _):
        index = (i // lead[1], i % lead[1]) if len(lead) == 2 else (i,)
        body(index)
        return 0

    lax.fori_loop(0, total, step, 0)


def add_into(dst, *others):
    def body(index):
        total = dst[index].astype(jnp.float32)
        for other in others:
            total = total + other[index].astype(jnp.float32)
        dst[index] = total.astype(dst.dtype)

    blockwise(dst.shape, body)


class Scatter:
    def __init__(self, place, order, grads, own, twin, half_in, full_in, out, base, other, start, count, half, sems):
        self.place, self.order = place, order
        self.grads, self.own, self.twin, self.half_in, self.full_in, self.out = grads, own, twin, half_in, full_in, out
        self.base, self.other, self.start, self.count, self.half = base, other, start, count, half
        self.send, self.recv, self.near, self.far_send, self.far_recv, self.out_send, self.out_recv = sems
        self.sent = []
        self.twins = {}

    def piece(self, ref, phase, by, start, count):
        at = self.place.shifted(self.order[2 - phase], by)
        return region(ref, at, self.order[: 2 - phase], start, count)

    def bring(self, k, by):
        src = self.piece(self.grads, 0, by, self.base + self.start, self.count)
        near = pltpu.make_async_copy(src, self.piece(self.own, 0, by, self.start, self.count), self.near.at[k])
        near.start()
        away = self.piece(self.grads, 0, by, self.other + self.start, self.count)
        far = remote(away, self.piece(self.twin, 0, by, self.start, self.count), self.far_send.at[k],
                     self.far_recv.at[k], self.place.sibling())
        far.start()
        self.twins[by] = (near, far)

    def join(self, by):
        near, far = self.twins[by]
        near.wait()
        far.wait()
        add_into(self.piece(self.own, 0, by, self.start, self.count), self.piece(self.twin, 0, by, self.start, self.count))

    def incoming(self, refs, phase, start, count):
        lead = (slice(None),) * (2 - phase)
        return refs[phase].at[lead + (pl.ds(start, count),)]

    def push(self, phase, i, src, dst, by):
        copy = remote(src, dst, self.send.at[phase, i], self.recv.at[phase, i],
                      self.place.neighbour(self.order[2 - phase], by))
        copy.start()
        self.sent.append(copy)
        return copy

    def halves(self):
        return ((self.start, self.half), (self.start + self.half, self.count - self.half))

    def opposite(self, phase):
        if phase == 0:
            self.join(2)
        self.now = [
            self.push(phase, i, self.piece(self.own, phase, 2, start, count),
                      self.incoming(self.half_in, phase, start, count), by)
            for i, (by, (start, count)) in enumerate(zip((1, -1), self.halves()))
        ]
        if phase == 0:
            self.join(1)
            self.join(-1)

    def sides(self, phase):
        later = []
        for i, (by, (start, count)) in enumerate(zip((1, -1), self.halves())):
            self.now[i].wait_recv()
            add_into(self.piece(self.own, phase, by, start, count), self.incoming(self.half_in, phase, start, count))
            lead = (slice(None),) * (2 - phase)
            later.append(
                self.push(phase, 2 + i, self.piece(self.own, phase, by, self.start, self.count),
                          self.full_in[phase].at[(i,) + lead + (pl.ds(self.start, self.count),)], by)
            )
        self.now = later
        if phase == 0:
            self.join(0)

    def centre(self, phase):
        for copy in self.now:
            copy.wait_recv()
        lead = (slice(None),) * (2 - phase)
        rows = (pl.ds(self.start, self.count),)
        mine = self.piece(self.own, phase, 0, self.start, self.count)
        arrived = [self.full_in[phase].at[(i,) + lead + rows] for i in range(2)]
        if phase < 2:
            add_into(mine, *arrived)
            return
        total = mine[...].astype(jnp.float32)
        for ref in arrived:
            total = total + ref[...].astype(jnp.float32)
        rows = pl.ds(self.base + self.start, self.count)
        self.out[rows, :] = total
        self.shown = remote(self.out.at[rows], self.out.at[rows], self.out_send, self.out_recv, self.place.sibling())
        self.shown.start()

    def finish(self):
        for copy in self.sent:
            copy.wait_send()
        self.shown.wait()


def scatter_kernel(units, *refs):
    n = len(units)
    grads, outs = refs[:n], refs[n : 2 * n]
    scratch = refs[2 * n :]
    place = Place()
    place.greet()
    parts = []
    for u in range(n):
        rows = units[u] // 2
        own, twin, h0, h1, h2, f0, f1, f2, send, recv, near, far_send, far_recv, out_send, out_recv = scratch[15 * u : 15 * (u + 1)]
        base = pl.multiple_of(place.core * rows, rows)
        other = pl.multiple_of((1 - place.core) * rows, rows)
        parts.append(
            [
                Scatter(place, ORDERS[p], grads[u], own, twin, (h0, h1, h2), (f0, f1, f2), outs[u], base, other,
                        start, count, half,
                        (send.at[p], recv.at[p], near.at[p], far_send.at[p], far_recv.at[p], out_send.at[p], out_recv.at[p]))
                for p, (start, count, half) in enumerate(CUTS[rows])
            ]
        )
    every = [part for unit in parts for part in unit]
    for k, by in enumerate((2, 1, -1, 0)):
        for part in every:
            part.bring(k, by)
    for phase in range(3):
        for part in every:
            part.opposite(phase)
        for part in every:
            part.sides(phase)
        for part in every:
            part.centre(phase)
    for part in every:
        part.finish()


def scatter_units(grads, collective_id):
    units = [g.shape[3] for g in grads]
    n = len(units)
    scratch = []
    for size in units:
        rows = size // 2
        block = (rows, 256)
        dma = pltpu.SemaphoreType.DMA
        scratch += [pltpu.VMEM((RING,) * 3 + block, jnp.bfloat16)] * 2
        scratch += [pltpu.VMEM((RING,) * (2 - t) + block, jnp.bfloat16) for t in range(3)]
        scratch += [pltpu.VMEM((2,) + (RING,) * (2 - t) + block, jnp.bfloat16) for t in range(3)]
        scratch += [dma((3, 3, 4)), dma((3, 3, 4)), dma((3, 4)), dma((3, 4)), dma((3, 4)), dma((3,)), dma((3,))]
    return pl.pallas_call(
        functools.partial(scatter_kernel, units),
        out_shape=[jax.ShapeDtypeStruct((size, 256), jnp.float32) for size in units],
        in_specs=[pl.BlockSpec(memory_space=pl.ANY)] * n,
        out_specs=[pl.BlockSpec(memory_space=pltpu.VMEM)] * n,
        scratch_shapes=scratch,
        compiler_params=pltpu.CompilerParams(
            collective_id=collective_id, has_side_effects=True, vmem_limit_bytes=58 * 2**20
        ),
        name="scatter_grads",
    )(*grads)


HEAD = 64
SEQ = 197
ROWS = 208
WIDTH = 1024
HEADS = 16
FF_BLOCK = 256
QKV = 192
EPS = 1e-06
VMEM_LIMIT = 48 * 2**20


def wide(block):
    return jnp.concatenate([block[i] for i in range(RING)], axis=1)


def store_blocks(ref, value):
    for i in range(RING):
        ref[0, 0, i] = value[:, i * 256 : (i + 1) * 256].astype(ref.dtype)


def feature_row(small_ref, row):
    return jnp.concatenate([small_ref[0, 0, i, row : row + 1, :] for i in range(RING)], axis=1)


def dot_nt(a, b):
    return lax.dot_general(a, b, (((1,), (1,)), ((), ())), preferred_element_type=jnp.float32)


def dot_nn(a, b):
    return lax.dot_general(a, b, (((1,), (0,)), ((), ())), preferred_element_type=jnp.float32)


def dot_tn(a, b):
    return lax.dot_general(a, b, (((0,), (0,)), ((), ())), preferred_element_type=jnp.float32)


def norm_parts(x):
    average = jnp.mean(x, axis=1, keepdims=True)
    centered = x - average
    inverse = lax.rsqrt(jnp.mean(centered * centered, axis=1, keepdims=True) + EPS)
    return centered * inverse, inverse


def norm_back(incoming, x, gain):
    normed, inverse = norm_parts(x)
    scaled = incoming * gain
    mean = jnp.mean(scaled, axis=1, keepdims=True)
    along = jnp.mean(scaled * normed, axis=1, keepdims=True)
    result = inverse * (scaled - mean - normed * along)
    return result, jnp.sum(incoming * normed, axis=0, keepdims=True), jnp.sum(incoming, axis=0, keepdims=True)


def softmax(queries, keys):
    scores = dot_nt(queries, keys) * HEAD**-0.5
    column = lax.broadcasted_iota(jnp.int32, scores.shape, 1)
    scores = jnp.where(column < SEQ, scores, -1e30)
    highest = jnp.max(scores, axis=1, keepdims=True)
    expon = jnp.exp(scores - highest)
    return expon / jnp.sum(expon, axis=1, keepdims=True)


def attend_forward_kernel(layer, x_ref, small_ref, here_ref, qkv_ref, proj_ref, mid_ref, mixed_ref, att_ref, h_ref):
    step = pl.program_id(0)

    @pl.when(step == 0)
    def _():
        x = x_ref[...].astype(jnp.float32)
        normed, _ = norm_parts(x)
        h_ref[...] = (normed * feature_row(small_ref, 8 * layer) + feature_row(small_ref, 8 * layer + 2)).astype(jnp.bfloat16)
        mid_ref[...] = x + feature_row(small_ref, 8 * layer + 4)

    bias = here_ref[0, 0, 0, 8 * layer + 7 : 8 * layer + 8, :QKV]
    mixed = (dot_nt(h_ref[...], wide(qkv_ref[0, 0])) + bias).astype(jnp.bfloat16)
    mixed_ref[0] = mixed
    probs = softmax(mixed[:, :HEAD], mixed[:, HEAD : 2 * HEAD]).astype(jnp.bfloat16)
    att = dot_nn(probs, mixed[:, 2 * HEAD :]).astype(jnp.bfloat16)
    att_ref[0] = att
    mid_ref[...] += dot_nn(att, wide(proj_ref[0, 0]))


def feed_forward_kernel(layer, mid_ref, small_ref, here_ref, up_ref, down_ref, out_ref, upward_ref, h_ref):
    step = pl.program_id(0)

    @pl.when(step == 0)
    def _():
        mid = mid_ref[...]
        normed, _ = norm_parts(mid)
        h_ref[...] = (normed * feature_row(small_ref, 8 * layer + 1) + feature_row(small_ref, 8 * layer + 3)).astype(jnp.bfloat16)
        out_ref[...] = mid + feature_row(small_ref, 8 * layer + 5)

    upward = dot_nt(h_ref[...], wide(up_ref[0, 0])) + here_ref[0, 0, 0, 8 * layer + 6 : 8 * layer + 7, :]
    upward_ref[0] = upward
    activated = (upward * (0.5 + 0.5 * lax.erf(upward * 2**-0.5))).astype(jnp.bfloat16)
    out_ref[...] += dot_nn(activated, wide(down_ref[0, 0]))


def feed_back_kernel(layer, g_ref, mid_ref, small_ref, upward_ref, up_ref, down_ref, gmid_ref, grad_ref, bias_ref, rows_ref, h_ref, low_ref, acc_ref):
    step = pl.program_id(0)

    @pl.when(step == 0)
    def _():
        normed, _ = norm_parts(mid_ref[...])
        h_ref[...] = (normed * feature_row(small_ref, 8 * layer + 1) + feature_row(small_ref, 8 * layer + 3)).astype(jnp.bfloat16)
        low_ref[...] = g_ref[...].astype(jnp.bfloat16)
        acc_ref[...] = jnp.zeros_like(acc_ref)

    low = low_ref[...]
    upward = upward_ref[0]
    phi_total = 0.5 + 0.5 * lax.erf(upward * 2**-0.5)
    density = jnp.exp(-0.5 * upward * upward) * (2 * jnp.pi) ** -0.5
    activated = (upward * phi_total).astype(jnp.bfloat16)
    g_up = (dot_nt(low, wide(down_ref[0, 0])) * (phi_total + upward * density)).astype(jnp.bfloat16)
    store_blocks(grad_ref.at[:, :, :, FF_BLOCK:], dot_tn(activated, low))
    store_blocks(grad_ref.at[:, :, :, :FF_BLOCK], dot_tn(g_up, h_ref[...]))
    bias_ref[0] = jnp.sum(g_up.astype(jnp.float32), axis=0, keepdims=True)
    acc_ref[...] += dot_nn(g_up, wide(up_ref[0, 0]))

    @pl.when(step == pl.num_programs(0) - 1)
    def _():
        part, gain, shift = norm_back(acc_ref[...], mid_ref[...], feature_row(small_ref, 8 * layer + 1))
        gmid_ref[...] = g_ref[...].astype(jnp.float32) + part
        rows_ref[0:1, :] = jnp.sum(low_ref[...].astype(jnp.float32), axis=0, keepdims=True)
        rows_ref[1:2, :] = gain
        rows_ref[2:3, :] = shift


def attend_back_kernel(layer, g_ref, x_ref, small_ref, mixed_ref, att_ref, qkv_ref, proj_ref, gx_ref, grad_ref, bias_ref, rows_ref, h_ref, low_ref, acc_ref):
    step = pl.program_id(0)

    @pl.when(step == 0)
    def _():
        normed, _ = norm_parts(x_ref[...].astype(jnp.float32))
        h_ref[...] = (normed * feature_row(small_ref, 8 * layer) + feature_row(small_ref, 8 * layer + 2)).astype(jnp.bfloat16)
        low_ref[...] = g_ref[...].astype(jnp.bfloat16)
        acc_ref[...] = jnp.zeros_like(acc_ref)

    low = low_ref[...]
    mixed = mixed_ref[0]
    queries, keys, values = mixed[:, :HEAD], mixed[:, HEAD : 2 * HEAD], mixed[:, 2 * HEAD :]
    store_blocks(grad_ref.at[:, :, :, QKV:], dot_tn(att_ref[0], low))
    g_att = dot_nt(low, wide(proj_ref[0, 0])).astype(jnp.bfloat16)
    probs = softmax(queries, keys)
    g_probs = dot_nt(g_att, values)
    g_values = dot_tn(probs.astype(jnp.bfloat16), g_att)
    centre = jnp.sum(probs * g_probs, axis=1, keepdims=True)
    g_scores = (probs * (g_probs - centre) * HEAD**-0.5).astype(jnp.bfloat16)
    g_mixed = jnp.concatenate([dot_nn(g_scores, keys), dot_tn(g_scores, queries), g_values], axis=1).astype(jnp.bfloat16)
    store_blocks(grad_ref.at[:, :, :, :QKV], dot_tn(g_mixed, h_ref[...]))
    bias_ref[0, :, :QKV] = jnp.sum(g_mixed.astype(jnp.float32), axis=0, keepdims=True)
    acc_ref[...] += dot_nn(g_mixed, wide(qkv_ref[0, 0]))

    @pl.when(step == pl.num_programs(0) - 1)
    def _():
        part, gain, shift = norm_back(acc_ref[...], x_ref[...].astype(jnp.float32), feature_row(small_ref, 8 * layer))
        gx_ref[...] = g_ref[...] + part
        rows_ref[0:1, :] = jnp.sum(low_ref[...].astype(jnp.float32), axis=0, keepdims=True)
        rows_ref[1:2, :] = gain
        rows_ref[2:3, :] = shift


def whole_spec(shape):
    return pl.BlockSpec(shape, lambda i: (0,) * len(shape))


def block_spec(rows, at):
    return pl.BlockSpec((1, 1, RING, rows, 256), lambda i: (i // RING, i % RING, 0, at, 0))


TOKENS_SPEC = whole_spec((ROWS, WIDTH))
SMALL_SPEC = pl.BlockSpec((1, 1, RING, 16, 256), lambda i: (0, 0, 0, 0, 0))
HERE_SPEC = pl.BlockSpec((1, 1, 1, 16, 256), lambda i: (i // RING, i % RING, 0, 0, 0))


def saved_spec(width):
    return pl.BlockSpec((1, ROWS, width), lambda i: (i, 0, 0))


def saved(width, dtype):
    return jax.ShapeDtypeStruct((HEADS, ROWS, width), dtype)


def compute(kernel, out_shape, in_specs, out_specs, scratch, name):
    return pl.pallas_call(
        kernel,
        grid=(HEADS,),
        out_shape=out_shape,
        in_specs=in_specs,
        out_specs=out_specs,
        scratch_shapes=scratch,
        compiler_params=pltpu.CompilerParams(vmem_limit_bytes=VMEM_LIMIT),
        name=name,
    )


TOKENS_F32 = jax.ShapeDtypeStruct((ROWS, WIDTH), jnp.float32)
LOW = pltpu.VMEM((ROWS, WIDTH), jnp.bfloat16)
FULL = pltpu.VMEM((ROWS, WIDTH), jnp.float32)


def attend_forward(layer, x, small, weights):
    return compute(
        functools.partial(attend_forward_kernel, layer),
        [TOKENS_F32, saved(QKV, jnp.bfloat16), saved(HEAD, jnp.bfloat16)],
        [TOKENS_SPEC, SMALL_SPEC, HERE_SPEC, block_spec(QKV, 0), block_spec(HEAD, 3)],
        [TOKENS_SPEC, saved_spec(QKV), saved_spec(HEAD)],
        [LOW],
        "attend_forward",
    )(x, small, small, weights, weights)


def feed_forward(layer, mid, small, weights):
    return compute(
        functools.partial(feed_forward_kernel, layer),
        [TOKENS_F32, saved(FF_BLOCK, jnp.float32)],
        [TOKENS_SPEC, SMALL_SPEC, HERE_SPEC, block_spec(FF_BLOCK, 0), block_spec(FF_BLOCK, 1)],
        [TOKENS_SPEC, saved_spec(FF_BLOCK)],
        [LOW],
        "feed_forward",
    )(mid, small, small, weights, weights)


def grads_shape(rows):
    return jax.ShapeDtypeStruct((RING, RING, RING, rows, 256), jnp.bfloat16)


BIAS_SHAPE = jax.ShapeDtypeStruct((HEADS, 1, 256), jnp.float32)
BIAS_SPEC = pl.BlockSpec((1, 1, 256), lambda i: (i, 0, 0))
SUMS_SHAPE = jax.ShapeDtypeStruct((8, WIDTH), jnp.float32)
SUMS_SPEC = whole_spec((8, WIDTH))


def feed_back(layer, g, mid, small, upward, weights):
    return compute(
        functools.partial(feed_back_kernel, layer),
        [TOKENS_F32, grads_shape(2 * FF_BLOCK), BIAS_SHAPE, SUMS_SHAPE],
        [TOKENS_SPEC, TOKENS_SPEC, SMALL_SPEC, saved_spec(FF_BLOCK), block_spec(FF_BLOCK, 0), block_spec(FF_BLOCK, 1)],
        [TOKENS_SPEC, block_spec(2 * FF_BLOCK, 0), BIAS_SPEC, SUMS_SPEC],
        [LOW, LOW, FULL],
        "feed_back",
    )(g, mid, small, upward, weights, weights)


def attend_back(layer, g, x, small, mixed, att, weights):
    return compute(
        functools.partial(attend_back_kernel, layer),
        [TOKENS_F32, grads_shape(QKV + HEAD), BIAS_SHAPE, SUMS_SHAPE],
        [TOKENS_SPEC, TOKENS_SPEC, SMALL_SPEC, saved_spec(QKV), saved_spec(HEAD), block_spec(QKV, 0), block_spec(HEAD, 3)],
        [TOKENS_SPEC, block_spec(QKV + HEAD, 0), BIAS_SPEC, SUMS_SPEC],
        [LOW, LOW, FULL],
        "attend_back",
    )(g, x, small, mixed, att, weights, weights)


def to_images(rows):
    padded = jnp.pad(rows.reshape(3, SEQ, 256), ((0, 1), (0, ROWS - SEQ), (0, 0)))
    return lax.all_to_all(padded, "row", 0, 0)


def from_images(image):
    parts = image.astype(jnp.bfloat16).reshape(ROWS, RING, 256).transpose(1, 0, 2)
    back = lax.all_to_all(parts, "row", 0, 0)
    return back[:3, :SEQ].reshape(3 * SEQ, 256).astype(jnp.float32)


def as_tokens(blocks):
    return blocks.transpose(1, 0, 2).reshape(ROWS, WIDTH)


def shards(tokens, norm_gain, norm_shift, qkv_weight, qv_bias, proj_weight, proj_bias, up_weight, up_bias, down_weight, down_bias, cotangent):
    layers = qkv_weight.shape[0]
    own, small = [], []
    for layer in range(layers):
        own.append(jnp.concatenate([qkv_weight[layer].T, proj_weight[layer]], axis=0))
        own.append(jnp.concatenate([up_weight[layer].T, down_weight[layer]], axis=0))
        qv = qv_bias[layer]
        zeros = jnp.zeros((HEAD,), jnp.float32)
        qkv_row = jnp.concatenate([qv[:HEAD], zeros, qv[HEAD:], zeros])
        small.append(
            jnp.stack([norm_gain[layer, 0], norm_gain[layer, 1], norm_shift[layer, 0], norm_shift[layer, 1],
                       proj_bias[layer], down_bias[layer], up_bias[layer], qkv_row])
        )
    *full, small = gather_all(own, jnp.concatenate(small), "mixed2", 0)
    x = as_tokens(to_images(tokens)).astype(jnp.float32)
    g = as_tokens(to_images(cotangent.astype(jnp.bfloat16))).astype(jnp.float32)
    kept = []
    for layer in range(layers):
        mid, mixed, att = attend_forward(layer, x, small, full[2 * layer])
        out, upward = feed_forward(layer, mid, small, full[2 * layer + 1])
        kept.append((x, mid, mixed, att, upward))
        x = out
    encoded = from_images(x)
    weight_grads, sums = [None] * layers, [None] * layers
    for layer in reversed(range(layers)):
        x, mid, mixed, att, upward = kept[layer]
        g_mid, feed_grad, up_sums, feed_rows = feed_back(layer, g, mid, small, upward, full[2 * layer + 1])
        g, attend_grad, qkv_sums, attend_rows = attend_back(layer, g_mid, x, small, mixed, att, full[2 * layer])
        weight_grads[layer] = scatter_units((feed_grad, attend_grad), 1)
        sums[layer] = jnp.concatenate(
            [up_sums.reshape(-1), qkv_sums.reshape(-1), feed_rows[:3].reshape(-1), attend_rows[:3].reshape(-1)]
        )
    grad_tokens = from_images(g)
    sums = lax.psum(jnp.stack(sums), ("dp", "row", "col"))
    row, col = lax.axis_index("row"), lax.axis_index("col")
    up_sums = lax.dynamic_slice_in_dim(sums[:, : 16 * 256].reshape(layers, 16, 256), col, 1, 1)[:, 0]
    qkv_sums = lax.dynamic_slice_in_dim(sums[:, 16 * 256 : 32 * 256].reshape(layers, 16, 256), col, 1, 1)[:, 0]
    features = lax.dynamic_slice_in_dim(sums[:, 32 * 256 :].reshape(layers, 6, RING, 256), row, 1, 2)[:, :, 0]
    feed = [weight_grads[layer][0] for layer in range(layers)]
    attend = [weight_grads[layer][1] for layer in range(layers)]
    return (
        encoded,
        grad_tokens,
        jnp.stack([features[:, 4], features[:, 1]], axis=1),
        jnp.stack([features[:, 5], features[:, 2]], axis=1),
        jnp.stack([a[:QKV].T for a in attend]),
        jnp.concatenate([qkv_sums[:, :HEAD], qkv_sums[:, 2 * HEAD : QKV]], axis=1),
        jnp.stack([a[QKV:] for a in attend]),
        features[:, 3],
        jnp.stack([f[:FF_BLOCK].T for f in feed]),
        up_sums,
        jnp.stack([f[FF_BLOCK:] for f in feed]),
        features[:, 0],
    )


def solution(mesh):
    in_specs = (
        P(("dp", "col"), "row"),
        P(None, None, "row"),
        P(None, None, "row"),
        P(None, "row", "col"),
        P(None, "col"),
        P(None, "col", "row"),
        P(None, "row"),
        P(None, "row", "col"),
        P(None, "col"),
        P(None, "col", "row"),
        P(None, "row"),
        P(("dp", "col"), "row"),
    )
    out_specs = (
        P(("dp", "col"), "row"),
        P(("dp", "col"), "row"),
        P(None, None, "row"),
        P(None, None, "row"),
        P(None, "row", "col"),
        P(None, "col"),
        P(None, "col", "row"),
        P(None, "row"),
        P(None, "row", "col"),
        P(None, "col"),
        P(None, "col", "row"),
        P(None, "row"),
    )
    return jax.shard_map(shards, mesh=mesh, in_specs=in_specs, out_specs=out_specs, check_vma=False)
```

```python
import functools

import jax
import jax.numpy as jnp
from jax import lax
from jax.experimental import pallas as pl
from jax.experimental.pallas import tpu as pltpu
from jax.sharding import PartitionSpec as P

MESH = pl.DeviceIdType.MESH
RING = 4
STEPS = 4
AXES = "yzx"
ORDERS = (("x", "y", "z"), ("y", "z", "x"), ("z", "x", "y"))
KINDS = 3
UNIT = 256
CORE = 128
CUTS = (((0, 48), (48, 48), (96, 32)), ((0, 48), (48, 32), (80, 48)), ((0, 32), (32, 48), (80, 48)))
NEAR = tuple((axis, by) for axis in "xyz" for by in (1, -1)) + (("core", 1),)
ROW_PEERS = (("x", 1), ("x", 2), ("x", -1))
VMEM_LIMIT = 60 * 2**20
DMA = pltpu.SemaphoreType.DMA
ANY = pl.BlockSpec(memory_space=pl.ANY)
VMEM = pl.BlockSpec(memory_space=pltpu.VMEM)
BF16 = jnp.bfloat16
F32 = jnp.float32


def number(kind, layer):
    return 2 * kind + layer


class Place:
    def __init__(self):
        self.core = lax.axis_index("dp")
        block = lax.axis_index("col")
        self.at = {"x": lax.axis_index("row"), "y": block // RING, "z": block % RING}
        self.mine = pl.ds(pl.multiple_of(self.core * CORE, CORE), CORE)
        self.other = pl.ds(pl.multiple_of((1 - self.core) * CORE, CORE), CORE)

    def shifted(self, axis, by):
        moved = dict(self.at)
        moved[axis] = (self.at[axis] + by + RING) % RING
        return moved

    def neighbour(self, axis, by):
        if axis == "core":
            return (1 - self.core, self.at["x"], self.at["y"] * RING + self.at["z"])
        at = self.shifted(axis, by)
        return (self.core, at["x"], at["y"] * RING + at["z"])

    def sibling(self):
        return self.neighbour("core", 1)

    def tell(self, semaphore, peers):
        for axis, by in peers:
            pl.semaphore_signal(semaphore, inc=1, device_id=self.neighbour(axis, by), device_id_type=MESH)

    def greet(self, peers):
        barrier = pltpu.get_barrier_semaphore()
        self.tell(barrier, peers)
        pl.semaphore_wait(barrier, len(peers))


def region(ref, axes, at, whole, start, count):
    index = tuple(pl.ds(0, RING) if a in whole else at[a] for a in axes)
    return ref.at[index + (pl.ds(start, count),)]


def remote(src, dst, send, recv, device):
    return pltpu.make_async_remote_copy(
        src_ref=src, dst_ref=dst, send_sem=send, recv_sem=recv, device_id=device, device_id_type=MESH
    )


class Ring:
    def __init__(self, place, full, units, order, phase, start, count, half, send, recv, own=None):
        self.place, self.full, self.units, self.own = place, full, units, own
        self.axis, self.whole = order[phase], order[:phase]
        self.start, self.count = start, count
        self.halves = ((start, half), (start + half, count - half))
        self.send, self.recv = send, recv

    def piece(self, by, start, count):
        at = self.place.shifted(self.axis, by)
        index = tuple(pl.ds(0, RING) if a in self.whole else at[a] for a in AXES)
        return self.full.at[(self.units,) + index + (pl.ds(start, count),)]

    def to(self, i):
        return self.place.neighbour(self.axis, (1, -1)[i])

    def whole_copy(self, i):
        here = self.piece(0, self.start, self.count)
        return remote(here if self.own is None else self.own, here, self.send.at[i], self.recv.at[i], self.to(i))

    def half_copy(self, i):
        ref = self.piece((-1, 1)[i], *self.halves[i])
        return remote(ref, ref, self.send.at[2 + i], self.recv.at[2 + i], self.to(i))

    def share(self, k):
        ref = self.piece((-1, 1)[k], self.start, self.count) if k < 2 else self.piece(2, *self.halves[k - 2])
        return remote(ref, ref, self.send.at[4 + k], self.recv.at[4 + k], self.place.sibling())

    def share_all(self):
        index = tuple(pl.ds(0, RING) if a in self.whole + (self.axis,) else self.place.at[a] for a in AXES)
        ref = self.full.at[(self.units,) + index + (pl.ds(self.start, self.count),)]
        return remote(ref, ref, self.send.at[4], self.recv.at[4], self.place.sibling())

    def first(self):
        for i in range(2):
            self.whole_copy(i).start()

    def second(self):
        for i in range(2):
            self.whole_copy(i).wait_recv()
            self.half_copy(i).start()

    def third(self):
        for i in range(2):
            self.half_copy(i).wait_recv()

    def finish(self):
        for i in range(2):
            self.whole_copy(i).wait_send()
            self.half_copy(i).wait_send()


class Gather:
    def __init__(self, place, own, full, small_own, small_full, sems):
        one_send, one_recv, two_send, two_recv, three_send, three_recv, small_send, small_recv = sems
        self.one, self.two, self.three = [], {}, {}
        base = pl.multiple_of(place.core * CORE, CORE)
        for kind in range(KINDS):
            for p, (start, count) in enumerate(CUTS[kind]):
                rows = base + start
                self.one.append(
                    Ring(place, full, pl.ds(2 * kind, 2), ORDERS[p], 0, rows, count, 16, one_send.at[kind, p],
                         one_recv.at[kind, p], own.at[pl.ds(2 * kind, 2), pl.ds(rows, count)])
                )
            for layer in range(2):
                u = number(kind, layer)
                for phase, into, send, recv in ((1, self.two, two_send, two_recv), (2, self.three, three_send, three_recv)):
                    into[u] = [
                        Ring(place, full, u, ORDERS[p], phase, base + start, count,
                             count // 2 if count == 32 else (16, 32)[(p + layer) % 2], send.at[u, p], recv.at[u, p])
                        for p, (start, count) in enumerate(CUTS[kind])
                    ]
        rows = small_own.shape[1]
        self.small = [
            Ring(place, small_full, pl.ds(0, 1), ORDERS[0], phase, 0, rows, rows // 2, small_send.at[phase],
                 small_recv.at[phase], small_own if phase == 0 else None)
            for phase in range(3)
        ]

    def begin(self):
        rings = self.one + [self.small[0]]
        for name in ("first", "second", "third"):
            for ring in rings:
                getattr(ring, name)()

    def small_phase(self, phase, name):
        getattr(self.small[phase], name)()

    def first_two(self, u):
        for ring in self.two[u]:
            ring.first()

    def second_two(self, u):
        for ring in self.two[u]:
            ring.second()

    def third_two(self, u):
        for ring in self.two[u]:
            ring.third()

    def first_three(self, u):
        for ring in self.three[u]:
            ring.first()
        for ring in self.two[u]:
            ring.share_all().start()

    def second_three(self, u):
        for ring in self.three[u]:
            ring.second()
        for ring in self.three[u]:
            for k in range(2):
                ring.share(k).start()

    def third_three(self, u):
        for ring in self.three[u]:
            ring.third()
            for k in range(2, 4):
                ring.share(k).start()

    def ready(self, u):
        for ring in self.two[u]:
            ring.share_all().wait()
            ring.finish()
        for ring in self.three[u]:
            for k in range(4):
                ring.share(k).wait()
            ring.finish()

    def finish(self):
        for ring in self.one + self.small:
            ring.finish()


def gather_semaphores():
    return [DMA((KINDS, 3, 4)), DMA((KINDS, 3, 4)), DMA((6, 3, 5)), DMA((6, 3, 5)), DMA((6, 3, 8)), DMA((6, 3, 8)),
            DMA((3, 4)), DMA((3, 4))]


def blockwise(shape, body):
    lead = shape[:-2]
    if not lead:
        body(())
        return

    def step(i, _):
        body((i // lead[1], i % lead[1]) if len(lead) == 2 else (i,))
        return 0

    total = 1
    for size in lead:
        total *= size
    lax.fori_loop(0, total, step, 0)


def add_to(dst, first, *others):
    def body(index):
        if len(others) == 1 and dst.dtype == BF16:
            dst[index] = first[index] + others[0][index]
            return
        total = first[index].astype(F32)
        for other in others:
            total = total + other[index].astype(F32)
        dst[index] = total.astype(dst.dtype)

    blockwise(dst.shape, body)


class Fold:
    def __init__(self, place, order, phase, work, half_in, full_in, dst, start, count, half, send, recv):
        self.place, self.work, self.half_in, self.full_in, self.dst = place, work, half_in, full_in, dst
        self.axis, self.whole = order[2 - phase], order[: 2 - phase]
        self.axes = tuple(a for a in AXES if a not in order[3 - phase :])
        self.start, self.count = start, count
        self.halves = ((start, half), (start + half, count - half))
        self.send, self.recv = send, recv
        self.lead = (slice(None),) * (2 - phase)

    def piece(self, by, start, count, ref=None):
        ref = self.work if ref is None else ref
        return region(ref, self.axes, self.place.shifted(self.axis, by), self.whole, start, count)

    def half_copy(self, i):
        src = self.piece(2, *self.halves[i])
        dst = self.half_in.at[self.lead + (pl.ds(*self.halves[i]),)]
        return remote(src, dst, self.send.at[i], self.recv.at[i], self.place.neighbour(self.axis, (1, -1)[i]))

    def arrived(self, i):
        return self.full_in.at[(i,) + self.lead + (pl.ds(self.start, self.count),)]

    def whole_copy(self, i):
        by = (1, -1)[i]
        src = self.piece(by, self.start, self.count)
        return remote(src, self.arrived(i), self.send.at[2 + i], self.recv.at[2 + i], self.place.neighbour(self.axis, by))

    def opposite(self):
        for i in range(2):
            self.half_copy(i).start()

    def sides(self):
        for i in range(2):
            self.half_copy(i).wait_recv()
            ref = self.piece((1, -1)[i], *self.halves[i])
            add_to(ref, ref, self.half_in.at[self.lead + (pl.ds(*self.halves[i]),)])
            self.whole_copy(i).start()

    def centre(self):
        for i in range(2):
            self.whole_copy(i).wait_recv()
        add_to(self.dst, self.piece(0, self.start, self.count), self.arrived(0), self.arrived(1))

    def finish(self):
        for i in range(2):
            self.half_copy(i).wait_send()
            self.whole_copy(i).wait_send()


class Scatter:
    def __init__(self, place, kind, layer, stage, first, second, third, out, result, sems):
        self.place, self.stage = place, stage
        self.work, self.twin, reduced, inner = first[0], first[1], second[0], third[0]
        self.out, self.result = out, result
        (self.near, self.far_send, self.far_recv, send, recv, self.show_send, self.show_recv, self.local) = sems
        base = pl.multiple_of(place.core * CORE, CORE)

        def parts(phase, work, half_in, full_in, dst_of):
            return [
                Fold(place, ORDERS[p], phase, work, half_in, full_in, dst_of(start, count), start, count,
                     count // 2 if count == 32 else (16, 32)[(p + layer) % 2], send.at[phase, p], recv.at[phase, p])
                for p, (start, count) in enumerate(CUTS[kind])
            ]

        self.one = parts(0, self.work, first[2], first[3], lambda start, count: reduced.at[:, :, pl.ds(start, count)])
        self.two = parts(1, reduced, second[1], second[2], lambda start, count: inner.at[:, pl.ds(start, count)])
        self.three = parts(2, inner, third[1], third[2], lambda start, count: out.at[pl.ds(base + start, count)])

    def stay(self, step):
        slot = step % 2
        return pltpu.make_async_copy(self.stage.at[slot, :, :, self.place.mine], self.work.at[step], self.near.at[slot])

    def go(self, step):
        slot = step % 2
        return remote(self.stage.at[slot, :, :, self.place.other], self.twin.at[step], self.far_send.at[slot],
                      self.far_recv.at[step], self.place.sibling())

    def free(self, step):
        self.stay(step).wait()
        self.go(step).wait_send()

    def hand_over(self, step):
        self.stay(step).start()
        self.go(step).start()

    def handed(self):
        for step in (STEPS - 2, STEPS - 1):
            self.free(step)
        for step in range(STEPS):
            self.go(step).wait_recv()

    def join(self, *which):
        for by in which:
            for part in self.one:
                ref = part.piece(by, part.start, part.count)
                add_to(ref, ref, part.piece(by, part.start, part.count, self.twin))

    def each(self, name, parts):
        for part in parts:
            getattr(part, name)()

    def show(self):
        ref = self.out.at[self.place.mine]
        return remote(ref, ref, self.show_send, self.show_recv, self.place.sibling())

    def keep(self):
        return pltpu.make_async_copy(self.out, self.result, self.local)

    def open(self):
        self.handed()
        self.join(2)
        self.each("opposite", self.one)
        self.join(1, -1)

    def sides_one(self):
        self.each("sides", self.one)
        self.join(0)

    def centre_one(self):
        self.each("centre", self.one)
        self.each("finish", self.one)

    def start_two(self):
        self.each("opposite", self.two)

    def sides_two(self):
        self.each("sides", self.two)

    def centre_two(self):
        self.each("centre", self.two)
        self.each("opposite", self.three)

    def sides_three(self):
        self.each("sides", self.three)

    def centre_three(self):
        self.each("centre", self.three)
        self.show().start()
        self.each("finish", self.two)
        self.each("finish", self.three)

    def finish(self):
        self.show().wait()
        self.keep().start()
        self.keep().wait()


def first_buffers():
    blocks = (RING,) * 3 + (CORE, 256)
    return [pltpu.VMEM(blocks, BF16), pltpu.VMEM(blocks, BF16), pltpu.VMEM(blocks[1:], BF16), pltpu.VMEM((2,) + blocks[1:], BF16)]


def later_buffers():
    def some(*lead):
        return pltpu.VMEM(lead + (CORE, 256), BF16)

    return [some(RING, RING), some(RING), some(2, RING), some(RING), some(), some(2)]


def scatter_semaphores():
    return [DMA((2,)), DMA((2,)), DMA((STEPS,)), DMA((3, 3, 4)), DMA((3, 3, 4)), DMA, DMA, DMA]


class Turn:
    def __init__(self, place, src, dst, send, recv, local):
        self.place, self.src, self.dst, self.send, self.recv, self.local = place, src, dst, send, recv, local

    def copies(self):
        row = self.place.at["x"]
        return [
            remote(self.src.at[self.place.shifted("x", by)["x"]], self.dst.at[row], self.send.at[k], self.recv.at[k],
                   self.place.neighbour("x", by))
            for k, (_, by) in enumerate(ROW_PEERS)
        ]

    def own(self):
        row = self.place.at["x"]
        return pltpu.make_async_copy(self.src.at[row], self.dst.at[row], self.local)

    def start(self):
        self.own().start()
        for copy in self.copies():
            copy.start()

    def end(self):
        self.own().wait()
        for copy in self.copies():
            copy.wait()


TURN_SEMAPHORES = [DMA((3,)), DMA((3,)), DMA]


class Total:
    def __init__(self, place, mine, out, result, slots, core_in, send, recv, core_sems):
        self.place, self.mine, self.out, self.result, self.slots = place, mine, out, result, slots
        self.send, self.recv, self.core_in, self.core_sems = send, recv, core_in, core_sems
        rows = mine.shape[0] // 2
        self.half = pl.ds(pl.multiple_of(place.core * rows, rows), rows)
        self.away = pl.ds(pl.multiple_of((1 - place.core) * rows, rows), rows)

    def core_copy(self):
        return remote(self.mine.at[self.away], self.core_in, self.core_sems.at[0], self.core_sems.at[1], self.place.sibling())

    def copies(self, k):
        axis = "xyz"[k]
        slot = self.slots.at[k, self.place.at[axis]]
        return [
            remote(slot, slot, self.send.at[k, j], self.recv.at[k, j], self.place.neighbour(axis, by))
            for j, by in enumerate((1, 2, -1))
        ]

    def start(self):
        self.core_copy().start()

    def core_sum(self):
        self.core_copy().wait_recv()
        self.put(0, self.mine[self.half] + self.core_in[...])

    def put(self, k, value):
        self.slots[k, self.place.at["xyz"[k]]] = value
        for copy in self.copies(k):
            copy.start()

    def take(self, k):
        for copy in self.copies(k):
            copy.wait_recv()
        return (self.slots[k, 0] + self.slots[k, 1]) + (self.slots[k, 2] + self.slots[k, 3])

    def out_copy(self):
        ref = self.out.at[self.half]
        return remote(ref, ref, self.core_sems.at[2], self.core_sems.at[3], self.place.sibling())

    def last(self):
        self.out[self.half] = self.take(2)
        self.out_copy().start()

    def finish(self):
        self.core_copy().wait_send()
        for k in range(3):
            for copy in self.copies(k):
                copy.wait_send()
        self.out_copy().wait()
        copy = pltpu.make_async_copy(self.out, self.result, self.core_sems.at[4])
        copy.start()
        copy.wait()


def total_buffers(rows):
    return [pltpu.VMEM((rows, 1024), F32), pltpu.VMEM((3, RING, rows // 2, 1024), F32), pltpu.VMEM((rows // 2, 1024), F32),
            DMA((3, 3)), DMA((3, 3)), DMA((5,))]


TOTAL_PEERS = NEAR + tuple((axis, 2) for axis in "xyz")


HEAD = 64
SEQ = 197
ROWS = 208
WIDTH = 1024
BLOCKS = RING
FF_HALF = 128
QKV = 192
EPS = 1e-06
SMALL = 16
SUM_ROWS = 32
LAYER_SUMS = 14


def wide(block):
    return jnp.concatenate([block[i] for i in range(RING)], axis=1)


def tall(ref, start, rows):
    return jnp.concatenate([wide(ref[j, :, start : start + rows, :]) for j in range(BLOCKS)], axis=0)


def as_rows(ref):
    return wide(ref[...]).astype(F32)


def put_rows(ref, value):
    for i in range(RING):
        ref[i] = value[:, i * 256 : (i + 1) * 256].astype(ref.dtype)


def store_blocks(stage, slot, start, value):
    rows = value.shape[0] // BLOCKS
    for j in range(BLOCKS):
        for i in range(RING):
            block = value[j * rows : (j + 1) * rows, i * 256 : (i + 1) * 256]
            stage[slot, j, i, start : start + rows, :] = block.astype(stage.dtype)


def feature_row(small, layer, row):
    return jnp.concatenate([small[0, 0, 0, i, 8 * layer + row : 8 * layer + row + 1, :] for i in range(RING)], axis=1)


def here_row(small, step, layer, row, start, width):
    at = 8 * layer + row
    return jnp.concatenate([small[0, step, j, 0, at : at + 1, start : start + width] for j in range(BLOCKS)], axis=1)


def dot_nt(a, b):
    return lax.dot_general(a, b, (((1,), (1,)), ((), ())), preferred_element_type=F32)


def dot_nn(a, b):
    return lax.dot_general(a, b, (((1,), (0,)), ((), ())), preferred_element_type=F32)


def dot_tn(a, b):
    return lax.dot_general(a, b, (((0,), (0,)), ((), ())), preferred_element_type=F32)


def norm_parts(x):
    average = jnp.mean(x, axis=1, keepdims=True)
    centered = x - average
    inverse = lax.rsqrt(jnp.mean(centered * centered, axis=1, keepdims=True) + EPS)
    return centered * inverse, inverse


def norm_low(x, small, layer, j):
    normed, _ = norm_parts(x)
    return (normed * feature_row(small, layer, j) + feature_row(small, layer, 2 + j)).astype(BF16)


def norm_back(incoming, x, gain):
    normed, inverse = norm_parts(x)
    scaled = incoming * gain
    mean = jnp.mean(scaled, axis=1, keepdims=True)
    along = jnp.mean(scaled * normed, axis=1, keepdims=True)
    result = inverse * (scaled - mean - normed * along)
    return result, jnp.sum(incoming * normed, axis=0, keepdims=True), jnp.sum(incoming, axis=0, keepdims=True)


def softmax(queries, keys):
    scores = dot_nt(queries, keys) * HEAD**-0.5
    column = lax.broadcasted_iota(jnp.int32, scores.shape, 1)
    scores = jnp.where(column < SEQ, scores, -1e30)
    highest = jnp.max(scores, axis=1, keepdims=True)
    expon = jnp.exp(scores - highest)
    return expon * (1.0 / jnp.sum(expon, axis=1, keepdims=True))


def head_parts(mixed, j):
    at = j * QKV
    return mixed[:, at : at + HEAD], mixed[:, at + HEAD : at + 2 * HEAD], mixed[:, at + 2 * HEAD : at + QKV]


class Stream:
    def __init__(self, pairs, sems):
        self.pairs, self.sems = pairs, sems

    def copies(self, step):
        slot = step % 2
        return [
            pltpu.make_async_copy(source(step), slots.at[slot], self.sems.at[slot, k])
            for k, (source, slots) in enumerate(self.pairs)
        ]

    def start(self, step):
        for copy in self.copies(step):
            copy.start()

    def run(self, body, hooks):
        def one(step, _):
            for copy in self.copies(step):
                copy.wait()

            @pl.when(step + 1 < STEPS)
            def _():
                self.start(step + 1)

            body(step, step % 2)
            for at in sorted(hooks):
                @pl.when(step == at)
                def _(at=at):
                    for act in hooks[at]:
                        act()
            return 0

        self.start(0)
        lax.fori_loop(0, STEPS, one, 0)


ORDER = [(0, 0), (1, 0), (2, 0), (0, 1), (1, 1), (2, 1)]
SAVED = [
    jax.ShapeDtypeStruct((2, STEPS, ROWS, BLOCKS * QKV), BF16),
    jax.ShapeDtypeStruct((2, STEPS, ROWS, BLOCKS * HEAD), BF16),
    jax.ShapeDtypeStruct((2, STEPS, BLOCKS, ROWS, ROWS), BF16),
    jax.ShapeDtypeStruct((2, 2, STEPS, ROWS, BLOCKS * FF_HALF), BF16),
    jax.ShapeDtypeStruct((2, 2, STEPS, ROWS, BLOCKS * FF_HALF), BF16),
]
TOKENS = jax.ShapeDtypeStruct((ROWS, WIDTH), F32)
TURNED = jax.ShapeDtypeStruct((RING, ROWS, 256), BF16)
WEIGHTS = jax.ShapeDtypeStruct((6, RING, RING, RING, UNIT, 256), BF16)
SMALLS = jax.ShapeDtypeStruct((1, RING, RING, RING, SMALL, 256), F32)


def scratch_like(shape):
    return pltpu.VMEM(shape.shape, shape.dtype)


def forward_kernel(own_ref, small_ref, tokens_ref, cotangent_ref, full, small_out, x0_out, g_out, mid_out, x1_out, end_out,
                   mixed_out, att_out, probs_out, act_out, slope_out,
                   small, x0, resid, low, acc, mids, ends, slots, mixed_all, att_all, probs_all, act_all, slope_all, *sems):
    place = Place()
    turn_x, turn_g = Turn(place, tokens_ref, x0, *sems[0:3]), Turn(place, cotangent_ref, g_out, *sems[3:6])
    load, saves, misc = sems[6:9]
    gather = Gather(place, own_ref, full, small_ref, small, sems[9:])
    units = [number(*pair) for pair in ORDER]

    own_copies = [
        pltpu.make_async_copy(own_ref.at[:, place.mine],
                              full.at[:, place.at["y"], place.at["z"], place.at["x"], place.mine], misc.at[0]),
        pltpu.make_async_copy(small_ref, small.at[:, place.at["y"], place.at["z"], place.at["x"]], misc.at[1]),
    ]
    for copy in own_copies:
        copy.start()
    place.greet(NEAR + (("x", 2),))
    gather.begin()
    turn_x.start()
    for copy in own_copies:
        copy.wait()
    gather.small_phase(1, "first")
    gather.first_two(units[0])
    gather.second_two(units[0])
    gather.small_phase(1, "second")
    gather.first_two(units[1])
    gather.third_two(units[0])
    gather.first_three(units[0])
    gather.small_phase(1, "third")
    gather.small_phase(2, "first")
    gather.second_two(units[1])
    gather.first_two(units[2])
    gather.third_two(units[1])
    gather.small_phase(2, "second")
    gather.second_three(units[0])
    gather.first_three(units[1])
    gather.small_phase(2, "third")
    turn_x.end()
    resid[...] = as_rows(x0)
    gather.third_three(units[0])
    gather.ready(units[0])
    kept = []

    def keep(src, dst, k):
        copy = pltpu.make_async_copy(src, dst, misc.at[k])
        copy.start()
        kept.append((src, dst, k))

    keep(x0, x0_out, 2)
    keep(small, small_out, 3)
    turn_g.start()

    for k, (kind, layer) in enumerate(ORDER):
        unit = units[k]
        hooks = {0: [], 1: [], 3: []}
        if k + 2 < 6:
            hooks[0] += [functools.partial(gather.second_two, units[k + 2])]
            if k + 3 < 6:
                hooks[0] += [functools.partial(gather.first_two, units[k + 3])]
            hooks[0] += [functools.partial(gather.third_two, units[k + 2])]
        if k + 1 < 6:
            hooks[1] += [functools.partial(gather.second_three, units[k + 1])]
            if k + 2 < 6:
                hooks[1] += [functools.partial(gather.first_three, units[k + 2])]
            hooks[3] += [functools.partial(gather.third_three, units[k + 1]), functools.partial(gather.ready, units[k + 1])]

        def save(which, src, dst, step):
            return pltpu.make_async_copy(src, dst, saves.at[which, k, step])

        if kind == 0:
            low[...] = norm_low(resid[...], small, layer, 0)
            acc[...] = resid[...] + feature_row(small, layer, 4)

            def body(step, slot):
                weights = slots.at[slot]
                mixed = dot_nt(low[...], tall(weights, 0, QKV)) + here_row(small, step, layer, 7, 0, QKV)
                mixed = mixed.astype(BF16)
                mixed_all[layer, step] = mixed
                attended = []
                for j in range(BLOCKS):
                    queries, keys, values = head_parts(mixed, j)
                    probs = softmax(queries, keys).astype(BF16)
                    probs_all[layer, step, j] = probs
                    attended.append(dot_nn(probs, values).astype(BF16))
                attended = jnp.concatenate(attended, axis=1)
                att_all[layer, step] = attended
                acc[...] += dot_nn(attended, tall(weights, QKV, HEAD))
                for copy in copies(step):
                    copy.start()

            def copies(step):
                pairs = ((mixed_all, mixed_out), (att_all, att_out), (probs_all, probs_out))
                return [save(i, src.at[layer, step], dst.at[layer, step], step) for i, (src, dst) in enumerate(pairs)]
        else:
            half = kind - 1
            if half == 0:
                mids[layer] = acc[...]
                resid[...] = acc[...]
                low[...] = norm_low(resid[...], small, layer, 1)
                acc[...] = resid[...] + feature_row(small, layer, 5)
                keep(mids.at[layer], mid_out.at[layer], 4 + layer)

            def body(step, slot):
                weights = slots.at[slot]
                upward = dot_nt(low[...], tall(weights, 0, FF_HALF)) + here_row(small, step, layer, 6, half * FF_HALF, FF_HALF)
                below = 0.5 + 0.5 * lax.erf(upward * 2**-0.5)
                activated = (upward * below).astype(BF16)
                act_all[layer, half, step] = activated
                slope = below + upward * (jnp.exp(-0.5 * upward * upward) * (2 * jnp.pi) ** -0.5)
                slope_all[layer, half, step] = slope.astype(BF16)
                acc[...] += dot_nn(activated, tall(weights, FF_HALF, FF_HALF))
                for copy in copies(step):
                    copy.start()

            def copies(step):
                pairs = ((act_all, act_out), (slope_all, slope_out))
                return [save(i, src.at[layer, half, step], dst.at[layer, half, step], step) for i, (src, dst) in enumerate(pairs)]

        Stream([(lambda step: full.at[unit, step], slots)], load.at[k]).run(body, hooks)
        for step in range(STEPS):
            for copy in copies(step):
                copy.wait()
        if kind == 2 and layer == 0:
            resid[...] = acc[...]
            keep(resid, x1_out, 6)
            pltpu.make_async_copy(resid, x1_out, misc.at[6]).wait()
            kept.pop()
    put_rows(ends, acc[...])
    keep(ends, end_out, 7)
    turn_g.end()
    gather.finish()
    for src, dst, k in kept:
        pltpu.make_async_copy(src, dst, misc.at[k]).wait()


def forward(own, small, tokens, cotangent):
    both = jax.ShapeDtypeStruct((2, ROWS, WIDTH), F32)
    return pl.pallas_call(
        forward_kernel,
        out_shape=[WEIGHTS, SMALLS, TURNED, TURNED, both, TOKENS, TURNED, *SAVED],
        in_specs=[VMEM] * 4,
        out_specs=[ANY] * 12,
        scratch_shapes=[
            scratch_like(SMALLS), scratch_like(TURNED), scratch_like(TOKENS), pltpu.VMEM((ROWS, WIDTH), BF16),
            scratch_like(TOKENS), scratch_like(both), scratch_like(TURNED), pltpu.VMEM((2, RING, RING, UNIT, 256), BF16),
            *[scratch_like(s) for s in SAVED],
            *TURN_SEMAPHORES, *TURN_SEMAPHORES, DMA((6, 2, 1)), DMA((3, 6, STEPS)), DMA((8,)),
            *gather_semaphores(),
        ],
        compiler_params=pltpu.CompilerParams(vmem_limit_bytes=VMEM_LIMIT, collective_id=0, has_side_effects=True),
        name="forward",
    )(own, small, tokens, cotangent)


BACK = [(2, 1), (1, 1), (0, 1), (2, 0), (1, 0), (0, 0)]


def backward_kernel(full, small, x0_ref, g_ref, mid_ref, x1_ref, end_ref, mixed_in, att_in, probs_in, act_in, slope_in,
                    encoded_out, tokens_out, grads_out, sums_out,
                    grad, low, here, acc, turned, sums, columns_all, slots, mixed_two, att_two, probs_two, act_two, slope_two, stage, outs,
                    *rest):
    first = [rest[0:4], rest[4:8]]
    later = [rest[8:14], rest[14:20]]
    total_scratch, sems = rest[20:26], rest[26:]
    place = Place()
    turn_out, turn_g = Turn(place, end_ref, encoded_out, *sems[0:3]), Turn(place, turned, tokens_out, *sems[3:6])
    load, free = sems[6:8]
    unit_sems = [[group.at[k] for group in sems[8:]] for k in range(6)]
    scatters = []
    for k, (kind, layer) in enumerate(BACK):
        scatters.append(
            Scatter(place, kind, layer, stage, first[k % 2], later[k % 2][0:3], later[k % 2][3:6], outs.at[k],
                    grads_out.at[number(kind, layer)], unit_sems[k])
        )
    total = Total(place, sums, total_scratch[0], sums_out, *total_scratch[1:])
    place.greet(TOTAL_PEERS)
    turn_out.start()
    grad[...] = as_rows(g_ref)
    sums[...] = jnp.zeros_like(sums)
    columns_all[...] = jnp.zeros_like(columns_all)

    def leave(k):
        place.tell(free.at[k], NEAR)

    def may(k):
        pl.semaphore_wait(free.at[k], len(NEAR))

    for k, (kind, layer) in enumerate(BACK):
        it = scatters[k]
        hooks = {0: [], 1: [], 2: [], 3: []}
        if k >= 2:
            hooks[0] += [scatters[k - 2].sides_two]
        if k >= 1:
            hooks[1] += [scatters[k - 1].sides_one]
        if k >= 2:
            hooks[1] += [scatters[k - 2].centre_two]
            hooks[2] += [scatters[k - 2].sides_three]
        base = LAYER_SUMS * layer

        def begin(step):
            @pl.when(step >= 2)
            def _():
                it.free(step - 2)

            if k >= 2:
                @pl.when(step == 0)
                def _():
                    may(k)

        if kind == 0:
            x = as_rows(x0_ref) if layer == 0 else x1_ref[...]
            here[...] = norm_low(x, small, layer, 0)
            low[...] = grad[...].astype(BF16)
            acc[...] = jnp.zeros_like(acc)

            def body(step, slot):
                weights = slots.at[slot]
                begin(step)
                g = low[...]
                mixed = mixed_two[slot]
                store_blocks(stage, slot, QKV, dot_tn(att_two[slot], g))
                g_all = dot_nt(g, tall(weights, QKV, HEAD)).astype(BF16)
                g_mixed = []
                for j in range(BLOCKS):
                    queries, keys, values = head_parts(mixed, j)
                    g_att = g_all[:, j * HEAD : (j + 1) * HEAD]
                    probs_low = probs_two[slot, j]
                    probs = probs_low.astype(F32)
                    g_probs = dot_nt(g_att, values)
                    g_values = dot_tn(probs_low, g_att)
                    centre = jnp.sum(probs * g_probs, axis=1, keepdims=True)
                    g_scores = (probs * (g_probs - centre) * HEAD**-0.5).astype(BF16)
                    g_mixed += [dot_nn(g_scores, keys), dot_tn(g_scores, queries), g_values]
                g_mixed = jnp.concatenate([part.astype(BF16) for part in g_mixed], axis=1)
                store_blocks(stage, slot, 0, dot_tn(g_mixed, here[...]))
                it.hand_over(step)
                columns_all[layer, 1, step, :, : BLOCKS * QKV] = jnp.sum(g_mixed.astype(F32), axis=0, keepdims=True)
                acc[...] += dot_nn(g_mixed, tall(weights, 0, QKV))

            pairs = [
                (lambda step: full.at[number(kind, layer), step], slots),
                (lambda step: mixed_in.at[layer, step], mixed_two),
                (lambda step: att_in.at[layer, step], att_two),
                (lambda step: probs_in.at[layer, step], probs_two),
            ]
        else:
            half = kind - 1
            if half == 1:
                here[...] = norm_low(mid_ref[layer], small, layer, 1)
                low[...] = grad[...].astype(BF16)
                acc[...] = jnp.zeros_like(acc)

            def body(step, slot):
                weights = slots.at[slot]
                begin(step)
                g = low[...]
                store_blocks(stage, slot, FF_HALF, dot_tn(act_two[slot], g))
                g_up = (dot_nt(g, tall(weights, FF_HALF, FF_HALF)) * slope_two[slot].astype(F32)).astype(BF16)
                store_blocks(stage, slot, 0, dot_tn(g_up, here[...]))
                it.hand_over(step)
                columns = jnp.sum(g_up.astype(F32), axis=0, keepdims=True)
                for j in range(BLOCKS):
                    at = j * 2 * FF_HALF + half * FF_HALF
                    columns_all[layer, 0, step, :, at : at + FF_HALF] = columns[:, j * FF_HALF : (j + 1) * FF_HALF]
                acc[...] += dot_nn(g_up, tall(weights, 0, FF_HALF))

            pairs = [
                (lambda step: full.at[number(kind, layer), step], slots),
                (lambda step: act_in.at[layer, half, step], act_two),
                (lambda step: slope_in.at[layer, half, step], slope_two),
            ]
        Stream(pairs, load.at[k]).run(body, hooks)
        if kind < 2:
            j = kind
            x = mid_ref[layer] if kind == 1 else (as_rows(x0_ref) if layer == 0 else x1_ref[...])
            part, gain, shift = norm_back(acc[...], x, feature_row(small, layer, j))
            at = base + (8 if kind == 1 else 11)
            sums[at : at + 1, :] = jnp.sum(low[...].astype(F32), axis=0, keepdims=True)
            sums[at + 1 : at + 2, :] = gain
            sums[at + 2 : at + 3, :] = shift
            grad[...] = grad[...] + part
        if k == 5:
            put_rows(turned, grad[...])
            turn_g.start()
            for i in range(2):
                for which in range(2):
                    for step in range(STEPS):
                        at = LAYER_SUMS * i + STEPS * which + step
                        sums[at : at + 1, :] = columns_all[i, which, step]
            total.start()
        it.open()
        if k >= 1:
            scatters[k - 1].centre_one()
        if k >= 2:
            scatters[k - 2].centre_three()
        if 1 <= k <= 5:
            leave(k + 1)
        if k >= 1:
            scatters[k - 1].start_two()
    early, late = scatters[4], scatters[5]
    total.core_sum()
    early.sides_two()
    late.sides_one()
    early.centre_two()
    total.put(1, total.take(0))
    late.centre_one()
    may(6)
    late.start_two()
    early.sides_three()
    total.put(2, total.take(1))
    late.sides_two()
    early.centre_three()
    total.last()
    late.centre_two()
    late.sides_three()
    for it in scatters[:4]:
        it.finish()
    late.centre_three()
    turn_out.end()
    turn_g.end()
    total.finish()
    early.finish()
    late.finish()


def backward(full, small, x0, g, mids, x1, ends, saved):
    saved_two = [pltpu.VMEM((2,) + s.shape[-3 if len(s.shape) == 5 and s.shape[1] == STEPS else -2 :], s.dtype) for s in SAVED]
    semaphores = [pltpu.SemaphoreType.DMA((6,) + (s.shape if hasattr(s, "shape") else ())) for s in scatter_semaphores()]
    return pl.pallas_call(
        backward_kernel,
        out_shape=[TURNED, TURNED, jax.ShapeDtypeStruct((6, UNIT, 256), F32), jax.ShapeDtypeStruct((SUM_ROWS, WIDTH), F32)],
        in_specs=[ANY] + [VMEM] * 6 + [ANY] * 5,
        out_specs=[ANY] * 4,
        scratch_shapes=[
            scratch_like(TOKENS), pltpu.VMEM((ROWS, WIDTH), BF16), pltpu.VMEM((ROWS, WIDTH), BF16), scratch_like(TOKENS),
            scratch_like(TURNED), pltpu.VMEM((SUM_ROWS, WIDTH), F32), pltpu.VMEM((2, 2, STEPS, 1, WIDTH), F32),
            pltpu.VMEM((2, RING, RING, UNIT, 256), BF16),
            *saved_two,
            pltpu.VMEM((2, RING, RING, UNIT, 256), BF16), pltpu.VMEM((6, UNIT, 256), F32),
            *first_buffers(), *first_buffers(), *later_buffers(), *later_buffers(),
            *total_buffers(SUM_ROWS),
            *TURN_SEMAPHORES, *TURN_SEMAPHORES, DMA((6, 2, 4)), pltpu.SemaphoreType.REGULAR((7,)),
            *semaphores,
        ],
        compiler_params=pltpu.CompilerParams(vmem_limit_bytes=VMEM_LIMIT, collective_id=1, has_side_effects=True),
        name="backward",
    )(full, small, x0, g, mids, x1, ends, *saved)


def to_images(rows):
    return jnp.pad(rows.reshape(3, SEQ, 256), ((0, 1), (0, ROWS - SEQ), (0, 0)))


def from_images(turned):
    return turned[:3, :SEQ].reshape(3 * SEQ, 256).astype(F32)


def shards(tokens, norm_gain, norm_shift, qkv_weight, qv_bias, proj_weight, proj_bias, up_weight, up_bias, down_weight, down_bias, cotangent):
    layers = qkv_weight.shape[0]
    attention = jnp.concatenate([qkv_weight.transpose(0, 2, 1), proj_weight], axis=1)
    up = up_weight.transpose(0, 2, 1)
    halves = [jnp.concatenate([part[:, at : at + FF_HALF] for part in (up, down_weight)], axis=1) for at in (0, FF_HALF)]
    own = jnp.concatenate([attention, *halves], axis=0)
    zeros = jnp.zeros((layers, HEAD), F32)
    qkv_row = jnp.concatenate([qv_bias[:, :HEAD], zeros, qv_bias[:, HEAD:], zeros], axis=1)
    small = jnp.stack([norm_gain[:, 0], norm_gain[:, 1], norm_shift[:, 0], norm_shift[:, 1], proj_bias, down_bias, up_bias, qkv_row], axis=1)
    full, small, x0, g, mids, x1, ends, *saved = forward(
        own, small.reshape(1, SMALL, 256), to_images(tokens), to_images(cotangent.astype(BF16))
    )
    encoded, grad_tokens, grads, sums = backward(full, small, x0, g, mids, x1, ends, saved)
    row, col = lax.axis_index("row"), lax.axis_index("col")
    sums = sums[: layers * LAYER_SUMS].reshape(layers, LAYER_SUMS, WIDTH)
    up_sums = lax.dynamic_slice_in_dim(sums[:, 0:4].reshape(layers, 16, 256), col, 1, 1)[:, 0]
    qkv_sums = sums[:, 4:8, : BLOCKS * QKV].reshape(layers, 16, QKV)
    qkv_sums = lax.dynamic_slice_in_dim(qkv_sums, col, 1, 1)[:, 0]
    features = lax.dynamic_slice_in_dim(sums[:, 8:].reshape(layers, 6, RING, 256), row, 1, 2)[:, :, 0]
    attention, first, second = grads[0:2], grads[2:4], grads[4:6]
    return (
        from_images(encoded),
        from_images(grad_tokens),
        jnp.stack([features[:, 4], features[:, 1]], axis=1),
        jnp.stack([features[:, 5], features[:, 2]], axis=1),
        attention[:, :QKV].transpose(0, 2, 1),
        jnp.concatenate([qkv_sums[:, :HEAD], qkv_sums[:, 2 * HEAD : QKV]], axis=1),
        attention[:, QKV:],
        features[:, 3],
        jnp.concatenate([first[:, :FF_HALF], second[:, :FF_HALF]], axis=1).transpose(0, 2, 1),
        up_sums,
        jnp.concatenate([first[:, FF_HALF:], second[:, FF_HALF:]], axis=1),
        features[:, 0],
    )


def solution(mesh):
    in_specs = (
        P(("dp", "col"), "row"),
        P(None, None, "row"),
        P(None, None, "row"),
        P(None, "row", "col"),
        P(None, "col"),
        P(None, "col", "row"),
        P(None, "row"),
        P(None, "row", "col"),
        P(None, "col"),
        P(None, "col", "row"),
        P(None, "row"),
        P(("dp", "col"), "row"),
    )
    out_specs = (
        P(("dp", "col"), "row"),
        P(("dp", "col"), "row"),
        P(None, None, "row"),
        P(None, None, "row"),
        P(None, "row", "col"),
        P(None, "col"),
        P(None, "col", "row"),
        P(None, "row"),
        P(None, "row", "col"),
        P(None, "col"),
        P(None, "col", "row"),
        P(None, "row"),
    )
    return jax.shard_map(shards, mesh=mesh, in_specs=in_specs, out_specs=out_specs, check_vma=False)
```

```python
import functools

import jax
import jax.numpy as jnp
from jax import lax
from jax.experimental import pallas as pl
from jax.experimental.pallas import tpu as pltpu
from jax.sharding import PartitionSpec as P

MESH = pl.DeviceIdType.MESH
RING = 4
STEPS = 4
AXES = "yzx"
ORDERS = (("x", "y", "z"), ("y", "z", "x"), ("z", "x", "y"))
KINDS = 3
UNIT = 256
CORE = 128
CUTS = (((0, 48), (48, 48), (96, 32)), ((0, 48), (48, 32), (80, 48)), ((0, 32), (32, 48), (80, 48)))
NEAR = tuple((axis, by) for axis in "xyz" for by in (1, -1)) + (("core", 1),)
ROW_PEERS = (("x", 1), ("x", 2), ("x", -1))
VMEM_LIMIT = 60 * 2**20
DMA = pltpu.SemaphoreType.DMA
ANY = pl.BlockSpec(memory_space=pl.ANY)
VMEM = pl.BlockSpec(memory_space=pltpu.VMEM)
BF16 = jnp.bfloat16
F32 = jnp.float32


def number(kind, layer):
    return 2 * kind + layer


class Place:
    def __init__(self):
        self.core = lax.axis_index("dp")
        block = lax.axis_index("col")
        self.at = {"x": lax.axis_index("row"), "y": block // RING, "z": block % RING}
        self.mine = pl.ds(pl.multiple_of(self.core * CORE, CORE), CORE)
        self.other = pl.ds(pl.multiple_of((1 - self.core) * CORE, CORE), CORE)

    def shifted(self, axis, by):
        moved = dict(self.at)
        moved[axis] = (self.at[axis] + by + RING) % RING
        return moved

    def neighbour(self, axis, by):
        if axis == "core":
            return (1 - self.core, self.at["x"], self.at["y"] * RING + self.at["z"])
        at = self.shifted(axis, by)
        return (self.core, at["x"], at["y"] * RING + at["z"])

    def sibling(self):
        return self.neighbour("core", 1)

    def tell(self, semaphore, peers):
        for axis, by in peers:
            pl.semaphore_signal(semaphore, inc=1, device_id=self.neighbour(axis, by), device_id_type=MESH)

    def greet(self, peers):
        barrier = pltpu.get_barrier_semaphore()
        self.tell(barrier, peers)
        pl.semaphore_wait(barrier, len(peers))


def region(ref, axes, at, whole, start, count):
    index = tuple(pl.ds(0, RING) if a in whole else at[a] for a in axes)
    return ref.at[index + (pl.ds(start, count),)]


def remote(src, dst, send, recv, device):
    return pltpu.make_async_remote_copy(
        src_ref=src, dst_ref=dst, send_sem=send, recv_sem=recv, device_id=device, device_id_type=MESH
    )


class Ring:
    def __init__(self, place, full, units, order, phase, start, count, half, send, recv, own=None):
        self.place, self.full, self.units, self.own = place, full, units, own
        self.axis, self.whole = order[phase], order[:phase]
        self.start, self.count = start, count
        self.halves = ((start, half), (start + half, count - half))
        self.send, self.recv = send, recv

    def piece(self, by, start, count):
        at = self.place.shifted(self.axis, by)
        index = tuple(pl.ds(0, RING) if a in self.whole else at[a] for a in AXES)
        return self.full.at[(self.units,) + index + (pl.ds(start, count),)]

    def to(self, i):
        return self.place.neighbour(self.axis, (1, -1)[i])

    def whole_copy(self, i):
        here = self.piece(0, self.start, self.count)
        return remote(here if self.own is None else self.own, here, self.send.at[i], self.recv.at[i], self.to(i))

    def half_copy(self, i):
        ref = self.piece((-1, 1)[i], *self.halves[i])
        return remote(ref, ref, self.send.at[2 + i], self.recv.at[2 + i], self.to(i))

    def share(self, k):
        ref = self.piece((-1, 1)[k], self.start, self.count) if k < 2 else self.piece(2, *self.halves[k - 2])
        return remote(ref, ref, self.send.at[4 + k], self.recv.at[4 + k], self.place.sibling())

    def share_all(self):
        index = tuple(pl.ds(0, RING) if a in self.whole + (self.axis,) else self.place.at[a] for a in AXES)
        ref = self.full.at[(self.units,) + index + (pl.ds(self.start, self.count),)]
        return remote(ref, ref, self.send.at[4], self.recv.at[4], self.place.sibling())

    def first(self):
        for i in range(2):
            self.whole_copy(i).start()

    def second(self):
        for i in range(2):
            self.whole_copy(i).wait_recv()
            self.half_copy(i).start()

    def third(self):
        for i in range(2):
            self.half_copy(i).wait_recv()

    def finish(self):
        for i in range(2):
            self.whole_copy(i).wait_send()
            self.half_copy(i).wait_send()


class Gather:
    def __init__(self, place, own, full, small_own, small_full, sems):
        one_send, one_recv, two_send, two_recv, three_send, three_recv, small_send, small_recv = sems
        self.one, self.two, self.three = [], {}, {}
        base = pl.multiple_of(place.core * CORE, CORE)
        for kind in range(KINDS):
            for p, (start, count) in enumerate(CUTS[kind]):
                rows = base + start
                self.one.append(
                    Ring(place, full, pl.ds(2 * kind, 2), ORDERS[p], 0, rows, count, 16, one_send.at[kind, p],
                         one_recv.at[kind, p], own.at[pl.ds(2 * kind, 2), pl.ds(rows, count)])
                )
            for layer in range(2):
                u = number(kind, layer)
                for phase, into, send, recv in ((1, self.two, two_send, two_recv), (2, self.three, three_send, three_recv)):
                    into[u] = [
                        Ring(place, full, u, ORDERS[p], phase, base + start, count,
                             count // 2 if count == 32 else (16, 32)[(p + layer) % 2], send.at[u, p], recv.at[u, p])
                        for p, (start, count) in enumerate(CUTS[kind])
                    ]
        rows = small_own.shape[1]
        self.small = [
            Ring(place, small_full, pl.ds(0, 1), ORDERS[0], phase, 0, rows, rows // 2, small_send.at[phase],
                 small_recv.at[phase], small_own if phase == 0 else None)
            for phase in range(3)
        ]

    def begin(self):
        rings = self.one + [self.small[0]]
        for name in ("first", "second", "third"):
            for ring in rings:
                getattr(ring, name)()

    def small_phase(self, phase, name):
        getattr(self.small[phase], name)()

    def first_two(self, u):
        for ring in self.two[u]:
            ring.first()

    def second_two(self, u):
        for ring in self.two[u]:
            ring.second()

    def third_two(self, u):
        for ring in self.two[u]:
            ring.third()

    def first_three(self, u):
        for ring in self.three[u]:
            ring.first()
        for ring in self.two[u]:
            ring.share_all().start()

    def second_three(self, u):
        for ring in self.three[u]:
            ring.second()
        for ring in self.three[u]:
            for k in range(2):
                ring.share(k).start()

    def third_three(self, u):
        for ring in self.three[u]:
            ring.third()
            for k in range(2, 4):
                ring.share(k).start()

    def ready(self, u):
        for ring in self.two[u]:
            ring.share_all().wait()
            ring.finish()
        for ring in self.three[u]:
            for k in range(4):
                ring.share(k).wait()
            ring.finish()

    def finish(self):
        for ring in self.one + self.small:
            ring.finish()


def gather_semaphores():
    return [DMA((KINDS, 3, 4)), DMA((KINDS, 3, 4)), DMA((6, 3, 5)), DMA((6, 3, 5)), DMA((6, 3, 8)), DMA((6, 3, 8)),
            DMA((3, 4)), DMA((3, 4))]


def blockwise(shape, body):
    if len(shape) < 4:
        body(())
        return

    def step(i, _):
        body((i,))
        return 0

    lax.fori_loop(0, shape[0], step, 0)


def add_to(dst, first, *others):
    def body(index):
        if len(others) == 1 and dst.dtype == BF16:
            dst[index] = first[index] + others[0][index]
            return
        total = first[index].astype(F32)
        for other in others:
            total = total + other[index].astype(F32)
        dst[index] = total.astype(dst.dtype)

    blockwise(dst.shape, body)


class Fold:
    def __init__(self, place, order, phase, work, half_in, full_in, dst, start, count, half, send, recv):
        self.place, self.work, self.half_in, self.full_in, self.dst = place, work, half_in, full_in, dst
        self.axis, self.whole = order[2 - phase], order[: 2 - phase]
        self.axes = tuple(a for a in AXES if a not in order[3 - phase :])
        self.start, self.count = start, count
        self.halves = ((start, half), (start + half, count - half))
        self.send, self.recv = send, recv
        self.lead = (slice(None),) * (2 - phase)

    def piece(self, by, start, count, ref=None):
        ref = self.work if ref is None else ref
        return region(ref, self.axes, self.place.shifted(self.axis, by), self.whole, start, count)

    def half_copy(self, i):
        src = self.piece(2, *self.halves[i])
        dst = self.half_in.at[self.lead + (pl.ds(*self.halves[i]),)]
        return remote(src, dst, self.send.at[i], self.recv.at[i], self.place.neighbour(self.axis, (1, -1)[i]))

    def arrived(self, i):
        return self.full_in.at[(i,) + self.lead + (pl.ds(self.start, self.count),)]

    def whole_copy(self, i):
        by = (1, -1)[i]
        src = self.piece(by, self.start, self.count)
        return remote(src, self.arrived(i), self.send.at[2 + i], self.recv.at[2 + i], self.place.neighbour(self.axis, by))

    def opposite(self):
        for i in range(2):
            self.half_copy(i).start()

    def sides(self):
        for i in range(2):
            self.half_copy(i).wait_recv()
            ref = self.piece((1, -1)[i], *self.halves[i])
            add_to(ref, ref, self.half_in.at[self.lead + (pl.ds(*self.halves[i]),)])
            self.whole_copy(i).start()

    def centre(self):
        for i in range(2):
            self.whole_copy(i).wait_recv()
        add_to(self.dst, self.piece(0, self.start, self.count), self.arrived(0), self.arrived(1))

    def finish(self):
        for i in range(2):
            self.half_copy(i).wait_send()
            self.whole_copy(i).wait_send()


class Scatter:
    def __init__(self, place, kind, layer, stage, first, second, third, out, result, sems):
        self.place, self.stage = place, stage
        self.work, self.twin, reduced, inner = first[0], first[1], second[0], third[0]
        self.out, self.result = out, result
        (self.near, self.far_send, self.far_recv, send, recv, self.show_send, self.show_recv, self.local) = sems
        base = pl.multiple_of(place.core * CORE, CORE)

        def parts(phase, work, half_in, full_in, dst_of):
            return [
                Fold(place, ORDERS[p], phase, work, half_in, full_in, dst_of(start, count), start, count,
                     count // 2 if count == 32 else (16, 32)[(p + layer) % 2], send.at[phase, p], recv.at[phase, p])
                for p, (start, count) in enumerate(CUTS[kind])
            ]

        self.one = parts(0, self.work, first[2], first[3], lambda start, count: reduced.at[:, :, pl.ds(start, count)])
        self.two = parts(1, reduced, second[1], second[2], lambda start, count: inner.at[:, pl.ds(start, count)])
        self.three = parts(2, inner, third[1], third[2], lambda start, count: out.at[pl.ds(base + start, count)])

    def stay(self, step):
        slot = step % 2
        return pltpu.make_async_copy(self.stage.at[slot, :, :, self.place.mine], self.work.at[step], self.near.at[slot])

    def go(self, step):
        slot = step % 2
        return remote(self.stage.at[slot, :, :, self.place.other], self.twin.at[step], self.far_send.at[slot],
                      self.far_recv.at[step], self.place.sibling())

    def free(self, step):
        self.stay(step).wait()
        self.go(step).wait_send()

    def hand_over(self, step):
        self.stay(step).start()
        self.go(step).start()

    def free_last(self):
        for step in (STEPS - 2, STEPS - 1):
            self.free(step)

    def join(self, *which):
        for by in which:
            for part in self.one:
                ref = part.piece(by, part.start, part.count)
                add_to(ref, ref, part.piece(by, part.start, part.count, self.twin))

    def each(self, name, parts):
        for part in parts:
            getattr(part, name)()

    def show(self):
        ref = self.out.at[self.place.mine]
        return remote(ref, ref, self.show_send, self.show_recv, self.place.sibling())

    def keep(self):
        return pltpu.make_async_copy(self.out, self.result, self.local)

    def open(self):
        for step in range(STEPS):
            self.go(step).wait_recv()
        self.join(2)
        self.each("opposite", self.one)
        self.join(1, -1)

    def sides_one(self):
        self.each("sides", self.one)
        self.join(0)

    def centre_one(self):
        self.each("centre", self.one)
        self.each("finish", self.one)

    def start_two(self):
        self.each("opposite", self.two)

    def sides_two(self):
        self.each("sides", self.two)

    def centre_two(self):
        self.each("centre", self.two)
        self.each("opposite", self.three)

    def sides_three(self):
        self.each("sides", self.three)

    def centre_three(self):
        self.each("centre", self.three)
        self.show().start()
        self.each("finish", self.two)
        self.each("finish", self.three)

    def shown(self):
        self.show().wait()
        self.keep().start()


def first_buffers():
    blocks = (RING,) * 3 + (CORE, 256)
    return [pltpu.VMEM(blocks, BF16), pltpu.VMEM(blocks, BF16)]


def pair_buffers():
    blocks = (RING,) * 2 + (CORE, 256)
    return [pltpu.VMEM(blocks, BF16), pltpu.VMEM((2,) + blocks, BF16)]


def later_buffers():
    def some(*lead):
        return pltpu.VMEM(lead + (CORE, 256), BF16)

    return [some(RING, RING), some(RING), some(2, RING), some(RING), some(), some(2)]


def scatter_semaphores():
    return [DMA((2,)), DMA((2,)), DMA((STEPS,)), DMA((3, 3, 4)), DMA((3, 3, 4)), DMA, DMA, DMA]


class Turn:
    def __init__(self, place, src, dst, send, recv, local):
        self.place, self.src, self.dst, self.send, self.recv, self.local = place, src, dst, send, recv, local

    def copies(self):
        row = self.place.at["x"]
        return [
            remote(self.src.at[self.place.shifted("x", by)["x"]], self.dst.at[row], self.send.at[k], self.recv.at[k],
                   self.place.neighbour("x", by))
            for k, (_, by) in enumerate(ROW_PEERS)
        ]

    def own(self):
        row = self.place.at["x"]
        return pltpu.make_async_copy(self.src.at[row], self.dst.at[row], self.local)

    def start(self):
        self.own().start()
        for copy in self.copies():
            copy.start()

    def end(self):
        self.own().wait()
        for copy in self.copies():
            copy.wait()


TURN_SEMAPHORES = [DMA((3,)), DMA((3,)), DMA]


class Total:
    def __init__(self, place, mine, out, result, slots, core_in, send, recv, core_sems):
        self.place, self.mine, self.out, self.result, self.slots = place, mine, out, result, slots
        self.send, self.recv, self.core_in, self.core_sems = send, recv, core_in, core_sems
        rows = mine.shape[0] // 2
        self.half = pl.ds(pl.multiple_of(place.core * rows, rows), rows)
        self.away = pl.ds(pl.multiple_of((1 - place.core) * rows, rows), rows)

    def core_copy(self):
        return remote(self.mine.at[self.away], self.core_in, self.core_sems.at[0], self.core_sems.at[1], self.place.sibling())

    def copies(self, k):
        axis = "xyz"[k]
        slot = self.slots.at[k, self.place.at[axis]]
        return [
            remote(slot, slot, self.send.at[k, j], self.recv.at[k, j], self.place.neighbour(axis, by))
            for j, by in enumerate((1, 2, -1))
        ]

    def start(self):
        self.core_copy().start()

    def core_sum(self):
        self.core_copy().wait_recv()
        self.put(0, self.mine[self.half] + self.core_in[...])

    def put(self, k, value):
        self.slots[k, self.place.at["xyz"[k]]] = value
        for copy in self.copies(k):
            copy.start()

    def take(self, k):
        for copy in self.copies(k):
            copy.wait_recv()
        return (self.slots[k, 0] + self.slots[k, 1]) + (self.slots[k, 2] + self.slots[k, 3])

    def out_copy(self):
        ref = self.out.at[self.half]
        return remote(ref, ref, self.core_sems.at[2], self.core_sems.at[3], self.place.sibling())

    def last(self):
        self.out[self.half] = self.take(2)
        self.out_copy().start()

    def finish(self):
        self.core_copy().wait_send()
        for k in range(3):
            for copy in self.copies(k):
                copy.wait_send()
        self.out_copy().wait()
        copy = pltpu.make_async_copy(self.out, self.result, self.core_sems.at[4])
        copy.start()
        copy.wait()


def total_buffers(rows):
    return [pltpu.VMEM((rows, 1024), F32), pltpu.VMEM((3, RING, rows // 2, 1024), F32), pltpu.VMEM((rows // 2, 1024), F32),
            DMA((3, 3)), DMA((3, 3)), DMA((5,))]


TOTAL_PEERS = NEAR + tuple((axis, 2) for axis in "xyz")


HEAD = 64
SEQ = 197
ROWS = 208
WIDTH = 1024
BLOCKS = RING
FF_HALF = 128
QKV = 192
EPS = 1e-06
SMALL = 16
SUM_ROWS = 32
LAYER_SUMS = 14


def wide(block):
    return jnp.concatenate([block[i] for i in range(RING)], axis=1)


def tall(ref, start, rows):
    return jnp.concatenate([wide(ref[j, :, start : start + rows, :]) for j in range(BLOCKS)], axis=0)


def as_rows(ref):
    return wide(ref[...]).astype(F32)


def put_rows(ref, value):
    for i in range(RING):
        ref[i] = value[:, i * 256 : (i + 1) * 256].astype(ref.dtype)


def store_blocks(stage, slot, start, value):
    rows = value.shape[0] // BLOCKS
    for j in range(BLOCKS):
        for i in range(RING):
            block = value[j * rows : (j + 1) * rows, i * 256 : (i + 1) * 256]
            stage[slot, j, i, start : start + rows, :] = block.astype(stage.dtype)


def feature_row(small, layer, row):
    return jnp.concatenate([small[0, 0, 0, i, 8 * layer + row : 8 * layer + row + 1, :] for i in range(RING)], axis=1)


def here_row(small, step, layer, row, start, width):
    at = 8 * layer + row
    return jnp.concatenate([small[0, step, j, 0, at : at + 1, start : start + width] for j in range(BLOCKS)], axis=1)


def dot_nt(a, b):
    return lax.dot_general(a, b, (((1,), (1,)), ((), ())), preferred_element_type=F32)


def dot_nn(a, b):
    return lax.dot_general(a, b, (((1,), (0,)), ((), ())), preferred_element_type=F32)


def dot_tn(a, b):
    return lax.dot_general(a, b, (((0,), (0,)), ((), ())), preferred_element_type=F32)


def norm_parts(x):
    average = jnp.mean(x, axis=1, keepdims=True)
    centered = x - average
    inverse = lax.rsqrt(jnp.mean(centered * centered, axis=1, keepdims=True) + EPS)
    return centered * inverse, inverse


def norm_low(x, small, layer, j):
    normed, _ = norm_parts(x)
    return (normed * feature_row(small, layer, j) + feature_row(small, layer, 2 + j)).astype(BF16)


def norm_back(incoming, x, gain):
    normed, inverse = norm_parts(x)
    scaled = incoming * gain
    mean = jnp.mean(scaled, axis=1, keepdims=True)
    along = jnp.mean(scaled * normed, axis=1, keepdims=True)
    result = inverse * (scaled - mean - normed * along)
    return result, jnp.sum(incoming * normed, axis=0, keepdims=True), jnp.sum(incoming, axis=0, keepdims=True)


def softmax(queries, keys):
    scores = dot_nt(queries, keys) * HEAD**-0.5
    column = lax.broadcasted_iota(jnp.int32, scores.shape, 1)
    scores = jnp.where(column < SEQ, scores, -1e30)
    highest = jnp.max(scores, axis=1, keepdims=True)
    expon = jnp.exp(scores - highest)
    return expon * (1.0 / jnp.sum(expon, axis=1, keepdims=True))


def head_parts(mixed, j):
    at = j * QKV
    return mixed[:, at : at + HEAD], mixed[:, at + HEAD : at + 2 * HEAD], mixed[:, at + 2 * HEAD : at + QKV]


class Stream:
    def __init__(self, pairs, sems):
        self.pairs, self.sems = pairs, sems

    def copies(self, step):
        slot = step % 2
        return [
            pltpu.make_async_copy(source(step), slots.at[slot], self.sems.at[slot, k])
            for k, (source, slots) in enumerate(self.pairs)
        ]

    def start(self, step):
        for copy in self.copies(step):
            copy.start()

    def run(self, body, hooks):
        def one(step, _):
            for copy in self.copies(step):
                copy.wait()

            @pl.when(step + 1 < STEPS)
            def _():
                self.start(step + 1)

            body(step, step % 2)
            for at in sorted(hooks):
                @pl.when(step == at)
                def _(at=at):
                    for act in hooks[at]:
                        act()
            return 0

        self.start(0)
        lax.fori_loop(0, STEPS, one, 0)


ORDER = [(0, 0), (1, 0), (2, 0), (0, 1), (1, 1), (2, 1)]
SAVED = [
    jax.ShapeDtypeStruct((2, STEPS, ROWS, BLOCKS * QKV), BF16),
    jax.ShapeDtypeStruct((2, STEPS, ROWS, BLOCKS * HEAD), BF16),
    jax.ShapeDtypeStruct((2, STEPS, BLOCKS, ROWS, ROWS), BF16),
    jax.ShapeDtypeStruct((2, 2, STEPS, ROWS, BLOCKS * FF_HALF), BF16),
    jax.ShapeDtypeStruct((2, 2, STEPS, ROWS, BLOCKS * FF_HALF), BF16),
]
TOKENS = jax.ShapeDtypeStruct((ROWS, WIDTH), F32)
TURNED = jax.ShapeDtypeStruct((RING, ROWS, 256), BF16)
LOWS = jax.ShapeDtypeStruct((2, 2, ROWS, WIDTH), BF16)
WEIGHTS = jax.ShapeDtypeStruct((6, RING, RING, RING, UNIT, 256), BF16)
SMALLS = jax.ShapeDtypeStruct((1, RING, RING, RING, SMALL, 256), F32)


def scratch_like(shape):
    return pltpu.VMEM(shape.shape, shape.dtype)


def forward_kernel(own_ref, small_ref, tokens_ref, cotangent_ref, full, small_out, x0_out, g_out, mid_out, x1_out, end_out, low_out,
                   mixed_out, att_out, probs_out, act_out, slope_out,
                   small, x0, resid, lows, acc, mids, ends, slots, mixed_all, att_all, probs_all, act_all, slope_all, *sems):
    place = Place()
    turn_x, turn_g = Turn(place, tokens_ref, x0, *sems[0:3]), Turn(place, cotangent_ref, g_out, *sems[3:6])
    load, saves, misc = sems[6:9]
    gather = Gather(place, own_ref, full, small_ref, small, sems[9:])
    units = [number(*pair) for pair in ORDER]

    own_copies = [
        pltpu.make_async_copy(own_ref.at[:, place.mine],
                              full.at[:, place.at["y"], place.at["z"], place.at["x"], place.mine], misc.at[0]),
        pltpu.make_async_copy(small_ref, small.at[:, place.at["y"], place.at["z"], place.at["x"]], misc.at[1]),
    ]
    for copy in own_copies:
        copy.start()
    place.greet(NEAR + (("x", 2),))
    gather.begin()
    turn_x.start()
    for copy in own_copies:
        copy.wait()
    gather.small_phase(1, "first")
    for unit in units[:2]:
        gather.first_two(unit)
    for unit in units[:2]:
        gather.second_two(unit)
    gather.small_phase(1, "second")
    for unit in units[:2]:
        gather.third_two(unit)
        gather.first_three(unit)
    for unit in units[2:]:
        gather.first_two(unit)
    gather.small_phase(1, "third")
    gather.small_phase(2, "first")
    gather.second_three(units[0])
    for unit in units[2:]:
        gather.second_two(unit)
    gather.small_phase(2, "second")
    gather.second_three(units[1])
    turn_x.end()
    resid[...] = as_rows(x0)
    gather.third_three(units[0])
    for unit in units[2:]:
        gather.third_two(unit)
    for unit in units[2:4]:
        gather.first_three(unit)
    gather.small_phase(2, "third")
    gather.ready(units[0])
    kept = []

    def keep(src, dst, k):
        copy = pltpu.make_async_copy(src, dst, misc.at[k])
        copy.start()
        kept.append((src, dst, k))

    keep(x0, x0_out, 2)
    keep(small, small_out, 3)
    turn_g.start()

    for k, (kind, layer) in enumerate(ORDER):
        unit = units[k]
        hooks = {3: []}
        if k + 1 < 6:
            hooks[3] += [functools.partial(gather.third_three, units[k + 1])]
            if k + 2 < 6:
                hooks[3] += [functools.partial(gather.second_three, units[k + 2])]
            if k + 4 < 6:
                hooks[3] += [functools.partial(gather.first_three, units[k + 4])]
            hooks[3] += [functools.partial(gather.ready, units[k + 1])]

        def save(which, src, dst, step):
            return pltpu.make_async_copy(src, dst, saves.at[which, k, step])

        if kind == 0:
            low = lows.at[layer, 0]
            low[...] = norm_low(resid[...], small, layer, 0)
            keep(low, low_out.at[layer, 0], 8 + 2 * layer)
            acc[...] = resid[...] + feature_row(small, layer, 4)

            def body(step, slot):
                weights = slots.at[slot]
                mixed = dot_nt(low[...], tall(weights, 0, QKV)) + here_row(small, step, layer, 7, 0, QKV)
                mixed = mixed.astype(BF16)
                mixed_all[layer, step] = mixed
                attended = []
                for j in range(BLOCKS):
                    queries, keys, values = head_parts(mixed, j)
                    probs = softmax(queries, keys).astype(BF16)
                    probs_all[layer, step, j] = probs
                    attended.append(dot_nn(probs, values).astype(BF16))
                attended = jnp.concatenate(attended, axis=1)
                att_all[layer, step] = attended
                acc[...] += dot_nn(attended, tall(weights, QKV, HEAD))
                for copy in copies(step):
                    copy.start()

            def copies(step):
                pairs = ((mixed_all, mixed_out), (att_all, att_out), (probs_all, probs_out))
                return [save(i, src.at[layer, step], dst.at[layer, step], step) for i, (src, dst) in enumerate(pairs)]
        else:
            half = kind - 1
            if half == 0:
                mids[layer] = acc[...]
                resid[...] = acc[...]
                low = lows.at[layer, 1]
                low[...] = norm_low(resid[...], small, layer, 1)
                keep(low, low_out.at[layer, 1], 9 + 2 * layer)
                acc[...] = resid[...] + feature_row(small, layer, 5)
                keep(mids.at[layer], mid_out.at[layer], 4 + layer)

            def body(step, slot):
                weights = slots.at[slot]
                upward = dot_nt(low[...], tall(weights, 0, FF_HALF)) + here_row(small, step, layer, 6, half * FF_HALF, FF_HALF)
                below = 0.5 + 0.5 * lax.erf(upward * 2**-0.5)
                activated = (upward * below).astype(BF16)
                act_all[layer, half, step] = activated
                slope = below + upward * (jnp.exp(-0.5 * upward * upward) * (2 * jnp.pi) ** -0.5)
                slope_all[layer, half, step] = slope.astype(BF16)
                acc[...] += dot_nn(activated, tall(weights, FF_HALF, FF_HALF))
                for copy in copies(step):
                    copy.start()

            def copies(step):
                pairs = ((act_all, act_out), (slope_all, slope_out))
                return [save(i, src.at[layer, half, step], dst.at[layer, half, step], step) for i, (src, dst) in enumerate(pairs)]

        Stream([(lambda step: full.at[unit, step], slots)], load.at[k]).run(body, hooks)
        for step in range(STEPS):
            for copy in copies(step):
                copy.wait()
        if kind == 2 and layer == 0:
            resid[...] = acc[...]
            keep(resid, x1_out, 6)
            pltpu.make_async_copy(resid, x1_out, misc.at[6]).wait()
            kept.pop()
    put_rows(ends, acc[...])
    keep(ends, end_out, 7)
    turn_g.end()
    gather.finish()
    for src, dst, k in kept:
        pltpu.make_async_copy(src, dst, misc.at[k]).wait()


def forward(own, small, tokens, cotangent):
    both = jax.ShapeDtypeStruct((2, ROWS, WIDTH), F32)
    return pl.pallas_call(
        forward_kernel,
        out_shape=[WEIGHTS, SMALLS, TURNED, TURNED, both, TOKENS, TURNED, LOWS, *SAVED],
        in_specs=[VMEM] * 4,
        out_specs=[ANY] * 13,
        scratch_shapes=[
            scratch_like(SMALLS), scratch_like(TURNED), scratch_like(TOKENS), scratch_like(LOWS),
            scratch_like(TOKENS), scratch_like(both), scratch_like(TURNED), pltpu.VMEM((2, RING, RING, UNIT, 256), BF16),
            *[scratch_like(s) for s in SAVED],
            *TURN_SEMAPHORES, *TURN_SEMAPHORES, DMA((6, 2, 1)), DMA((3, 6, STEPS)), DMA((12,)),
            *gather_semaphores(),
        ],
        compiler_params=pltpu.CompilerParams(vmem_limit_bytes=VMEM_LIMIT, collective_id=0, has_side_effects=True),
        name="forward",
    )(own, small, tokens, cotangent)


BACK = [(2, 1), (1, 1), (0, 1), (2, 0), (1, 0), (0, 0)]


def backward_kernel(full, small_in, x0_in, g_in, mid_in, x1_in, end_ref, lows_in, mixed_in, att_in, probs_in, act_in, slope_in,
                    encoded_out, tokens_out, grads_out, sums_out,
                    grad, low, acc, turned, small, lows, xbuf, sums, columns_all, slots, mixed_two, att_two, probs_two, act_two, slope_two, stage, outs,
                    *rest):
    first, pair = [rest[0:2], rest[2:4], rest[4:6]], [rest[6:8], rest[8:10]]
    later = [rest[10:16], rest[16:22]]
    total_scratch, sems = rest[22:28], rest[28:]
    place = Place()
    turn_out, turn_g = Turn(place, end_ref, encoded_out, *sems[0:3]), Turn(place, turned, tokens_out, *sems[3:6])
    load, free, misc = sems[6:9]
    unit_sems = [[group.at[k] for group in sems[9:]] for k in range(6)]
    scatters = []
    for k, (kind, layer) in enumerate(BACK):
        scatters.append(
            Scatter(place, kind, layer, stage, [*first[k % 3], *pair[k % 2]], later[k % 2][0:3], later[k % 2][3:6], outs.at[k],
                    grads_out.at[number(kind, layer)], unit_sems[k])
        )
    total = Total(place, sums, total_scratch[0], sums_out, *total_scratch[1:])
    norms = [(1, 1), (1, 0), (0, 1), (0, 0)]

    def fetch_low(phase):
        return pltpu.make_async_copy(lows_in.at[norms[phase][0], norms[phase][1]], lows.at[phase % 2], misc.at[phase])

    def fetch_x(phase):
        source = (mid_in.at[1], x1_in, mid_in.at[0], x0_in)[phase]
        return pltpu.make_async_copy(source, turned if phase == 3 else xbuf, misc.at[4 + phase])

    starts = [pltpu.make_async_copy(g_in, turned, misc.at[8]),
              pltpu.make_async_copy(small_in.at[:, pl.ds(0, 1), pl.ds(0, 1)], small, misc.at[9]),
              fetch_low(0)]
    for copy in starts:
        copy.start()
    place.greet(TOTAL_PEERS)
    turn_out.start()
    for copy in starts:
        copy.wait()
    grad[...] = as_rows(turned)
    sums[...] = jnp.zeros_like(sums)
    columns_all[...] = jnp.zeros_like(columns_all)

    def leave(k):
        place.tell(free.at[k], NEAR)

    def may(k):
        pl.semaphore_wait(free.at[k], len(NEAR))

    for k, (kind, layer) in enumerate(BACK):
        it = scatters[k]
        hooks = {0: [], 1: [], 2: [], 3: []}
        if k >= 1:
            hooks[0] += [scatters[k - 1].open]
            hooks[2] += [scatters[k - 1].sides_one]
        if k >= 2:
            hooks[1] += [scatters[k - 2].centre_one, scatters[k - 2].start_two]
            hooks[2] += [scatters[k - 2].sides_two]
            hooks[3] += [scatters[k - 2].centre_two]
        if k >= 3:
            hooks[0] += [scatters[k - 3].sides_three]
            hooks[1] += [scatters[k - 3].centre_three]
        if k >= 2:
            hooks[1] += [functools.partial(leave, k + 1)]
        base = LAYER_SUMS * layer

        def begin(step):
            @pl.when(step >= 2)
            def _():
                it.free(step - 2)

            if k >= 1:
                @pl.when(step == 0)
                def _():
                    scatters[k - 1].free_last()
                    if k >= 3:
                        may(k)

        if kind == 0:
            phase = 3 - 2 * layer
            here = lows.at[phase % 2]
            fetch_low(phase).wait()
            if phase < 3:
                fetch_low(phase + 1).start()
            fetch_x(phase).start()
            low[...] = grad[...].astype(BF16)
            acc[...] = jnp.zeros_like(acc)

            def body(step, slot):
                weights = slots.at[slot]
                begin(step)
                g = low[...]
                mixed = mixed_two[slot]
                store_blocks(stage, slot, QKV, dot_tn(att_two[slot], g))
                g_all = dot_nt(g, tall(weights, QKV, HEAD)).astype(BF16)
                g_mixed = []
                for j in range(BLOCKS):
                    queries, keys, values = head_parts(mixed, j)
                    g_att = g_all[:, j * HEAD : (j + 1) * HEAD]
                    probs_low = probs_two[slot, j]
                    probs = probs_low.astype(F32)
                    g_probs = dot_nt(g_att, values)
                    g_values = dot_tn(probs_low, g_att)
                    centre = jnp.sum(probs * g_probs, axis=1, keepdims=True)
                    g_scores = (probs * (g_probs - centre) * HEAD**-0.5).astype(BF16)
                    g_mixed += [dot_nn(g_scores, keys), dot_tn(g_scores, queries), g_values]
                g_mixed = jnp.concatenate([part.astype(BF16) for part in g_mixed], axis=1)
                store_blocks(stage, slot, 0, dot_tn(g_mixed, here[...]))
                it.hand_over(step)
                columns_all[layer, 1, step, :, : BLOCKS * QKV] = jnp.sum(g_mixed.astype(F32), axis=0, keepdims=True)
                acc[...] += dot_nn(g_mixed, tall(weights, 0, QKV))

            pairs = [
                (lambda step: full.at[number(kind, layer), step], slots),
                (lambda step: mixed_in.at[layer, step], mixed_two),
                (lambda step: att_in.at[layer, step], att_two),
                (lambda step: probs_in.at[layer, step], probs_two),
            ]
        else:
            half = kind - 1
            phase = 2 - 2 * layer
            here = lows.at[phase % 2]
            if half == 1:
                if phase > 0:
                    fetch_low(phase).wait()
                fetch_low(phase + 1).start()
                fetch_x(phase).start()
                low[...] = grad[...].astype(BF16)
                acc[...] = jnp.zeros_like(acc)

            def body(step, slot):
                weights = slots.at[slot]
                begin(step)
                g = low[...]
                store_blocks(stage, slot, FF_HALF, dot_tn(act_two[slot], g))
                g_up = (dot_nt(g, tall(weights, FF_HALF, FF_HALF)) * slope_two[slot].astype(F32)).astype(BF16)
                store_blocks(stage, slot, 0, dot_tn(g_up, here[...]))
                it.hand_over(step)
                columns = jnp.sum(g_up.astype(F32), axis=0, keepdims=True)
                for j in range(BLOCKS):
                    at = j * 2 * FF_HALF + half * FF_HALF
                    columns_all[layer, 0, step, :, at : at + FF_HALF] = columns[:, j * FF_HALF : (j + 1) * FF_HALF]
                acc[...] += dot_nn(g_up, tall(weights, 0, FF_HALF))

            pairs = [
                (lambda step: full.at[number(kind, layer), step], slots),
                (lambda step: act_in.at[layer, half, step], act_two),
                (lambda step: slope_in.at[layer, half, step], slope_two),
            ]
        Stream(pairs, load.at[k]).run(body, hooks)
        if kind < 2:
            j = kind
            fetch_x(phase).wait()
            x = as_rows(turned) if phase == 3 else xbuf[...]
            part, gain, shift = norm_back(acc[...], x, feature_row(small, layer, j))
            at = base + (8 if kind == 1 else 11)
            sums[at : at + 1, :] = jnp.sum(low[...].astype(F32), axis=0, keepdims=True)
            sums[at + 1 : at + 2, :] = gain
            sums[at + 2 : at + 3, :] = shift
            grad[...] = grad[...] + part
        if k == 5:
            put_rows(turned, grad[...])
            turn_g.start()
            for i in range(2):
                for which in range(2):
                    for step in range(STEPS):
                        at = LAYER_SUMS * i + STEPS * which + step
                        sums[at : at + 1, :] = columns_all[i, which, step]
            total.start()
    early, late = scatters[4], scatters[5]
    late.free_last()
    may(6)
    late.open()
    scatters[3].sides_three()
    total.core_sum()
    early.centre_one()
    early.start_two()
    scatters[3].centre_three()
    leave(7)
    late.sides_one()
    total.put(1, total.take(0))
    early.sides_two()
    early.centre_two()
    for it in scatters[:4]:
        it.shown()
    total.put(2, total.take(1))
    early.sides_three()
    late.centre_one()
    may(7)
    late.start_two()
    early.centre_three()
    total.last()
    late.sides_two()
    late.centre_two()
    turn_out.end()
    turn_g.end()
    late.sides_three()
    early.shown()
    total.finish()
    late.centre_three()
    late.shown()
    for it in scatters:
        it.keep().wait()


def backward(full, small, x0, g, mids, x1, ends, lows, saved):
    saved_two = [pltpu.VMEM((2,) + s.shape[-3 if len(s.shape) == 5 and s.shape[1] == STEPS else -2 :], s.dtype) for s in SAVED]
    semaphores = [pltpu.SemaphoreType.DMA((6,) + (s.shape if hasattr(s, "shape") else ())) for s in scatter_semaphores()]
    return pl.pallas_call(
        backward_kernel,
        out_shape=[TURNED, TURNED, jax.ShapeDtypeStruct((6, UNIT, 256), F32), jax.ShapeDtypeStruct((SUM_ROWS, WIDTH), F32)],
        in_specs=[ANY] * 13,
        out_specs=[ANY] * 4,
        scratch_shapes=[
            scratch_like(TOKENS), pltpu.VMEM((ROWS, WIDTH), BF16), scratch_like(TOKENS),
            scratch_like(TURNED), pltpu.VMEM((1, 1, 1, RING, SMALL, 256), F32), pltpu.VMEM((2, ROWS, WIDTH), BF16), scratch_like(TOKENS),
            pltpu.VMEM((SUM_ROWS, WIDTH), F32), pltpu.VMEM((2, 2, STEPS, 1, WIDTH), F32),
            pltpu.VMEM((2, RING, RING, UNIT, 256), BF16),
            *saved_two,
            pltpu.VMEM((2, RING, RING, UNIT, 256), BF16), pltpu.VMEM((6, UNIT, 256), F32),
            *first_buffers(), *first_buffers(), *first_buffers(), *pair_buffers(), *pair_buffers(), *later_buffers(), *later_buffers(),
            *total_buffers(SUM_ROWS),
            *TURN_SEMAPHORES, *TURN_SEMAPHORES, DMA((6, 2, 4)), pltpu.SemaphoreType.REGULAR((8,)), DMA((10,)),
            *semaphores,
        ],
        compiler_params=pltpu.CompilerParams(vmem_limit_bytes=VMEM_LIMIT, collective_id=1, has_side_effects=True),
        name="backward",
    )(full, small, x0, g, mids, x1, ends, lows, *saved)


def to_images(rows):
    return jnp.pad(rows.reshape(3, SEQ, 256), ((0, 1), (0, ROWS - SEQ), (0, 0)))


def from_images(turned):
    return turned[:3, :SEQ].reshape(3 * SEQ, 256).astype(F32)


def shards(tokens, norm_gain, norm_shift, qkv_weight, qv_bias, proj_weight, proj_bias, up_weight, up_bias, down_weight, down_bias, cotangent):
    layers = qkv_weight.shape[0]
    attention = jnp.concatenate([qkv_weight.transpose(0, 2, 1), proj_weight], axis=1)
    up = up_weight.transpose(0, 2, 1)
    halves = [jnp.concatenate([part[:, at : at + FF_HALF] for part in (up, down_weight)], axis=1) for at in (0, FF_HALF)]
    own = jnp.concatenate([attention, *halves], axis=0)
    zeros = jnp.zeros((layers, HEAD), F32)
    qkv_row = jnp.concatenate([qv_bias[:, :HEAD], zeros, qv_bias[:, HEAD:], zeros], axis=1)
    small = jnp.stack([norm_gain[:, 0], norm_gain[:, 1], norm_shift[:, 0], norm_shift[:, 1], proj_bias, down_bias, up_bias, qkv_row], axis=1)
    full, small, x0, g, mids, x1, ends, lows, *saved = forward(
        own, small.reshape(1, SMALL, 256), to_images(tokens), to_images(cotangent.astype(BF16))
    )
    encoded, grad_tokens, grads, sums = backward(full, small, x0, g, mids, x1, ends, lows, saved)
    row, col = lax.axis_index("row"), lax.axis_index("col")
    sums = sums[: layers * LAYER_SUMS].reshape(layers, LAYER_SUMS, WIDTH)
    up_sums = lax.dynamic_slice_in_dim(sums[:, 0:4].reshape(layers, 16, 256), col, 1, 1)[:, 0]
    qkv_sums = sums[:, 4:8, : BLOCKS * QKV].reshape(layers, 16, QKV)
    qkv_sums = lax.dynamic_slice_in_dim(qkv_sums, col, 1, 1)[:, 0]
    features = lax.dynamic_slice_in_dim(sums[:, 8:].reshape(layers, 6, RING, 256), row, 1, 2)[:, :, 0]
    attention, first, second = grads[0:2], grads[2:4], grads[4:6]
    return (
        from_images(encoded),
        from_images(grad_tokens),
        jnp.stack([features[:, 4], features[:, 1]], axis=1),
        jnp.stack([features[:, 5], features[:, 2]], axis=1),
        attention[:, :QKV].transpose(0, 2, 1),
        jnp.concatenate([qkv_sums[:, :HEAD], qkv_sums[:, 2 * HEAD : QKV]], axis=1),
        attention[:, QKV:],
        features[:, 3],
        jnp.concatenate([first[:, :FF_HALF], second[:, :FF_HALF]], axis=1).transpose(0, 2, 1),
        up_sums,
        jnp.concatenate([first[:, FF_HALF:], second[:, FF_HALF:]], axis=1),
        features[:, 0],
    )


def solution(mesh):
    in_specs = (
        P(("dp", "col"), "row"),
        P(None, None, "row"),
        P(None, None, "row"),
        P(None, "row", "col"),
        P(None, "col"),
        P(None, "col", "row"),
        P(None, "row"),
        P(None, "row", "col"),
        P(None, "col"),
        P(None, "col", "row"),
        P(None, "row"),
        P(("dp", "col"), "row"),
    )
    out_specs = (
        P(("dp", "col"), "row"),
        P(("dp", "col"), "row"),
        P(None, None, "row"),
        P(None, None, "row"),
        P(None, "row", "col"),
        P(None, "col"),
        P(None, "col", "row"),
        P(None, "row"),
        P(None, "row", "col"),
        P(None, "col"),
        P(None, "col", "row"),
        P(None, "row"),
    )
    return jax.shard_map(shards, mesh=mesh, in_specs=in_specs, out_specs=out_specs, check_vma=False)
```

```python
import functools

import jax
import jax.numpy as jnp
from jax import lax
from jax.experimental import pallas as pl
from jax.experimental.pallas import tpu as pltpu
from jax.sharding import PartitionSpec as P

MESH = pl.DeviceIdType.MESH
RING = 4
STEPS = 4
AXES = "yzx"
ORDERS = (("x", "y", "z"), ("y", "z", "x"), ("z", "x", "y"))
KINDS = 3
UNIT = 256
CORE = 128
CUTS = (((0, 48), (48, 48), (96, 32)), ((0, 48), (48, 32), (80, 48)), ((0, 32), (32, 48), (80, 48)))
NEAR = tuple((axis, by) for axis in "xyz" for by in (1, -1)) + (("core", 1),)
ROW_PEERS = (("x", 1), ("x", 2), ("x", -1))
VMEM_LIMIT = 60 * 2**20
DMA = pltpu.SemaphoreType.DMA
ANY = pl.BlockSpec(memory_space=pl.ANY)
VMEM = pl.BlockSpec(memory_space=pltpu.VMEM)
BF16 = jnp.bfloat16
F32 = jnp.float32


def number(kind, layer):
    return 2 * kind + layer


class Place:
    def __init__(self):
        self.core = lax.axis_index("dp")
        block = lax.axis_index("col")
        self.at = {"x": lax.axis_index("row"), "y": block // RING, "z": block % RING}
        self.mine = pl.ds(pl.multiple_of(self.core * CORE, CORE), CORE)
        self.other = pl.ds(pl.multiple_of((1 - self.core) * CORE, CORE), CORE)

    def shifted(self, axis, by):
        moved = dict(self.at)
        moved[axis] = (self.at[axis] + by + RING) % RING
        return moved

    def neighbour(self, axis, by):
        if axis == "core":
            return (1 - self.core, self.at["x"], self.at["y"] * RING + self.at["z"])
        at = self.shifted(axis, by)
        return (self.core, at["x"], at["y"] * RING + at["z"])

    def sibling(self):
        return self.neighbour("core", 1)

    def tell(self, semaphore, peers):
        for axis, by in peers:
            pl.semaphore_signal(semaphore, inc=1, device_id=self.neighbour(axis, by), device_id_type=MESH)

    def greet(self, peers):
        barrier = pltpu.get_barrier_semaphore()
        self.tell(barrier, peers)
        pl.semaphore_wait(barrier, len(peers))


def region(ref, axes, at, whole, start, count):
    index = tuple(pl.ds(0, RING) if a in whole else at[a] for a in axes)
    return ref.at[index + (pl.ds(start, count),)]


def remote(src, dst, send, recv, device):
    return pltpu.make_async_remote_copy(
        src_ref=src, dst_ref=dst, send_sem=send, recv_sem=recv, device_id=device, device_id_type=MESH
    )


class Ring:
    def __init__(self, place, full, units, order, phase, start, count, half, sems, own=None):
        self.place, self.full, self.units, self.own = place, full, units, own
        self.axis, self.whole = order[phase], order[:phase]
        self.start, self.count = start, count
        self.halves = ((start, half), (start + half, count - half))
        self.whole_send, self.half_send, self.whole_recv, self.half_recv = sems

    def piece(self, by, start, count):
        at = self.place.shifted(self.axis, by)
        index = tuple(pl.ds(0, RING) if a in self.whole else at[a] for a in AXES)
        return self.full.at[(self.units,) + index + (pl.ds(start, count),)]

    def to(self, i):
        return self.place.neighbour(self.axis, (1, -1)[i])

    def whole_copy(self, i):
        here = self.piece(0, self.start, self.count)
        return remote(here if self.own is None else self.own, here, self.whole_send[i], self.whole_recv[i], self.to(i))

    def half_copy(self, i):
        ref = self.piece((-1, 1)[i], *self.halves[i])
        return remote(ref, ref, self.half_send[i], self.half_recv[i], self.to(i))

    def share(self, send, recv, *which):
        for by in which:
            if by is None:
                index = tuple(pl.ds(0, RING) if a in self.whole + (self.axis,) else self.place.at[a] for a in AXES)
                ref = self.full.at[(self.units,) + index + (pl.ds(self.start, self.count),)]
            else:
                ref = self.piece(by, self.start, self.count)
            remote(ref, ref, send, recv, self.place.sibling()).start()

    def first(self):
        for i in range(2):
            self.whole_copy(i).start()

    def second(self):
        for i in range(2):
            self.half_copy(i).start()


class Gather:
    def __init__(self, place, own, full, small_own, small_full, sems):
        self.place, self.full = place, full
        self.send, self.whole, self.half, self.share_send, self.share_recv, small_send, small_recv = sems
        self.one, self.two, self.three = [], {}, {}
        base = pl.multiple_of(place.core * CORE, CORE)

        def shared(k):
            return tuple([group.at[k]] * 2 for group in (self.send, self.send, self.whole, self.half))

        for kind in range(KINDS):
            for p, (start, count) in enumerate(CUTS[kind]):
                rows = base + start
                self.one.append(
                    Ring(place, full, pl.ds(2 * kind, 2), ORDERS[p], 0, rows, count, 16, shared(0),
                         own.at[pl.ds(2 * kind, 2), pl.ds(rows, count)])
                )
            for layer in range(2):
                u = number(kind, layer)
                for phase, into in ((1, self.two), (2, self.three)):
                    into[u] = [
                        Ring(place, full, u, ORDERS[p], phase, base + start, count,
                             count // 2 if count == 32 else (16, 32)[(p + layer) % 2], shared(self.place_of(u, phase)))
                        for p, (start, count) in enumerate(CUTS[kind])
                    ]
        rows = small_own.shape[1]
        self.small = [
            Ring(place, small_full, pl.ds(0, 1), ORDERS[0], phase, 0, rows, rows // 2,
                 [[group.at[phase, k + i] for i in range(2)] for group, k in
                  ((small_send, 0), (small_send, 2), (small_recv, 0), (small_recv, 2))],
                 small_own if phase == 0 else None)
            for phase in range(3)
        ]

    @staticmethod
    def place_of(u, phase):
        return 0 if phase == 0 else 1 + u + 6 * (phase - 1)

    def amount(self, u, phase, times):
        if phase == 0:
            return self.full.at[:, 0, 0, pl.ds(0, times), self.place.mine]
        if phase == 1:
            return self.full.at[u, pl.ds(0, times), :, 0, self.place.mine]
        return self.full.at[u, pl.ds(0, times), :, :, self.place.mine]

    def came(self, u, phase, sems, times):
        ref = self.amount(u, phase, times)
        at = self.place_of(u, phase)
        remote(ref, ref, self.send.at[at], sems.at[at], self.place.sibling()).wait_recv()

    def sent(self, u, phase):
        ref = self.amount(u, phase, 3)
        at = self.place_of(u, phase)
        remote(ref, ref, self.send.at[at], self.whole.at[at], self.place.sibling()).wait_send()

    def rings(self, u, phase):
        return self.one if phase == 0 else (self.two if phase == 1 else self.three)[u]

    def first(self, u, phase):
        for ring in self.rings(u, phase):
            ring.first()

    def second(self, u, phase):
        self.came(u, phase, self.whole, 2)
        for ring in self.rings(u, phase):
            ring.second()

    def third(self, u, phase):
        self.came(u, phase, self.half, 1)

    def begin(self):
        self.first(0, 0)
        self.small_phase(0, "first")
        self.second(0, 0)
        self.small_phase(0, "second")
        self.third(0, 0)
        self.small_phase(0, "third")

    def small_phase(self, phase, name):
        ring = self.small[phase]
        if name == "first":
            ring.first()
            return
        for i in range(2):
            if name == "second":
                ring.whole_copy(i).wait_recv()
                ring.half_copy(i).start()
            else:
                ring.half_copy(i).wait_recv()

    def first_two(self, u):
        self.first(u, 1)

    def second_two(self, u):
        self.second(u, 1)

    def third_two(self, u):
        self.third(u, 1)

    def share(self, u, phase, *which):
        for ring in self.rings(u, phase):
            ring.share(self.share_send.at[u], self.share_recv.at[u], *which)

    def first_three(self, u):
        self.first(u, 2)
        self.share(u, 1, None)

    def second_three(self, u):
        self.second(u, 2)
        self.share(u, 2, -1, 1)

    def third_three(self, u):
        self.third(u, 2)
        self.share(u, 2, 2)

    def ready(self, u):
        ref = self.full.at[u, :, :, :, self.place.mine]
        remote(ref, ref, self.share_send.at[u], self.share_recv.at[u], self.place.sibling()).wait()

    def finish(self):
        self.sent(0, 0)
        for u in range(6):
            self.sent(u, 1)
            self.sent(u, 2)
        for ring in self.small:
            for i in range(2):
                ring.whole_copy(i).wait_send()
                ring.half_copy(i).wait_send()


def gather_semaphores():
    return [DMA((13,)), DMA((13,)), DMA((13,)), DMA((6,)), DMA((6,)), DMA((3, 4)), DMA((3, 4))]


def blockwise(shape, body):
    if len(shape) < 4:
        body(())
        return

    def step(i, _):
        body((i,))
        return 0

    lax.fori_loop(0, shape[0], step, 0)


def add_to(dst, first, *others):
    def body(index):
        if len(others) == 1 and dst.dtype == BF16:
            dst[index] = first[index] + others[0][index]
            return
        total = first[index].astype(F32)
        for other in others:
            total = total + other[index].astype(F32)
        dst[index] = total.astype(dst.dtype)

    blockwise(dst.shape, body)


class Fold:
    def __init__(self, place, order, phase, work, half_in, full_in, dst, start, count, half, sems):
        self.place, self.work, self.half_in, self.full_in, self.dst = place, work, half_in, full_in, dst
        self.axis, self.whole = order[2 - phase], order[: 2 - phase]
        self.axes = tuple(a for a in AXES if a not in order[3 - phase :])
        self.start, self.count = start, count
        self.halves = ((start, half), (start + half, count - half))
        self.send, self.half_recv, self.whole_recv = sems
        self.lead = (slice(None),) * (2 - phase)

    def piece(self, by, start, count, ref=None):
        ref = self.work if ref is None else ref
        return region(ref, self.axes, self.place.shifted(self.axis, by), self.whole, start, count)

    def came(self, start, count):
        return self.half_in.at[self.lead + (pl.ds(start, count),)]

    def arrived(self, i):
        return self.full_in.at[(i,) + self.lead + (pl.ds(self.start, self.count),)]

    def opposite(self):
        for i in range(2):
            src, dst = self.piece(2, *self.halves[i]), self.came(*self.halves[i])
            remote(src, dst, self.send, self.half_recv, self.place.neighbour(self.axis, (1, -1)[i])).start()

    def side(self, i):
        by = (1, -1)[i]
        src = self.piece(by, self.start, self.count)
        remote(src, self.arrived(i), self.send, self.whole_recv, self.place.neighbour(self.axis, by)).start()

    def sides(self):
        for i in range(2):
            ref = self.piece((1, -1)[i], *self.halves[i])
            add_to(ref, ref, self.came(*self.halves[i]))
            self.side(i)

    def centre(self):
        add_to(self.dst, self.piece(0, self.start, self.count), self.arrived(0), self.arrived(1))

    def direct(self):
        for i in range(2):
            self.side(i)
        src = self.piece(2, self.start, self.count)
        remote(src, self.came(self.start, self.count), self.send, self.half_recv, self.place.neighbour(self.axis, 2)).start()

    def direct_centre(self):
        add_to(self.dst, self.piece(0, self.start, self.count), self.arrived(0), self.arrived(1),
               self.came(self.start, self.count))


class Scatter:
    def __init__(self, place, kind, layer, stage, first, second, third, out, result, sems):
        self.place, self.stage = place, stage
        self.work, self.twin, reduced, inner = first[0], first[1], second[0], third[0]
        self.out, self.result = out, result
        (self.near, self.far_send, self.far_recv, self.send, self.half, self.whole, self.show_send, self.show_recv,
         self.local) = sems
        base = pl.multiple_of(place.core * CORE, CORE)
        self.works = (self.work, reduced, inner)
        self.half_in = (first[2], second[1], third[1])
        self.full_in = (first[3], second[2], third[2])
        targets = (
            lambda start, count: reduced.at[:, :, pl.ds(start, count)],
            lambda start, count: inner.at[:, pl.ds(start, count)],
            lambda start, count: out.at[pl.ds(base + start, count)],
        )
        self.parts = [
            [
                Fold(place, ORDERS[p], phase, self.works[phase], self.half_in[phase], self.full_in[phase],
                     targets[phase](start, count), start, count,
                     count // 2 if count == 32 else (16, 32)[(p + layer) % 2],
                     (self.send.at[phase], self.half.at[phase], self.whole.at[phase]))
                for p, (start, count) in enumerate(CUTS[kind])
            ]
            for phase in range(3)
        ]

    def stay(self, step):
        slot = step % 2
        return pltpu.make_async_copy(self.stage.at[slot, :, :, self.place.mine], self.work.at[step], self.near.at[slot])

    def go(self, step):
        slot = step % 2
        return remote(self.stage.at[slot, :, :, self.place.other], self.twin.at[step], self.far_send.at[slot],
                      self.far_recv, self.place.sibling())

    def free(self, step):
        self.stay(step).wait()
        self.go(step).wait_send()

    def hand_over(self, step):
        self.stay(step).start()
        self.go(step).start()

    def free_last(self):
        for step in (STEPS - 2, STEPS - 1):
            self.free(step)

    def join(self, *which):
        for by in which:
            for part in self.parts[0]:
                ref = part.piece(by, part.start, part.count)
                add_to(ref, ref, part.piece(by, part.start, part.count, self.twin))

    def each(self, name, phase):
        for part in self.parts[phase]:
            getattr(part, name)()

    def came(self, refs, sems, phase):
        remote(refs[phase], refs[phase], self.send.at[phase], sems.at[phase], self.place.sibling()).wait_recv()

    def sent(self, phase):
        ref = self.works[phase].at[pl.ds(0, 3)]
        remote(ref, ref, self.send.at[phase], self.half.at[phase], self.place.sibling()).wait_send()

    def show(self):
        ref = self.out.at[self.place.mine]
        return remote(ref, ref, self.show_send, self.show_recv, self.place.sibling())

    def keep(self):
        return pltpu.make_async_copy(self.out, self.result, self.local)

    def sides(self, phase):
        self.came(self.half_in, self.half, phase)
        self.each("sides", phase)

    def centre(self, phase):
        self.came(self.full_in, self.whole, phase)
        self.each("centre", phase)

    def direct_centre(self, phase):
        self.came(self.full_in, self.whole, phase)
        self.came(self.half_in, self.half, phase)
        self.each("direct_centre", phase)

    def open(self):
        remote(self.twin, self.twin, self.far_send.at[0], self.far_recv, self.place.sibling()).wait_recv()
        self.join(2)
        self.each("opposite", 0)
        self.join(1, -1)

    def sides_one(self):
        self.sides(0)
        self.join(0)

    def centre_one(self):
        self.centre(0)
        self.sent(0)

    def start_two(self):
        self.each("opposite", 1)

    def sides_two(self):
        self.sides(1)

    def centre_two(self):
        self.centre(1)
        self.each("opposite", 2)

    def sides_three(self):
        self.sides(2)

    def centre_three(self):
        self.centre(2)
        self.show().start()
        self.sent(1)
        self.sent(2)

    def shown(self):
        self.show().wait()
        self.keep().start()


def first_buffers():
    blocks = (RING,) * 3 + (CORE, 256)
    return [pltpu.VMEM(blocks, BF16), pltpu.VMEM(blocks, BF16)]


def pair_buffers():
    blocks = (RING,) * 2 + (CORE, 256)
    return [pltpu.VMEM(blocks, BF16), pltpu.VMEM((2,) + blocks, BF16)]


def later_buffers():
    def some(*lead):
        return pltpu.VMEM(lead + (CORE, 256), BF16)

    return [some(RING, RING), some(RING), some(2, RING), some(RING), some(), some(2)]


def scatter_semaphores():
    return [DMA((2,)), DMA((2,)), DMA, DMA((3,)), DMA((3,)), DMA((3,)), DMA, DMA, DMA]


class Turn:
    def __init__(self, place, src, dst, send, recv, local):
        self.place, self.src, self.dst, self.send, self.recv, self.local = place, src, dst, send, recv, local

    def copies(self):
        row = self.place.at["x"]
        return [
            remote(self.src.at[self.place.shifted("x", by)["x"]], self.dst.at[row], self.send.at[k], self.recv.at[k],
                   self.place.neighbour("x", by))
            for k, (_, by) in enumerate(ROW_PEERS)
        ]

    def own(self):
        row = self.place.at["x"]
        return pltpu.make_async_copy(self.src.at[row], self.dst.at[row], self.local)

    def start(self):
        self.own().start()
        for copy in self.copies():
            copy.start()

    def end(self):
        self.own().wait()
        for copy in self.copies():
            copy.wait()


TURN_SEMAPHORES = [DMA((3,)), DMA((3,)), DMA]


class Total:
    def __init__(self, place, mine, out, result, slots, core_in, send, recv, core_sems):
        self.place, self.mine, self.out, self.result, self.slots = place, mine, out, result, slots
        self.send, self.recv, self.core_in, self.core_sems = send, recv, core_in, core_sems
        rows = mine.shape[0] // 2
        self.half = pl.ds(pl.multiple_of(place.core * rows, rows), rows)
        self.away = pl.ds(pl.multiple_of((1 - place.core) * rows, rows), rows)

    def core_copy(self):
        return remote(self.mine.at[self.away], self.core_in, self.core_sems.at[0], self.core_sems.at[1], self.place.sibling())

    def copies(self, k):
        axis = "xyz"[k]
        slot = self.slots.at[k, self.place.at[axis]]
        return [
            remote(slot, slot, self.send.at[k, j], self.recv.at[k, j], self.place.neighbour(axis, by))
            for j, by in enumerate((1, 2, -1))
        ]

    def start(self):
        self.core_copy().start()

    def core_sum(self):
        self.core_copy().wait_recv()
        self.put(0, self.mine[self.half] + self.core_in[...])

    def put(self, k, value):
        self.slots[k, self.place.at["xyz"[k]]] = value
        for copy in self.copies(k):
            copy.start()

    def take(self, k):
        for copy in self.copies(k):
            copy.wait_recv()
        return (self.slots[k, 0] + self.slots[k, 1]) + (self.slots[k, 2] + self.slots[k, 3])

    def out_copy(self):
        ref = self.out.at[self.half]
        return remote(ref, ref, self.core_sems.at[2], self.core_sems.at[3], self.place.sibling())

    def last(self):
        self.out[self.half] = self.take(2)
        self.out_copy().start()

    def finish(self):
        self.core_copy().wait_send()
        for k in range(3):
            for copy in self.copies(k):
                copy.wait_send()
        self.out_copy().wait()
        copy = pltpu.make_async_copy(self.out, self.result, self.core_sems.at[4])
        copy.start()
        copy.wait()


def total_buffers(rows):
    return [pltpu.VMEM((rows, 1024), F32), pltpu.VMEM((3, RING, rows // 2, 1024), F32), pltpu.VMEM((rows // 2, 1024), F32),
            DMA((3, 3)), DMA((3, 3)), DMA((5,))]


TOTAL_PEERS = NEAR + tuple((axis, 2) for axis in "xyz")


HEAD = 64
SEQ = 197
ROWS = 208
WIDTH = 1024
BLOCKS = RING
FF_HALF = 128
QKV = 192
EPS = 1e-06
SMALL = 16
SUM_ROWS = 32
LAYER_SUMS = 14


def wide(block):
    return jnp.concatenate([block[i] for i in range(RING)], axis=1)


def tall(ref, start, rows):
    return jnp.concatenate([wide(ref[j, :, start : start + rows, :]) for j in range(BLOCKS)], axis=0)


def as_rows(ref):
    return wide(ref[...]).astype(F32)


def put_rows(ref, value):
    for i in range(RING):
        ref[i] = value[:, i * 256 : (i + 1) * 256].astype(ref.dtype)


def store_blocks(stage, slot, start, value):
    rows = value.shape[0] // BLOCKS
    for j in range(BLOCKS):
        for i in range(RING):
            block = value[j * rows : (j + 1) * rows, i * 256 : (i + 1) * 256]
            stage[slot, j, i, start : start + rows, :] = block.astype(stage.dtype)


def feature_row(small, layer, row):
    return jnp.concatenate([small[0, 0, 0, i, 8 * layer + row : 8 * layer + row + 1, :] for i in range(RING)], axis=1)


def here_row(small, step, layer, row, start, width):
    at = 8 * layer + row
    return jnp.concatenate([small[0, step, j, 0, at : at + 1, start : start + width] for j in range(BLOCKS)], axis=1)


def dot_nt(a, b):
    return lax.dot_general(a, b, (((1,), (1,)), ((), ())), preferred_element_type=F32)


def dot_nn(a, b):
    return lax.dot_general(a, b, (((1,), (0,)), ((), ())), preferred_element_type=F32)


def dot_tn(a, b):
    return lax.dot_general(a, b, (((0,), (0,)), ((), ())), preferred_element_type=F32)


def norm_parts(x):
    average = jnp.mean(x, axis=1, keepdims=True)
    centered = x - average
    inverse = lax.rsqrt(jnp.mean(centered * centered, axis=1, keepdims=True) + EPS)
    return centered * inverse, inverse


def norm_low(x, small, layer, j):
    normed, _ = norm_parts(x)
    return (normed * feature_row(small, layer, j) + feature_row(small, layer, 2 + j)).astype(BF16)


def norm_back(incoming, x, gain):
    normed, inverse = norm_parts(x)
    scaled = incoming * gain
    mean = jnp.mean(scaled, axis=1, keepdims=True)
    along = jnp.mean(scaled * normed, axis=1, keepdims=True)
    result = inverse * (scaled - mean - normed * along)
    return result, jnp.sum(incoming * normed, axis=0, keepdims=True), jnp.sum(incoming, axis=0, keepdims=True)


def softmax(queries, keys):
    scores = dot_nt(queries, keys) * HEAD**-0.5
    column = lax.broadcasted_iota(jnp.int32, scores.shape, 1)
    scores = jnp.where(column < SEQ, scores, -1e30)
    highest = jnp.max(scores, axis=1, keepdims=True)
    expon = jnp.exp(scores - highest)
    return expon * (1.0 / jnp.sum(expon, axis=1, keepdims=True))


def head_parts(mixed, j):
    at = j * QKV
    return mixed[:, at : at + HEAD], mixed[:, at + HEAD : at + 2 * HEAD], mixed[:, at + 2 * HEAD : at + QKV]


class Stream:
    def __init__(self, pairs, sems):
        self.pairs, self.sems = pairs, sems

    def copies(self, step):
        slot = step % 2
        return [
            pltpu.make_async_copy(source(step), slots.at[slot], self.sems.at[slot, k])
            for k, (source, slots) in enumerate(self.pairs)
        ]

    def start(self, step):
        for copy in self.copies(step):
            copy.start()

    def run(self, body, hooks):
        def one(step, _):
            for copy in self.copies(step):
                copy.wait()

            @pl.when(step + 1 < STEPS)
            def _():
                self.start(step + 1)

            body(step, step % 2)
            for at in sorted(hooks):
                @pl.when(step == at)
                def _(at=at):
                    for act in hooks[at]:
                        act()
            return 0

        self.start(0)
        lax.fori_loop(0, STEPS, one, 0)


ORDER = [(0, 0), (1, 0), (2, 0), (0, 1), (1, 1), (2, 1)]
SAVED = [
    jax.ShapeDtypeStruct((2, STEPS, ROWS, BLOCKS * QKV), BF16),
    jax.ShapeDtypeStruct((2, STEPS, ROWS, BLOCKS * HEAD), BF16),
    jax.ShapeDtypeStruct((2, STEPS, BLOCKS, ROWS, ROWS), BF16),
    jax.ShapeDtypeStruct((2, 2, STEPS, ROWS, BLOCKS * FF_HALF), BF16),
    jax.ShapeDtypeStruct((2, 2, STEPS, ROWS, BLOCKS * FF_HALF), BF16),
]
TOKENS = jax.ShapeDtypeStruct((ROWS, WIDTH), F32)
TURNED = jax.ShapeDtypeStruct((RING, ROWS, 256), BF16)
LOWS = jax.ShapeDtypeStruct((2, 2, ROWS, WIDTH), BF16)
WEIGHTS = jax.ShapeDtypeStruct((6, RING, RING, RING, UNIT, 256), BF16)
SMALLS = jax.ShapeDtypeStruct((1, RING, RING, RING, SMALL, 256), F32)


def scratch_like(shape):
    return pltpu.VMEM(shape.shape, shape.dtype)


def forward_kernel(own_ref, small_ref, tokens_ref, cotangent_ref, full, small_out, x0_out, g_out, mid_out, x1_out, end_out, low_out,
                   mixed_out, att_out, probs_out, act_out, slope_out,
                   small, x0, resid, lows, acc, mids, ends, slots, mixed_all, att_all, probs_all, act_all, slope_all, *sems):
    place = Place()
    turn_x, turn_g = Turn(place, tokens_ref, x0, *sems[0:3]), Turn(place, cotangent_ref, g_out, *sems[3:6])
    load, saves, misc = sems[6:9]
    gather = Gather(place, own_ref, full, small_ref, small, sems[9:])
    units = [number(*pair) for pair in ORDER]

    own_copies = [
        pltpu.make_async_copy(own_ref.at[:, place.mine],
                              full.at[:, place.at["y"], place.at["z"], place.at["x"], place.mine], misc.at[0]),
        pltpu.make_async_copy(small_ref, small.at[:, place.at["y"], place.at["z"], place.at["x"]], misc.at[1]),
    ]
    for copy in own_copies:
        copy.start()
    place.greet(NEAR + (("x", 2),))
    gather.begin()
    turn_x.start()
    for copy in own_copies:
        copy.wait()
    gather.small_phase(1, "first")
    for unit in units[:2]:
        gather.first_two(unit)
    for unit in units[:2]:
        gather.second_two(unit)
    gather.small_phase(1, "second")
    for unit in units[:2]:
        gather.third_two(unit)
        gather.first_three(unit)
    for unit in units[2:]:
        gather.first_two(unit)
    gather.small_phase(1, "third")
    gather.small_phase(2, "first")
    gather.second_three(units[0])
    for unit in units[2:]:
        gather.second_two(unit)
    gather.small_phase(2, "second")
    gather.second_three(units[1])
    turn_x.end()
    resid[...] = as_rows(x0)
    gather.third_three(units[0])
    for unit in units[2:]:
        gather.third_two(unit)
    for unit in units[2:4]:
        gather.first_three(unit)
    gather.small_phase(2, "third")
    gather.ready(units[0])
    kept = []

    def keep(src, dst, k):
        copy = pltpu.make_async_copy(src, dst, misc.at[k])
        copy.start()
        kept.append((src, dst, k))

    keep(x0, x0_out, 2)
    keep(small, small_out, 3)
    turn_g.start()

    for k, (kind, layer) in enumerate(ORDER):
        unit = units[k]
        hooks = {2: [], 3: []}
        if k + 1 < 6:
            hooks[2] += [functools.partial(gather.third_three, units[k + 1])]
            if k + 2 < 6:
                hooks[2] += [functools.partial(gather.second_three, units[k + 2])]
            if k + 4 < 6:
                hooks[2] += [functools.partial(gather.first_three, units[k + 4])]
            hooks[3] += [functools.partial(gather.ready, units[k + 1])]

        def save(which, src, dst, step):
            return pltpu.make_async_copy(src, dst, saves.at[which, k, step])

        if kind == 0:
            low = lows.at[layer, 0]
            low[...] = norm_low(resid[...], small, layer, 0)
            keep(low, low_out.at[layer, 0], 8 + 2 * layer)
            acc[...] = resid[...] + feature_row(small, layer, 4)

            def body(step, slot):
                weights = slots.at[slot]
                mixed = dot_nt(low[...], tall(weights, 0, QKV)) + here_row(small, step, layer, 7, 0, QKV)
                mixed = mixed.astype(BF16)
                mixed_all[layer, step] = mixed
                attended = []
                for j in range(BLOCKS):
                    queries, keys, values = head_parts(mixed, j)
                    probs = softmax(queries, keys).astype(BF16)
                    probs_all[layer, step, j] = probs
                    attended.append(dot_nn(probs, values).astype(BF16))
                attended = jnp.concatenate(attended, axis=1)
                att_all[layer, step] = attended
                acc[...] += dot_nn(attended, tall(weights, QKV, HEAD))
                for copy in copies(step):
                    copy.start()

            def copies(step):
                pairs = ((mixed_all, mixed_out), (att_all, att_out), (probs_all, probs_out))
                return [save(i, src.at[layer, step], dst.at[layer, step], step) for i, (src, dst) in enumerate(pairs)]
        else:
            half = kind - 1
            if half == 0:
                mids[layer] = acc[...]
                resid[...] = acc[...]
                low = lows.at[layer, 1]
                low[...] = norm_low(resid[...], small, layer, 1)
                keep(low, low_out.at[layer, 1], 9 + 2 * layer)
                acc[...] = resid[...] + feature_row(small, layer, 5)
                keep(mids.at[layer], mid_out.at[layer], 4 + layer)

            def body(step, slot):
                weights = slots.at[slot]
                upward = dot_nt(low[...], tall(weights, 0, FF_HALF)) + here_row(small, step, layer, 6, half * FF_HALF, FF_HALF)
                below = 0.5 + 0.5 * lax.erf(upward * 2**-0.5)
                activated = (upward * below).astype(BF16)
                act_all[layer, half, step] = activated
                slope = below + upward * (jnp.exp(-0.5 * upward * upward) * (2 * jnp.pi) ** -0.5)
                slope_all[layer, half, step] = slope.astype(BF16)
                acc[...] += dot_nn(activated, tall(weights, FF_HALF, FF_HALF))
                for copy in copies(step):
                    copy.start()

            def copies(step):
                pairs = ((act_all, act_out), (slope_all, slope_out))
                return [save(i, src.at[layer, half, step], dst.at[layer, half, step], step) for i, (src, dst) in enumerate(pairs)]

        Stream([(lambda step: full.at[unit, step], slots)], load.at[k]).run(body, hooks)
        for step in range(STEPS):
            for copy in copies(step):
                copy.wait()
        if kind == 2 and layer == 0:
            resid[...] = acc[...]
            keep(resid, x1_out, 6)
            pltpu.make_async_copy(resid, x1_out, misc.at[6]).wait()
            kept.pop()
    put_rows(ends, acc[...])
    keep(ends, end_out, 7)
    turn_g.end()
    gather.finish()
    for src, dst, k in kept:
        pltpu.make_async_copy(src, dst, misc.at[k]).wait()


def forward(own, small, tokens, cotangent):
    both = jax.ShapeDtypeStruct((2, ROWS, WIDTH), F32)
    return pl.pallas_call(
        forward_kernel,
        out_shape=[WEIGHTS, SMALLS, TURNED, TURNED, both, TOKENS, TURNED, LOWS, *SAVED],
        in_specs=[VMEM] * 4,
        out_specs=[ANY] * 13,
        scratch_shapes=[
            scratch_like(SMALLS), scratch_like(TURNED), scratch_like(TOKENS), scratch_like(LOWS),
            scratch_like(TOKENS), scratch_like(both), scratch_like(TURNED), pltpu.VMEM((2, RING, RING, UNIT, 256), BF16),
            *[scratch_like(s) for s in SAVED],
            *TURN_SEMAPHORES, *TURN_SEMAPHORES, DMA((6, 2, 1)), DMA((3, 6, STEPS)), DMA((12,)),
            *gather_semaphores(),
        ],
        compiler_params=pltpu.CompilerParams(vmem_limit_bytes=VMEM_LIMIT, collective_id=0, has_side_effects=True),
        name="forward",
    )(own, small, tokens, cotangent)


BACK = [(2, 1), (1, 1), (0, 1), (2, 0), (1, 0), (0, 0)]


def backward_kernel(full, small_in, x0_in, g_in, mid_in, x1_in, end_ref, lows_in, mixed_in, att_in, probs_in, act_in, slope_in,
                    encoded_out, tokens_out, grads_out, sums_out,
                    grad, low, acc, turned, small, lows, xbuf, sums, columns_all, slots, mixed_two, att_two, probs_two, act_two, slope_two, stage, outs,
                    *rest):
    first, pair = [rest[0:2], rest[2:4], rest[4:6]], [rest[6:8], rest[8:10]]
    later = [rest[10:16], rest[16:22]]
    total_scratch, sems = rest[22:28], rest[28:]
    place = Place()
    turn_out, turn_g = Turn(place, end_ref, encoded_out, *sems[0:3]), Turn(place, turned, tokens_out, *sems[3:6])
    load, free, misc = sems[6:9]
    unit_sems = [[group.at[k] for group in sems[9:]] for k in range(6)]
    scatters = []
    for k, (kind, layer) in enumerate(BACK):
        scatters.append(
            Scatter(place, kind, layer, stage, [*first[k % 3], *pair[k % 2]], later[k % 2][0:3], later[k % 2][3:6], outs.at[k],
                    grads_out.at[number(kind, layer)], unit_sems[k])
        )
    total = Total(place, sums, total_scratch[0], sums_out, *total_scratch[1:])
    norms = [(1, 1), (1, 0), (0, 1), (0, 0)]

    def fetch_low(phase):
        return pltpu.make_async_copy(lows_in.at[norms[phase][0], norms[phase][1]], lows.at[phase % 2], misc.at[phase])

    def fetch_x(phase):
        source = (mid_in.at[1], x1_in, mid_in.at[0], x0_in)[phase]
        return pltpu.make_async_copy(source, turned if phase == 3 else xbuf, misc.at[4 + phase])

    starts = [pltpu.make_async_copy(g_in, turned, misc.at[8]),
              pltpu.make_async_copy(small_in.at[:, pl.ds(0, 1), pl.ds(0, 1)], small, misc.at[9]),
              fetch_low(0)]
    for copy in starts:
        copy.start()
    place.greet(TOTAL_PEERS)
    turn_out.start()
    for copy in starts:
        copy.wait()
    grad[...] = as_rows(turned)
    sums[...] = jnp.zeros_like(sums)
    columns_all[...] = jnp.zeros_like(columns_all)

    def leave(k, peers=NEAR):
        place.tell(free.at[k], peers)

    def may(k, peers=NEAR):
        pl.semaphore_wait(free.at[k], len(peers))

    for k, (kind, layer) in enumerate(BACK):
        it = scatters[k]
        hooks = {0: [], 1: [], 2: [], 3: []}
        if k >= 1:
            hooks[0] += [scatters[k - 1].open]
            hooks[2] += [scatters[k - 1].sides_one]
        if k >= 2:
            hooks[1] += [scatters[k - 2].centre_one, scatters[k - 2].start_two]
            hooks[2] += [scatters[k - 2].sides_two]
            hooks[3] += [scatters[k - 2].centre_two]
        if k >= 3:
            hooks[0] += [scatters[k - 3].sides_three]
            hooks[1] += [scatters[k - 3].centre_three]
        if k >= 2:
            hooks[1] += [functools.partial(leave, k + 1)]
        base = LAYER_SUMS * layer

        def begin(step):
            @pl.when(step >= 2)
            def _():
                it.free(step - 2)

            if k >= 1:
                @pl.when(step == 0)
                def _():
                    scatters[k - 1].free_last()
                    if k >= 3:
                        may(k)

        if kind == 0:
            phase = 3 - 2 * layer
            here = lows.at[phase % 2]
            fetch_low(phase).wait()
            if phase < 3:
                fetch_low(phase + 1).start()
            fetch_x(phase).start()
            low[...] = grad[...].astype(BF16)
            acc[...] = jnp.zeros_like(acc)

            def body(step, slot):
                weights = slots.at[slot]
                begin(step)
                g = low[...]
                mixed = mixed_two[slot]
                store_blocks(stage, slot, QKV, dot_tn(att_two[slot], g))
                g_all = dot_nt(g, tall(weights, QKV, HEAD)).astype(BF16)
                g_mixed = []
                for j in range(BLOCKS):
                    queries, keys, values = head_parts(mixed, j)
                    g_att = g_all[:, j * HEAD : (j + 1) * HEAD]
                    probs_low = probs_two[slot, j]
                    probs = probs_low.astype(F32)
                    g_probs = dot_nt(g_att, values)
                    g_values = dot_tn(probs_low, g_att)
                    centre = jnp.sum(probs * g_probs, axis=1, keepdims=True)
                    g_scores = (probs * (g_probs - centre) * HEAD**-0.5).astype(BF16)
                    g_mixed += [dot_nn(g_scores, keys), dot_tn(g_scores, queries), g_values]
                g_mixed = jnp.concatenate([part.astype(BF16) for part in g_mixed], axis=1)
                store_blocks(stage, slot, 0, dot_tn(g_mixed, here[...]))
                it.hand_over(step)
                columns_all[layer, 1, step, :, : BLOCKS * QKV] = jnp.sum(g_mixed.astype(F32), axis=0, keepdims=True)
                acc[...] += dot_nn(g_mixed, tall(weights, 0, QKV))

            pairs = [
                (lambda step: full.at[number(kind, layer), step], slots),
                (lambda step: mixed_in.at[layer, step], mixed_two),
                (lambda step: att_in.at[layer, step], att_two),
                (lambda step: probs_in.at[layer, step], probs_two),
            ]
        else:
            half = kind - 1
            phase = 2 - 2 * layer
            here = lows.at[phase % 2]
            if half == 1:
                if phase > 0:
                    fetch_low(phase).wait()
                fetch_low(phase + 1).start()
                fetch_x(phase).start()
                low[...] = grad[...].astype(BF16)
                acc[...] = jnp.zeros_like(acc)

            def body(step, slot):
                weights = slots.at[slot]
                begin(step)
                g = low[...]
                store_blocks(stage, slot, FF_HALF, dot_tn(act_two[slot], g))
                g_up = (dot_nt(g, tall(weights, FF_HALF, FF_HALF)) * slope_two[slot].astype(F32)).astype(BF16)
                store_blocks(stage, slot, 0, dot_tn(g_up, here[...]))
                it.hand_over(step)
                columns = jnp.sum(g_up.astype(F32), axis=0, keepdims=True)
                for j in range(BLOCKS):
                    at = j * 2 * FF_HALF + half * FF_HALF
                    columns_all[layer, 0, step, :, at : at + FF_HALF] = columns[:, j * FF_HALF : (j + 1) * FF_HALF]
                acc[...] += dot_nn(g_up, tall(weights, 0, FF_HALF))

            pairs = [
                (lambda step: full.at[number(kind, layer), step], slots),
                (lambda step: act_in.at[layer, half, step], act_two),
                (lambda step: slope_in.at[layer, half, step], slope_two),
            ]
        Stream(pairs, load.at[k]).run(body, hooks)
        if kind < 2:
            j = kind
            fetch_x(phase).wait()
            x = as_rows(turned) if phase == 3 else xbuf[...]
            part, gain, shift = norm_back(acc[...], x, feature_row(small, layer, j))
            at = base + (8 if kind == 1 else 11)
            sums[at : at + 1, :] = jnp.sum(low[...].astype(F32), axis=0, keepdims=True)
            sums[at + 1 : at + 2, :] = gain
            sums[at + 2 : at + 3, :] = shift
            grad[...] = grad[...] + part
        if k == 5:
            put_rows(turned, grad[...])
            turn_g.start()
            for i in range(2):
                for which in range(2):
                    for step in range(STEPS):
                        at = LAYER_SUMS * i + STEPS * which + step
                        sums[at : at + 1, :] = columns_all[i, which, step]
            total.start()
    early, late = scatters[4], scatters[5]
    late.free_last()
    may(6)
    late.open()
    scatters[3].sides_three()
    total.core_sum()
    early.centre_one()
    early.start_two()
    scatters[3].centre_three()
    leave(7, TOTAL_PEERS)
    late.sides_one()
    total.put(1, total.take(0))
    early.sides_two()
    early.centre_two()
    for it in scatters[:4]:
        it.shown()
    total.put(2, total.take(1))
    early.sides_three()
    late.centre_one()
    may(7, TOTAL_PEERS)
    late.each("direct", 1)
    early.centre_three()
    total.last()
    late.direct_centre(1)
    late.each("direct", 2)
    turn_out.end()
    turn_g.end()
    early.shown()
    total.finish()
    late.direct_centre(2)
    late.show().start()
    late.sent(1)
    late.sent(2)
    late.shown()
    for it in scatters:
        it.keep().wait()


def backward(full, small, x0, g, mids, x1, ends, lows, saved):
    saved_two = [pltpu.VMEM((2,) + s.shape[-3 if len(s.shape) == 5 and s.shape[1] == STEPS else -2 :], s.dtype) for s in SAVED]
    semaphores = [pltpu.SemaphoreType.DMA((6,) + (s.shape if hasattr(s, "shape") else ())) for s in scatter_semaphores()]
    return pl.pallas_call(
        backward_kernel,
        out_shape=[TURNED, TURNED, jax.ShapeDtypeStruct((6, UNIT, 256), F32), jax.ShapeDtypeStruct((SUM_ROWS, WIDTH), F32)],
        in_specs=[ANY] * 13,
        out_specs=[ANY] * 4,
        scratch_shapes=[
            scratch_like(TOKENS), pltpu.VMEM((ROWS, WIDTH), BF16), scratch_like(TOKENS),
            scratch_like(TURNED), pltpu.VMEM((1, 1, 1, RING, SMALL, 256), F32), pltpu.VMEM((2, ROWS, WIDTH), BF16), scratch_like(TOKENS),
            pltpu.VMEM((SUM_ROWS, WIDTH), F32), pltpu.VMEM((2, 2, STEPS, 1, WIDTH), F32),
            pltpu.VMEM((2, RING, RING, UNIT, 256), BF16),
            *saved_two,
            pltpu.VMEM((2, RING, RING, UNIT, 256), BF16), pltpu.VMEM((6, UNIT, 256), F32),
            *first_buffers(), *first_buffers(), *first_buffers(), *pair_buffers(), *pair_buffers(), *later_buffers(), *later_buffers(),
            *total_buffers(SUM_ROWS),
            *TURN_SEMAPHORES, *TURN_SEMAPHORES, DMA((6, 2, 4)), pltpu.SemaphoreType.REGULAR((8,)), DMA((10,)),
            *semaphores,
        ],
        compiler_params=pltpu.CompilerParams(vmem_limit_bytes=VMEM_LIMIT, collective_id=1, has_side_effects=True),
        name="backward",
    )(full, small, x0, g, mids, x1, ends, lows, *saved)


def to_images(rows):
    return jnp.pad(rows.reshape(3, SEQ, 256), ((0, 1), (0, ROWS - SEQ), (0, 0)))


def from_images(turned):
    return turned[:3, :SEQ].reshape(3 * SEQ, 256).astype(F32)


def shards(tokens, norm_gain, norm_shift, qkv_weight, qv_bias, proj_weight, proj_bias, up_weight, up_bias, down_weight, down_bias, cotangent):
    layers = qkv_weight.shape[0]
    attention = jnp.concatenate([qkv_weight.transpose(0, 2, 1), proj_weight], axis=1)
    up = up_weight.transpose(0, 2, 1)
    halves = [jnp.concatenate([part[:, at : at + FF_HALF] for part in (up, down_weight)], axis=1) for at in (0, FF_HALF)]
    own = jnp.concatenate([attention, *halves], axis=0)
    zeros = jnp.zeros((layers, HEAD), F32)
    qkv_row = jnp.concatenate([qv_bias[:, :HEAD], zeros, qv_bias[:, HEAD:], zeros], axis=1)
    small = jnp.stack([norm_gain[:, 0], norm_gain[:, 1], norm_shift[:, 0], norm_shift[:, 1], proj_bias, down_bias, up_bias, qkv_row], axis=1)
    full, small, x0, g, mids, x1, ends, lows, *saved = forward(
        own, small.reshape(1, SMALL, 256), to_images(tokens), to_images(cotangent.astype(BF16))
    )
    encoded, grad_tokens, grads, sums = backward(full, small, x0, g, mids, x1, ends, lows, saved)
    row, col = lax.axis_index("row"), lax.axis_index("col")
    sums = sums[: layers * LAYER_SUMS].reshape(layers, LAYER_SUMS, WIDTH)
    up_sums = lax.dynamic_slice_in_dim(sums[:, 0:4].reshape(layers, 16, 256), col, 1, 1)[:, 0]
    qkv_sums = sums[:, 4:8, : BLOCKS * QKV].reshape(layers, 16, QKV)
    qkv_sums = lax.dynamic_slice_in_dim(qkv_sums, col, 1, 1)[:, 0]
    features = lax.dynamic_slice_in_dim(sums[:, 8:].reshape(layers, 6, RING, 256), row, 1, 2)[:, :, 0]
    attention, first, second = grads[0:2], grads[2:4], grads[4:6]
    return (
        from_images(encoded),
        from_images(grad_tokens),
        jnp.stack([features[:, 4], features[:, 1]], axis=1),
        jnp.stack([features[:, 5], features[:, 2]], axis=1),
        attention[:, :QKV].transpose(0, 2, 1),
        jnp.concatenate([qkv_sums[:, :HEAD], qkv_sums[:, 2 * HEAD : QKV]], axis=1),
        attention[:, QKV:],
        features[:, 3],
        jnp.concatenate([first[:, :FF_HALF], second[:, :FF_HALF]], axis=1).transpose(0, 2, 1),
        up_sums,
        jnp.concatenate([first[:, FF_HALF:], second[:, FF_HALF:]], axis=1),
        features[:, 0],
    )


def solution(mesh):
    in_specs = (
        P(("dp", "col"), "row"),
        P(None, None, "row"),
        P(None, None, "row"),
        P(None, "row", "col"),
        P(None, "col"),
        P(None, "col", "row"),
        P(None, "row"),
        P(None, "row", "col"),
        P(None, "col"),
        P(None, "col", "row"),
        P(None, "row"),
        P(("dp", "col"), "row"),
    )
    out_specs = (
        P(("dp", "col"), "row"),
        P(("dp", "col"), "row"),
        P(None, None, "row"),
        P(None, None, "row"),
        P(None, "row", "col"),
        P(None, "col"),
        P(None, "col", "row"),
        P(None, "row"),
        P(None, "row", "col"),
        P(None, "col"),
        P(None, "col", "row"),
        P(None, "row"),
    )
    return jax.shard_map(shards, mesh=mesh, in_specs=in_specs, out_specs=out_specs, check_vma=False)
```

```python
import functools

import jax
import jax.numpy as jnp
from jax import lax
from jax.experimental import pallas as pl
from jax.experimental.pallas import tpu as pltpu
from jax.sharding import PartitionSpec as P

MESH = pl.DeviceIdType.MESH
RING = 4
STEPS = 4
AXES = "yzx"
ORDERS = (("x", "y", "z"), ("y", "z", "x"), ("z", "x", "y"))
KINDS = 3
UNIT = 256
CORE = 128
CUTS = (((0, 48), (48, 48), (96, 32)), ((0, 48), (48, 32), (80, 48)), ((0, 32), (32, 48), (80, 48)))
NEAR = tuple((axis, by) for axis in "xyz" for by in (1, -1)) + (("core", 1),)
ROW_PEERS = (("x", 1), ("x", 2), ("x", -1))
VMEM_LIMIT = 60 * 2**20
DMA = pltpu.SemaphoreType.DMA
ANY = pl.BlockSpec(memory_space=pl.ANY)
VMEM = pl.BlockSpec(memory_space=pltpu.VMEM)
BF16 = jnp.bfloat16
F32 = jnp.float32


def number(kind, layer):
    return 2 * kind + layer


class Place:
    def __init__(self):
        self.core = lax.axis_index("dp")
        block = lax.axis_index("col")
        self.at = {"x": lax.axis_index("row"), "y": block // RING, "z": block % RING}
        self.mine = pl.ds(pl.multiple_of(self.core * CORE, CORE), CORE)
        self.other = pl.ds(pl.multiple_of((1 - self.core) * CORE, CORE), CORE)

    def shifted(self, axis, by):
        moved = dict(self.at)
        moved[axis] = (self.at[axis] + by + RING) % RING
        return moved

    def neighbour(self, axis, by):
        if axis == "core":
            return (1 - self.core, self.at["x"], self.at["y"] * RING + self.at["z"])
        at = self.shifted(axis, by)
        return (self.core, at["x"], at["y"] * RING + at["z"])

    def sibling(self):
        return self.neighbour("core", 1)

    def tell(self, semaphore, peers):
        for axis, by in peers:
            pl.semaphore_signal(semaphore, inc=1, device_id=self.neighbour(axis, by), device_id_type=MESH)

    def greet(self, peers):
        barrier = pltpu.get_barrier_semaphore()
        self.tell(barrier, peers)
        pl.semaphore_wait(barrier, len(peers))


def region(ref, axes, at, whole, start, count):
    index = tuple(pl.ds(0, RING) if a in whole else at[a] for a in axes)
    return ref.at[index + (pl.ds(start, count),)]


def remote(src, dst, send, recv, device):
    return pltpu.make_async_remote_copy(
        src_ref=src, dst_ref=dst, send_sem=send, recv_sem=recv, device_id=device, device_id_type=MESH
    )


class Ring:
    def __init__(self, place, full, units, order, phase, start, count, half, sems, own=None):
        self.place, self.full, self.units, self.own = place, full, units, own
        self.axis, self.whole = order[phase], order[:phase]
        self.start, self.count = start, count
        self.halves = ((start, half), (start + half, count - half))
        self.whole_send, self.half_send, self.whole_recv, self.half_recv = sems

    def piece(self, by, start, count):
        at = self.place.shifted(self.axis, by)
        index = tuple(pl.ds(0, RING) if a in self.whole else at[a] for a in AXES)
        return self.full.at[(self.units,) + index + (pl.ds(start, count),)]

    def to(self, i):
        return self.place.neighbour(self.axis, (1, -1)[i])

    def whole_copy(self, i):
        here = self.piece(0, self.start, self.count)
        return remote(here if self.own is None else self.own, here, self.whole_send[i], self.whole_recv[i], self.to(i))

    def half_copy(self, i):
        ref = self.piece((-1, 1)[i], *self.halves[i])
        return remote(ref, ref, self.half_send[i], self.half_recv[i], self.to(i))

    def share(self, send, recv, *which):
        for by in which:
            if by is None:
                index = tuple(pl.ds(0, RING) if a in self.whole + (self.axis,) else self.place.at[a] for a in AXES)
                ref = self.full.at[(self.units,) + index + (pl.ds(self.start, self.count),)]
            else:
                ref = self.piece(by, self.start, self.count)
            remote(ref, ref, send, recv, self.place.sibling()).start()

    def first(self):
        for i in range(2):
            self.whole_copy(i).start()

    def second(self):
        for i in range(2):
            self.half_copy(i).start()


class Gather:
    def __init__(self, place, own, full, small_own, small_full, sems):
        self.place, self.full = place, full
        self.send, self.whole, self.half, self.share_send, self.share_recv, small_send, small_recv = sems
        self.one, self.two, self.three = [], {}, {}
        base = pl.multiple_of(place.core * CORE, CORE)

        def shared(k):
            return tuple([group.at[k]] * 2 for group in (self.send, self.send, self.whole, self.half))

        for kind in range(KINDS):
            for p, (start, count) in enumerate(CUTS[kind]):
                rows = base + start
                self.one.append(
                    Ring(place, full, pl.ds(2 * kind, 2), ORDERS[p], 0, rows, count, 16, shared(0),
                         own.at[pl.ds(2 * kind, 2), pl.ds(rows, count)])
                )
            for layer in range(2):
                u = number(kind, layer)
                for phase, into in ((1, self.two), (2, self.three)):
                    into[u] = [
                        Ring(place, full, u, ORDERS[p], phase, base + start, count,
                             count // 2 if count == 32 else (16, 32)[(p + layer) % 2], shared(self.place_of(u, phase)))
                        for p, (start, count) in enumerate(CUTS[kind])
                    ]
        rows = small_own.shape[1]
        self.small = [
            Ring(place, small_full, pl.ds(0, 1), ORDERS[0], phase, 0, rows, rows // 2,
                 [[group.at[phase, k + i] for i in range(2)] for group, k in
                  ((small_send, 0), (small_send, 2), (small_recv, 0), (small_recv, 2))],
                 small_own if phase == 0 else None)
            for phase in range(3)
        ]

    @staticmethod
    def place_of(u, phase):
        return 0 if phase == 0 else 1 + u + 6 * (phase - 1)

    def amount(self, u, phase, times):
        if phase == 0:
            return self.full.at[:, 0, 0, pl.ds(0, times), self.place.mine]
        if phase == 1:
            return self.full.at[u, pl.ds(0, times), :, 0, self.place.mine]
        return self.full.at[u, pl.ds(0, times), :, :, self.place.mine]

    def came(self, u, phase, sems, times):
        ref = self.amount(u, phase, times)
        at = self.place_of(u, phase)
        remote(ref, ref, self.send.at[at], sems.at[at], self.place.sibling()).wait_recv()

    def sent(self, u, phase):
        ref = self.amount(u, phase, 3)
        at = self.place_of(u, phase)
        remote(ref, ref, self.send.at[at], self.whole.at[at], self.place.sibling()).wait_send()

    def rings(self, u, phase):
        return self.one if phase == 0 else (self.two if phase == 1 else self.three)[u]

    def first(self, u, phase):
        for ring in self.rings(u, phase):
            ring.first()

    def second(self, u, phase):
        self.came(u, phase, self.whole, 2)
        for ring in self.rings(u, phase):
            ring.second()

    def third(self, u, phase):
        self.came(u, phase, self.half, 1)

    def begin(self):
        self.first(0, 0)
        self.small_phase(0, "first")
        self.second(0, 0)
        self.small_phase(0, "second")
        self.third(0, 0)
        self.small_phase(0, "third")

    def small_phase(self, phase, name):
        ring = self.small[phase]
        if name == "first":
            ring.first()
            return
        for i in range(2):
            if name == "second":
                ring.whole_copy(i).wait_recv()
                ring.half_copy(i).start()
            else:
                ring.half_copy(i).wait_recv()

    def first_two(self, u):
        self.first(u, 1)

    def second_two(self, u):
        self.second(u, 1)

    def third_two(self, u):
        self.third(u, 1)

    def share(self, u, phase, *which):
        for ring in self.rings(u, phase):
            ring.share(self.share_send.at[u], self.share_recv.at[u], *which)

    def first_three(self, u):
        self.first(u, 2)
        self.share(u, 1, None)

    def second_three(self, u):
        self.second(u, 2)
        self.share(u, 2, -1, 1)

    def third_three(self, u):
        self.third(u, 2)
        self.share(u, 2, 2)

    def ready(self, u):
        ref = self.full.at[u, :, :, :, self.place.mine]
        remote(ref, ref, self.share_send.at[u], self.share_recv.at[u], self.place.sibling()).wait()

    def finish(self):
        self.sent(0, 0)
        for u in range(6):
            self.sent(u, 1)
            self.sent(u, 2)
        for ring in self.small:
            for i in range(2):
                ring.whole_copy(i).wait_send()
                ring.half_copy(i).wait_send()


def gather_semaphores():
    return [DMA((13,)), DMA((13,)), DMA((13,)), DMA((6,)), DMA((6,)), DMA((3, 4)), DMA((3, 4))]


def blockwise(shape, body):
    if len(shape) < 4:
        body(())
        return

    def step(i, _):
        body((i,))
        return 0

    lax.fori_loop(0, shape[0], step, 0)


def add_to(dst, first, *others):
    def body(index):
        if len(others) == 1 and dst.dtype == BF16:
            dst[index] = first[index] + others[0][index]
            return
        total = first[index].astype(F32)
        for other in others:
            total = total + other[index].astype(F32)
        dst[index] = total.astype(dst.dtype)

    blockwise(dst.shape, body)


class Fold:
    def __init__(self, place, order, phase, work, half_in, full_in, dst, start, count, half, sems):
        self.place, self.work, self.half_in, self.full_in, self.dst = place, work, half_in, full_in, dst
        self.axis, self.whole = order[2 - phase], order[: 2 - phase]
        self.axes = tuple(a for a in AXES if a not in order[3 - phase :])
        self.start, self.count = start, count
        self.halves = ((start, half), (start + half, count - half))
        self.send, self.half_recv, self.whole_recv = sems
        self.lead = (slice(None),) * (2 - phase)

    def piece(self, by, start, count, ref=None):
        ref = self.work if ref is None else ref
        return region(ref, self.axes, self.place.shifted(self.axis, by), self.whole, start, count)

    def came(self, start, count):
        return self.half_in.at[self.lead + (pl.ds(start, count),)]

    def arrived(self, i):
        return self.full_in.at[(i,) + self.lead + (pl.ds(self.start, self.count),)]

    def opposite(self):
        for i in range(2):
            src, dst = self.piece(2, *self.halves[i]), self.came(*self.halves[i])
            remote(src, dst, self.send, self.half_recv, self.place.neighbour(self.axis, (1, -1)[i])).start()

    def side(self, i):
        by = (1, -1)[i]
        src = self.piece(by, self.start, self.count)
        remote(src, self.arrived(i), self.send, self.whole_recv, self.place.neighbour(self.axis, by)).start()

    def sides(self):
        for i in range(2):
            ref = self.piece((1, -1)[i], *self.halves[i])
            add_to(ref, ref, self.came(*self.halves[i]))
            self.side(i)

    def centre(self):
        add_to(self.dst, self.piece(0, self.start, self.count), self.arrived(0), self.arrived(1))

    def direct(self):
        for i in range(2):
            self.side(i)
        src = self.piece(2, self.start, self.count)
        remote(src, self.came(self.start, self.count), self.send, self.half_recv, self.place.neighbour(self.axis, 2)).start()

    def direct_centre(self):
        add_to(self.dst, self.piece(0, self.start, self.count), self.arrived(0), self.arrived(1),
               self.came(self.start, self.count))


class Scatter:
    def __init__(self, place, kind, layer, stage, first, second, third, out, result, sems):
        self.place, self.stage = place, stage
        self.work, self.twin, reduced, inner = first[0], first[1], second[0], third[0]
        self.out, self.result = out, result
        (self.near, self.far_send, self.far_recv, self.send, self.half, self.whole, self.show_send, self.show_recv,
         self.local) = sems
        base = pl.multiple_of(place.core * CORE, CORE)
        self.works = (self.work, reduced, inner)
        self.half_in = (first[2], second[1], third[1])
        self.full_in = (first[3], second[2], third[2])
        targets = (
            lambda start, count: reduced.at[:, :, pl.ds(start, count)],
            lambda start, count: inner.at[:, pl.ds(start, count)],
            lambda start, count: out.at[pl.ds(base + start, count)],
        )
        self.parts = [
            [
                Fold(place, ORDERS[p], phase, self.works[phase], self.half_in[phase], self.full_in[phase],
                     targets[phase](start, count), start, count,
                     count // 2 if count == 32 else (16, 32)[(p + layer) % 2],
                     (self.send.at[phase], self.half.at[phase], self.whole.at[phase]))
                for p, (start, count) in enumerate(CUTS[kind])
            ]
            for phase in range(3)
        ]

    def stay(self, step):
        slot = step % 2
        return pltpu.make_async_copy(self.stage.at[slot, :, :, self.place.mine], self.work.at[step], self.near.at[slot])

    def go(self, step):
        slot = step % 2
        return remote(self.stage.at[slot, :, :, self.place.other], self.twin.at[step], self.far_send.at[slot],
                      self.far_recv, self.place.sibling())

    def free(self, step):
        self.stay(step).wait()
        self.go(step).wait_send()

    def hand_over(self, step):
        self.stay(step).start()
        self.go(step).start()

    def free_last(self):
        for step in (STEPS - 2, STEPS - 1):
            self.free(step)

    def join(self, *which):
        for by in which:
            for part in self.parts[0]:
                ref = part.piece(by, part.start, part.count)
                add_to(ref, ref, part.piece(by, part.start, part.count, self.twin))

    def each(self, name, phase):
        for part in self.parts[phase]:
            getattr(part, name)()

    def came(self, refs, sems, phase):
        remote(refs[phase], refs[phase], self.send.at[phase], sems.at[phase], self.place.sibling()).wait_recv()

    def sent(self, phase):
        ref = self.works[phase].at[pl.ds(0, 3)]
        remote(ref, ref, self.send.at[phase], self.half.at[phase], self.place.sibling()).wait_send()

    def show(self):
        ref = self.out.at[self.place.mine]
        return remote(ref, ref, self.show_send, self.show_recv, self.place.sibling())

    def keep(self):
        return pltpu.make_async_copy(self.out, self.result, self.local)

    def sides(self, phase):
        self.came(self.half_in, self.half, phase)
        self.each("sides", phase)

    def centre(self, phase):
        self.came(self.full_in, self.whole, phase)
        self.each("centre", phase)

    def direct_centre(self, phase):
        self.came(self.full_in, self.whole, phase)
        self.came(self.half_in, self.half, phase)
        self.each("direct_centre", phase)

    def open(self):
        remote(self.twin, self.twin, self.far_send.at[0], self.far_recv, self.place.sibling()).wait_recv()
        self.join(2)
        self.each("opposite", 0)
        self.join(1, -1)

    def sides_one(self):
        self.sides(0)
        self.join(0)

    def centre_one(self):
        self.centre(0)
        self.sent(0)

    def start_two(self):
        self.each("opposite", 1)

    def sides_two(self):
        self.sides(1)

    def centre_two(self):
        self.centre(1)
        self.each("opposite", 2)

    def sides_three(self):
        self.sides(2)

    def centre_three(self):
        self.centre(2)
        self.show().start()
        self.sent(1)
        self.sent(2)

    def shown(self):
        self.show().wait()
        self.keep().start()


def first_buffers():
    blocks = (RING,) * 3 + (CORE, 256)
    return [pltpu.VMEM(blocks, BF16), pltpu.VMEM(blocks, BF16)]


def pair_buffers():
    blocks = (RING,) * 2 + (CORE, 256)
    return [pltpu.VMEM(blocks, BF16), pltpu.VMEM((2,) + blocks, BF16)]


def later_buffers():
    def some(*lead):
        return pltpu.VMEM(lead + (CORE, 256), BF16)

    return [some(RING, RING), some(RING), some(2, RING), some(RING), some(), some(2)]


def scatter_semaphores():
    return [DMA((2,)), DMA((2,)), DMA, DMA((3,)), DMA((3,)), DMA((3,)), DMA, DMA, DMA]


class Turn:
    def __init__(self, place, src, dst, send, recv, local):
        self.place, self.src, self.dst, self.send, self.recv, self.local = place, src, dst, send, recv, local

    def copies(self):
        row = self.place.at["x"]
        return [
            remote(self.src.at[self.place.shifted("x", by)["x"]], self.dst.at[row], self.send.at[k], self.recv.at[k],
                   self.place.neighbour("x", by))
            for k, (_, by) in enumerate(ROW_PEERS)
        ]

    def own(self):
        row = self.place.at["x"]
        return pltpu.make_async_copy(self.src.at[row], self.dst.at[row], self.local)

    def start(self):
        self.own().start()
        for copy in self.copies():
            copy.start()

    def end(self):
        self.own().wait()
        for copy in self.copies():
            copy.wait()


TURN_SEMAPHORES = [DMA((3,)), DMA((3,)), DMA]


class Total:
    def __init__(self, place, mine, out, result, slots, core_in, send, recv, core_sems):
        self.place, self.mine, self.out, self.result, self.slots = place, mine, out, result, slots
        self.send, self.recv, self.core_in, self.core_sems = send, recv, core_in, core_sems
        rows = mine.shape[0] // 2
        self.half = pl.ds(pl.multiple_of(place.core * rows, rows), rows)
        self.away = pl.ds(pl.multiple_of((1 - place.core) * rows, rows), rows)

    def core_copy(self):
        return remote(self.mine.at[self.away], self.core_in, self.core_sems.at[0], self.core_sems.at[1], self.place.sibling())

    def copies(self, k):
        axis = "xyz"[k]
        slot = self.slots.at[k, self.place.at[axis]]
        return [
            remote(slot, slot, self.send.at[k, j], self.recv.at[k, j], self.place.neighbour(axis, by))
            for j, by in enumerate((1, 2, -1))
        ]

    def start(self):
        self.core_copy().start()

    def core_sum(self):
        self.core_copy().wait_recv()
        self.put(0, self.mine[self.half] + self.core_in[...])

    def put(self, k, value):
        self.slots[k, self.place.at["xyz"[k]]] = value
        for copy in self.copies(k):
            copy.start()

    def take(self, k):
        for copy in self.copies(k):
            copy.wait_recv()
        return (self.slots[k, 0] + self.slots[k, 1]) + (self.slots[k, 2] + self.slots[k, 3])

    def out_copy(self):
        ref = self.out.at[self.half]
        return remote(ref, ref, self.core_sems.at[2], self.core_sems.at[3], self.place.sibling())

    def last(self):
        self.out[self.half] = self.take(2)
        self.out_copy().start()

    def finish(self):
        self.core_copy().wait_send()
        for k in range(3):
            for copy in self.copies(k):
                copy.wait_send()
        self.out_copy().wait()
        copy = pltpu.make_async_copy(self.out, self.result, self.core_sems.at[4])
        copy.start()
        copy.wait()


def total_buffers(rows):
    return [pltpu.VMEM((rows, 1024), F32), pltpu.VMEM((3, RING, rows // 2, 1024), F32), pltpu.VMEM((rows // 2, 1024), F32),
            DMA((3, 3)), DMA((3, 3)), DMA((5,))]


TOTAL_PEERS = NEAR + tuple((axis, 2) for axis in "xyz")


HEAD = 64
SEQ = 197
ROWS = 208
WIDTH = 1024
BLOCKS = RING
FF_HALF = 128
QKV = 192
EPS = 1e-06
SMALL = 16
SUM_ROWS = 32
LAYER_SUMS = 14


def wide(block):
    return jnp.concatenate([block[i] for i in range(RING)], axis=1)


def tall(ref, start, rows):
    return jnp.concatenate([wide(ref[j, :, start : start + rows, :]) for j in range(BLOCKS)], axis=0)


def as_rows(ref):
    return wide(ref[...]).astype(F32)


def put_rows(ref, value):
    for i in range(RING):
        ref[i] = value[:, i * 256 : (i + 1) * 256].astype(ref.dtype)


def store_blocks(stage, slot, start, value):
    rows = value.shape[0] // BLOCKS
    for j in range(BLOCKS):
        for i in range(RING):
            block = value[j * rows : (j + 1) * rows, i * 256 : (i + 1) * 256]
            stage[slot, j, i, start : start + rows, :] = block.astype(stage.dtype)


def feature_row(small, layer, row):
    return jnp.concatenate([small[0, 0, 0, i, 8 * layer + row : 8 * layer + row + 1, :] for i in range(RING)], axis=1)


def here_row(small, step, layer, row, start, width):
    at = 8 * layer + row
    return jnp.concatenate([small[0, step, j, 0, at : at + 1, start : start + width] for j in range(BLOCKS)], axis=1)


def dot_nt(a, b):
    return lax.dot_general(a, b, (((1,), (1,)), ((), ())), preferred_element_type=F32)


def dot_nn(a, b):
    return lax.dot_general(a, b, (((1,), (0,)), ((), ())), preferred_element_type=F32)


def dot_tn(a, b):
    return lax.dot_general(a, b, (((0,), (0,)), ((), ())), preferred_element_type=F32)


def norm_parts(x):
    average = jnp.mean(x, axis=1, keepdims=True)
    centered = x - average
    inverse = lax.rsqrt(jnp.mean(centered * centered, axis=1, keepdims=True) + EPS)
    return centered * inverse, inverse


def norm_low(x, small, layer, j):
    normed, _ = norm_parts(x)
    return (normed * feature_row(small, layer, j) + feature_row(small, layer, 2 + j)).astype(BF16)


def norm_back(incoming, x, gain):
    normed, inverse = norm_parts(x)
    scaled = incoming * gain
    mean = jnp.mean(scaled, axis=1, keepdims=True)
    along = jnp.mean(scaled * normed, axis=1, keepdims=True)
    result = inverse * (scaled - mean - normed * along)
    return result, jnp.sum(incoming * normed, axis=0, keepdims=True), jnp.sum(incoming, axis=0, keepdims=True)


def softmax(queries, keys):
    scores = dot_nt(queries, keys) * HEAD**-0.5
    column = lax.broadcasted_iota(jnp.int32, scores.shape, 1)
    scores = jnp.where(column < SEQ, scores, -1e30)
    highest = jnp.max(scores, axis=1, keepdims=True)
    expon = jnp.exp(scores - highest)
    return expon * (1.0 / jnp.sum(expon, axis=1, keepdims=True))


def head_parts(mixed, j):
    at = j * QKV
    return mixed[:, at : at + HEAD], mixed[:, at + HEAD : at + 2 * HEAD], mixed[:, at + 2 * HEAD : at + QKV]


class Stream:
    def __init__(self, pairs, sems):
        self.pairs, self.sems = pairs, sems

    def copies(self, step):
        slot = step % 2
        return [
            pltpu.make_async_copy(source(step), slots.at[slot], self.sems.at[slot, k])
            for k, (source, slots) in enumerate(self.pairs)
        ]

    def start(self, step):
        for copy in self.copies(step):
            copy.start()

    def run(self, body, hooks):
        def one(step, _):
            for copy in self.copies(step):
                copy.wait()

            @pl.when(step + 1 < STEPS)
            def _():
                self.start(step + 1)

            body(step, step % 2)
            for at in sorted(hooks):
                @pl.when(step == at)
                def _(at=at):
                    for act in hooks[at]:
                        act()
            return 0

        self.start(0)
        lax.fori_loop(0, STEPS, one, 0)


ORDER = [(0, 0), (1, 0), (2, 0), (0, 1), (1, 1), (2, 1)]
SAVED = [
    jax.ShapeDtypeStruct((2, STEPS, ROWS, BLOCKS * QKV), BF16),
    jax.ShapeDtypeStruct((2, STEPS, ROWS, BLOCKS * HEAD), BF16),
    jax.ShapeDtypeStruct((2, STEPS, BLOCKS, ROWS, ROWS), BF16),
    jax.ShapeDtypeStruct((2, 2, STEPS, ROWS, BLOCKS * FF_HALF), BF16),
    jax.ShapeDtypeStruct((2, 2, STEPS, ROWS, BLOCKS * FF_HALF), BF16),
]
TOKENS = jax.ShapeDtypeStruct((ROWS, WIDTH), F32)
TURNED = jax.ShapeDtypeStruct((RING, ROWS, 256), BF16)
LOWS = jax.ShapeDtypeStruct((2, 2, ROWS, WIDTH), BF16)
WEIGHTS = jax.ShapeDtypeStruct((6, RING, RING, RING, UNIT, 256), BF16)
SMALLS = jax.ShapeDtypeStruct((1, RING, RING, RING, SMALL, 256), F32)


def scratch_like(shape):
    return pltpu.VMEM(shape.shape, shape.dtype)


def forward_kernel(own_ref, small_ref, tokens_ref, cotangent_ref, full, small_out, x0_out, g_out, mid_out, x1_out, end_out, low_out,
                   mixed_out, att_out, probs_out, act_out, slope_out,
                   small, x0, resid, lows, acc, mids, ends, slots, mixed_all, att_all, probs_all, act_all, slope_all, *sems):
    place = Place()
    turn_x, turn_g = Turn(place, tokens_ref, x0, *sems[0:3]), Turn(place, cotangent_ref, g_out, *sems[3:6])
    load, saves, misc = sems[6:9]
    gather = Gather(place, own_ref, full, small_ref, small, sems[9:])
    units = [number(*pair) for pair in ORDER]

    own_copies = [
        pltpu.make_async_copy(own_ref.at[:, place.mine],
                              full.at[:, place.at["y"], place.at["z"], place.at["x"], place.mine], misc.at[0]),
        pltpu.make_async_copy(small_ref, small.at[:, place.at["y"], place.at["z"], place.at["x"]], misc.at[1]),
    ]
    for copy in own_copies:
        copy.start()
    place.greet(NEAR + (("x", 2),))
    gather.begin()
    turn_x.start()
    for copy in own_copies:
        copy.wait()
    gather.small_phase(1, "first")
    for unit in units[:2]:
        gather.first_two(unit)
    for unit in units[:2]:
        gather.second_two(unit)
    gather.small_phase(1, "second")
    for unit in units[:2]:
        gather.third_two(unit)
        gather.first_three(unit)
    for unit in units[2:]:
        gather.first_two(unit)
    gather.small_phase(1, "third")
    gather.small_phase(2, "first")
    gather.second_three(units[0])
    for unit in units[2:]:
        gather.second_two(unit)
    gather.small_phase(2, "second")
    gather.second_three(units[1])
    turn_x.end()
    resid[...] = as_rows(x0)
    gather.third_three(units[0])
    for unit in units[2:]:
        gather.third_two(unit)
    for unit in units[2:4]:
        gather.first_three(unit)
    gather.small_phase(2, "third")
    gather.ready(units[0])
    kept = []

    def keep(src, dst, k):
        copy = pltpu.make_async_copy(src, dst, misc.at[k])
        copy.start()
        kept.append((src, dst, k))

    keep(x0, x0_out, 2)
    keep(small, small_out, 3)
    turn_g.start()

    for k, (kind, layer) in enumerate(ORDER):
        unit = units[k]
        hooks = {2: [], 3: []}
        if k + 1 < 6:
            hooks[2] += [functools.partial(gather.third_three, units[k + 1])]
            if k + 2 < 6:
                hooks[2] += [functools.partial(gather.second_three, units[k + 2])]
            if k + 4 < 6:
                hooks[2] += [functools.partial(gather.first_three, units[k + 4])]
            hooks[3] += [functools.partial(gather.ready, units[k + 1])]

        def save(which, src, dst, step):
            return pltpu.make_async_copy(src, dst, saves.at[which, k, step])

        if kind == 0:
            low = lows.at[layer, 0]
            low[...] = norm_low(resid[...], small, layer, 0)
            keep(low, low_out.at[layer, 0], 8 + 2 * layer)
            acc[...] = resid[...] + feature_row(small, layer, 4)

            def body(step, slot):
                weights = slots.at[slot]
                mixed = dot_nt(low[...], tall(weights, 0, QKV)) + here_row(small, step, layer, 7, 0, QKV)
                mixed = mixed.astype(BF16)
                mixed_all[layer, step] = mixed
                attended = []
                for j in range(BLOCKS):
                    queries, keys, values = head_parts(mixed, j)
                    probs = softmax(queries, keys).astype(BF16)
                    probs_all[layer, step, j] = probs
                    attended.append(dot_nn(probs, values).astype(BF16))
                attended = jnp.concatenate(attended, axis=1)
                att_all[layer, step] = attended
                acc[...] += dot_nn(attended, tall(weights, QKV, HEAD))
                for copy in copies(step):
                    copy.start()

            def copies(step):
                pairs = ((mixed_all, mixed_out), (att_all, att_out), (probs_all, probs_out))
                return [save(i, src.at[layer, step], dst.at[layer, step], step) for i, (src, dst) in enumerate(pairs)]
        else:
            half = kind - 1
            if half == 0:
                mids[layer] = acc[...]
                resid[...] = acc[...]
                low = lows.at[layer, 1]
                low[...] = norm_low(resid[...], small, layer, 1)
                keep(low, low_out.at[layer, 1], 9 + 2 * layer)
                acc[...] = resid[...] + feature_row(small, layer, 5)
                keep(mids.at[layer], mid_out.at[layer], 4 + layer)

            def body(step, slot):
                weights = slots.at[slot]
                upward = dot_nt(low[...], tall(weights, 0, FF_HALF)) + here_row(small, step, layer, 6, half * FF_HALF, FF_HALF)
                below = 0.5 + 0.5 * lax.erf(upward * 2**-0.5)
                activated = (upward * below).astype(BF16)
                act_all[layer, half, step] = activated
                slope = below + upward * (jnp.exp(-0.5 * upward * upward) * (2 * jnp.pi) ** -0.5)
                slope_all[layer, half, step] = slope.astype(BF16)
                acc[...] += dot_nn(activated, tall(weights, FF_HALF, FF_HALF))
                for copy in copies(step):
                    copy.start()

            def copies(step):
                pairs = ((act_all, act_out), (slope_all, slope_out))
                return [save(i, src.at[layer, half, step], dst.at[layer, half, step], step) for i, (src, dst) in enumerate(pairs)]

        Stream([(lambda step: full.at[unit, step], slots)], load.at[k]).run(body, hooks)
        for step in range(STEPS):
            for copy in copies(step):
                copy.wait()
        if kind == 2 and layer == 0:
            resid[...] = acc[...]
            keep(resid, x1_out, 6)
            pltpu.make_async_copy(resid, x1_out, misc.at[6]).wait()
            kept.pop()
    put_rows(ends, acc[...])
    keep(ends, end_out, 7)
    turn_g.end()
    gather.finish()
    for src, dst, k in kept:
        pltpu.make_async_copy(src, dst, misc.at[k]).wait()


def forward(own, small, tokens, cotangent):
    both = jax.ShapeDtypeStruct((2, ROWS, WIDTH), F32)
    return pl.pallas_call(
        forward_kernel,
        out_shape=[WEIGHTS, SMALLS, TURNED, TURNED, both, TOKENS, TURNED, LOWS, *SAVED],
        in_specs=[VMEM] * 4,
        out_specs=[ANY] * 13,
        scratch_shapes=[
            scratch_like(SMALLS), scratch_like(TURNED), scratch_like(TOKENS), scratch_like(LOWS),
            scratch_like(TOKENS), scratch_like(both), scratch_like(TURNED), pltpu.VMEM((2, RING, RING, UNIT, 256), BF16),
            *[scratch_like(s) for s in SAVED],
            *TURN_SEMAPHORES, *TURN_SEMAPHORES, DMA((6, 2, 1)), DMA((3, 6, STEPS)), DMA((12,)),
            *gather_semaphores(),
        ],
        compiler_params=pltpu.CompilerParams(vmem_limit_bytes=VMEM_LIMIT, collective_id=0, has_side_effects=True),
        name="forward",
    )(own, small, tokens, cotangent)


BACK = [(2, 1), (1, 1), (0, 1), (2, 0), (1, 0), (0, 0)]


def backward_kernel(full, small_in, x0_in, g_in, mid_in, x1_in, end_ref, lows_in, mixed_in, att_in, probs_in, act_in, slope_in,
                    encoded_out, tokens_out, grads_out, sums_out,
                    grad, low, acc, turned, small, lows, xbuf, sums, columns_all, slots, mixed_two, att_two, probs_two, act_two, slope_two, stage, outs,
                    *rest):
    first, pair = [rest[0:2], rest[2:4], rest[4:6]], [rest[6:8], rest[8:10]]
    later = [rest[10:16], rest[16:22]]
    total_scratch, sems = rest[22:28], rest[28:]
    place = Place()
    turn_out, turn_g = Turn(place, end_ref, encoded_out, *sems[0:3]), Turn(place, turned, tokens_out, *sems[3:6])
    load, free, misc = sems[6:9]
    unit_sems = [[group.at[k] for group in sems[9:]] for k in range(6)]
    scatters = []
    for k, (kind, layer) in enumerate(BACK):
        scatters.append(
            Scatter(place, kind, layer, stage, [*first[k % 3], *pair[k % 2]], later[k % 2][0:3], later[k % 2][3:6], outs.at[k],
                    grads_out.at[number(kind, layer)], unit_sems[k])
        )
    total = Total(place, sums, total_scratch[0], sums_out, *total_scratch[1:])
    norms = [(1, 1), (1, 0), (0, 1), (0, 0)]

    def fetch_low(phase):
        return pltpu.make_async_copy(lows_in.at[norms[phase][0], norms[phase][1]], lows.at[phase % 2], misc.at[phase])

    def fetch_x(phase):
        source = (mid_in.at[1], x1_in, mid_in.at[0], x0_in)[phase]
        return pltpu.make_async_copy(source, turned if phase == 3 else xbuf, misc.at[4 + phase])

    starts = [pltpu.make_async_copy(g_in, turned, misc.at[8]),
              pltpu.make_async_copy(small_in.at[:, pl.ds(0, 1), pl.ds(0, 1)], small, misc.at[9]),
              fetch_low(0)]
    for copy in starts:
        copy.start()
    place.greet(TOTAL_PEERS)
    turn_out.start()
    for copy in starts:
        copy.wait()
    grad[...] = as_rows(turned)
    sums[...] = jnp.zeros_like(sums)
    columns_all[...] = jnp.zeros_like(columns_all)

    def leave(k, peers=NEAR):
        place.tell(free.at[k], peers)

    def may(k, peers=NEAR):
        pl.semaphore_wait(free.at[k], len(peers))

    for k, (kind, layer) in enumerate(BACK):
        it = scatters[k]
        hooks = {0: [], 1: [], 2: [], 3: []}
        if k >= 1:
            hooks[0] += [scatters[k - 1].open]
            hooks[2] += [scatters[k - 1].sides_one]
        if k >= 2:
            hooks[1] += [scatters[k - 2].centre_one, scatters[k - 2].start_two]
            hooks[2] += [scatters[k - 2].sides_two]
            hooks[3] += [scatters[k - 2].centre_two]
        if k >= 3:
            hooks[0] += [scatters[k - 3].sides_three]
            hooks[1] += [scatters[k - 3].centre_three]
        if k >= 2:
            hooks[1] += [functools.partial(leave, k + 1)]
        base = LAYER_SUMS * layer

        def begin(step):
            @pl.when(step >= 2)
            def _():
                it.free(step - 2)

            if k >= 1:
                @pl.when(step == 0)
                def _():
                    scatters[k - 1].free_last()
                    if k >= 3:
                        may(k)

        if kind == 0:
            phase = 3 - 2 * layer
            here = lows.at[phase % 2]
            fetch_low(phase).wait()
            if phase < 3:
                fetch_low(phase + 1).start()
            fetch_x(phase).start()
            low[...] = grad[...].astype(BF16)
            acc[...] = jnp.zeros_like(acc)

            def body(step, slot):
                weights = slots.at[slot]
                begin(step)
                g = low[...]
                mixed = mixed_two[slot]
                store_blocks(stage, slot, QKV, dot_tn(att_two[slot], g))
                g_all = dot_nt(g, tall(weights, QKV, HEAD)).astype(BF16)
                g_mixed = []
                for j in range(BLOCKS):
                    queries, keys, values = head_parts(mixed, j)
                    g_att = g_all[:, j * HEAD : (j + 1) * HEAD]
                    probs_low = probs_two[slot, j]
                    probs = probs_low.astype(F32)
                    g_probs = dot_nt(g_att, values)
                    g_values = dot_tn(probs_low, g_att)
                    centre = jnp.sum(probs * g_probs, axis=1, keepdims=True)
                    g_scores = (probs * (g_probs - centre) * HEAD**-0.5).astype(BF16)
                    g_mixed += [dot_nn(g_scores, keys), dot_tn(g_scores, queries), g_values]
                g_mixed = jnp.concatenate([part.astype(BF16) for part in g_mixed], axis=1)
                store_blocks(stage, slot, 0, dot_tn(g_mixed, here[...]))
                it.hand_over(step)
                columns_all[layer, 1, step, :, : BLOCKS * QKV] = jnp.sum(g_mixed.astype(F32), axis=0, keepdims=True)
                acc[...] += dot_nn(g_mixed, tall(weights, 0, QKV))

            pairs = [
                (lambda step: full.at[number(kind, layer), step], slots),
                (lambda step: mixed_in.at[layer, step], mixed_two),
                (lambda step: att_in.at[layer, step], att_two),
                (lambda step: probs_in.at[layer, step], probs_two),
            ]
        else:
            half = kind - 1
            phase = 2 - 2 * layer
            here = lows.at[phase % 2]
            if half == 1:
                if phase > 0:
                    fetch_low(phase).wait()
                fetch_low(phase + 1).start()
                fetch_x(phase).start()
                low[...] = grad[...].astype(BF16)
                acc[...] = jnp.zeros_like(acc)

            def body(step, slot):
                weights = slots.at[slot]
                begin(step)
                g = low[...]
                store_blocks(stage, slot, FF_HALF, dot_tn(act_two[slot], g))
                g_up = (dot_nt(g, tall(weights, FF_HALF, FF_HALF)) * slope_two[slot].astype(F32)).astype(BF16)
                store_blocks(stage, slot, 0, dot_tn(g_up, here[...]))
                it.hand_over(step)
                columns = jnp.sum(g_up.astype(F32), axis=0, keepdims=True)
                for j in range(BLOCKS):
                    at = j * 2 * FF_HALF + half * FF_HALF
                    columns_all[layer, 0, step, :, at : at + FF_HALF] = columns[:, j * FF_HALF : (j + 1) * FF_HALF]
                acc[...] += dot_nn(g_up, tall(weights, 0, FF_HALF))

            pairs = [
                (lambda step: full.at[number(kind, layer), step], slots),
                (lambda step: act_in.at[layer, half, step], act_two),
                (lambda step: slope_in.at[layer, half, step], slope_two),
            ]
        Stream(pairs, load.at[k]).run(body, hooks)
        if kind < 2:
            j = kind
            fetch_x(phase).wait()
            x = as_rows(turned) if phase == 3 else xbuf[...]
            part, gain, shift = norm_back(acc[...], x, feature_row(small, layer, j))
            at = base + (8 if kind == 1 else 11)
            sums[at : at + 1, :] = jnp.sum(low[...].astype(F32), axis=0, keepdims=True)
            sums[at + 1 : at + 2, :] = gain
            sums[at + 2 : at + 3, :] = shift
            grad[...] = grad[...] + part
        if k == 5:
            put_rows(turned, grad[...])
            turn_g.start()
            for i in range(2):
                for which in range(2):
                    for step in range(STEPS):
                        at = LAYER_SUMS * i + STEPS * which + step
                        sums[at : at + 1, :] = columns_all[i, which, step]
            total.start()
    early, late = scatters[4], scatters[5]
    late.free_last()
    may(6)
    late.open()
    scatters[3].sides_three()
    early.centre_one()
    early.start_two()
    scatters[3].centre_three()
    leave(7, TOTAL_PEERS)
    total.core_sum()
    late.sides_one()
    early.sides_two()
    total.put(1, total.take(0))
    early.centre_two()
    late.centre_one()
    may(7, TOTAL_PEERS)
    late.each("direct", 1)
    total.put(2, total.take(1))
    early.sides_three()
    late.direct_centre(1)
    late.each("direct", 2)
    for it in scatters[:4]:
        it.shown()
    early.centre_three()
    total.last()
    late.direct_centre(2)
    late.show().start()
    turn_out.end()
    turn_g.end()
    early.shown()
    total.finish()
    late.sent(1)
    late.sent(2)
    late.shown()
    for it in scatters:
        it.keep().wait()


def backward(full, small, x0, g, mids, x1, ends, lows, saved):
    saved_two = [pltpu.VMEM((2,) + s.shape[-3 if len(s.shape) == 5 and s.shape[1] == STEPS else -2 :], s.dtype) for s in SAVED]
    semaphores = [pltpu.SemaphoreType.DMA((6,) + (s.shape if hasattr(s, "shape") else ())) for s in scatter_semaphores()]
    return pl.pallas_call(
        backward_kernel,
        out_shape=[TURNED, TURNED, jax.ShapeDtypeStruct((6, UNIT, 256), F32), jax.ShapeDtypeStruct((SUM_ROWS, WIDTH), F32)],
        in_specs=[ANY] * 13,
        out_specs=[ANY] * 4,
        scratch_shapes=[
            scratch_like(TOKENS), pltpu.VMEM((ROWS, WIDTH), BF16), scratch_like(TOKENS),
            scratch_like(TURNED), pltpu.VMEM((1, 1, 1, RING, SMALL, 256), F32), pltpu.VMEM((2, ROWS, WIDTH), BF16), scratch_like(TOKENS),
            pltpu.VMEM((SUM_ROWS, WIDTH), F32), pltpu.VMEM((2, 2, STEPS, 1, WIDTH), F32),
            pltpu.VMEM((2, RING, RING, UNIT, 256), BF16),
            *saved_two,
            pltpu.VMEM((2, RING, RING, UNIT, 256), BF16), pltpu.VMEM((6, UNIT, 256), F32),
            *first_buffers(), *first_buffers(), *first_buffers(), *pair_buffers(), *pair_buffers(), *later_buffers(), *later_buffers(),
            *total_buffers(SUM_ROWS),
            *TURN_SEMAPHORES, *TURN_SEMAPHORES, DMA((6, 2, 4)), pltpu.SemaphoreType.REGULAR((8,)), DMA((10,)),
            *semaphores,
        ],
        compiler_params=pltpu.CompilerParams(vmem_limit_bytes=VMEM_LIMIT, collective_id=1, has_side_effects=True),
        name="backward",
    )(full, small, x0, g, mids, x1, ends, lows, *saved)


def to_images(rows):
    return jnp.pad(rows.reshape(3, SEQ, 256), ((0, 1), (0, ROWS - SEQ), (0, 0)))


def from_images(turned):
    return turned[:3, :SEQ].reshape(3 * SEQ, 256).astype(F32)


def shards(tokens, norm_gain, norm_shift, qkv_weight, qv_bias, proj_weight, proj_bias, up_weight, up_bias, down_weight, down_bias, cotangent):
    layers = qkv_weight.shape[0]
    attention = jnp.concatenate([qkv_weight.transpose(0, 2, 1), proj_weight], axis=1)
    up = up_weight.transpose(0, 2, 1)
    halves = [jnp.concatenate([part[:, at : at + FF_HALF] for part in (up, down_weight)], axis=1) for at in (0, FF_HALF)]
    own = jnp.concatenate([attention, *halves], axis=0)
    zeros = jnp.zeros((layers, HEAD), F32)
    qkv_row = jnp.concatenate([qv_bias[:, :HEAD], zeros, qv_bias[:, HEAD:], zeros], axis=1)
    small = jnp.stack([norm_gain[:, 0], norm_gain[:, 1], norm_shift[:, 0], norm_shift[:, 1], proj_bias, down_bias, up_bias, qkv_row], axis=1)
    full, small, x0, g, mids, x1, ends, lows, *saved = forward(
        own, small.reshape(1, SMALL, 256), to_images(tokens), to_images(cotangent.astype(BF16))
    )
    encoded, grad_tokens, grads, sums = backward(full, small, x0, g, mids, x1, ends, lows, saved)
    row, col = lax.axis_index("row"), lax.axis_index("col")
    sums = sums[: layers * LAYER_SUMS].reshape(layers, LAYER_SUMS, WIDTH)
    up_sums = lax.dynamic_slice_in_dim(sums[:, 0:4].reshape(layers, 16, 256), col, 1, 1)[:, 0]
    qkv_sums = sums[:, 4:8, : BLOCKS * QKV].reshape(layers, 16, QKV)
    qkv_sums = lax.dynamic_slice_in_dim(qkv_sums, col, 1, 1)[:, 0]
    features = lax.dynamic_slice_in_dim(sums[:, 8:].reshape(layers, 6, RING, 256), row, 1, 2)[:, :, 0]
    attention, first, second = grads[0:2], grads[2:4], grads[4:6]
    return (
        from_images(encoded),
        from_images(grad_tokens),
        jnp.stack([features[:, 4], features[:, 1]], axis=1),
        jnp.stack([features[:, 5], features[:, 2]], axis=1),
        attention[:, :QKV].transpose(0, 2, 1),
        jnp.concatenate([qkv_sums[:, :HEAD], qkv_sums[:, 2 * HEAD : QKV]], axis=1),
        attention[:, QKV:],
        features[:, 3],
        jnp.concatenate([first[:, :FF_HALF], second[:, :FF_HALF]], axis=1).transpose(0, 2, 1),
        up_sums,
        jnp.concatenate([first[:, FF_HALF:], second[:, FF_HALF:]], axis=1),
        features[:, 0],
    )


def solution(mesh):
    in_specs = (
        P(("dp", "col"), "row"),
        P(None, None, "row"),
        P(None, None, "row"),
        P(None, "row", "col"),
        P(None, "col"),
        P(None, "col", "row"),
        P(None, "row"),
        P(None, "row", "col"),
        P(None, "col"),
        P(None, "col", "row"),
        P(None, "row"),
        P(("dp", "col"), "row"),
    )
    out_specs = (
        P(("dp", "col"), "row"),
        P(("dp", "col"), "row"),
        P(None, None, "row"),
        P(None, None, "row"),
        P(None, "row", "col"),
        P(None, "col"),
        P(None, "col", "row"),
        P(None, "row"),
        P(None, "row", "col"),
        P(None, "col"),
        P(None, "col", "row"),
        P(None, "row"),
    )
    return jax.shard_map(shards, mesh=mesh, in_specs=in_specs, out_specs=out_specs, check_vma=False)
```
